32 devices in a mesh: ctx: 16 (over z, y, x), fsdp: 2 (over core).
Axes of the slice: x: 2, y: 2, z: 4, core: 2. Of those that a mesh axis runs over, the one named last changes fastest.
Arguments:
- tokens: bfloat16 [2, 2048, 1024], P('fsdp', 'ctx'), may hold values from -6 to 6
- block_order: int32 [16, 2], P('ctx'), may hold values from 0 to 31, as said below
- ln_gain: bfloat16 [1024], P('fsdp'), may hold values from 0.25 to 1.75
- ln_bias: bfloat16 [1024], P('fsdp'), may hold values from -1.75 to 1.75
- w_qkv: bfloat16 [1024, 3072], P('fsdp')
- qv_bias: bfloat16 [2, 1024], P(None, 'fsdp'), may hold values from -3 to 3
- w_out: bfloat16 [1024, 1024], P('fsdp'), may hold values from -1.5 to 1.5
- b_out: bfloat16 [1024], P('fsdp'), may hold values from -3 to 3
- w_in: bfloat16 [1024, 4096], P('fsdp'), may hold values from -0.1875 to 0.1875
- b_in: bfloat16 [4096], P('fsdp'), may hold values from -3 to 3
- w_down: bfloat16 [4096, 1024], P('fsdp'), may hold values from -0.09375 to 0.09375
- b_down: bfloat16 [1024], P('fsdp'), may hold values from -3 to 3
- cotangent: bfloat16 [2, 2048, 1024], P('fsdp', 'ctx'), may hold values from -6 to 6
Outputs:
- layer_out: bfloat16 [2, 2048, 1024], P('fsdp', 'ctx')
- grad_tokens: bfloat16 [2, 2048, 1024], P('fsdp', 'ctx')
- grad_ln_gain: float32 [1024], P(('ctx', 'fsdp'))
- grad_ln_bias: float32 [1024], P(('ctx', 'fsdp'))
- grad_w_qkv: float32 [1024, 3072], P(('ctx', 'fsdp'))
- grad_qv_bias: float32 [2, 1024], P(None, ('ctx', 'fsdp'))
- grad_w_out: float32 [1024, 1024], P(('ctx', 'fsdp'))
- grad_b_out: float32 [1024], P(('ctx', 'fsdp'))
- grad_w_in: float32 [1024, 4096], P(('ctx', 'fsdp'))
- grad_b_in: float32 [4096], P(('ctx', 'fsdp'))
- grad_w_down: float32 [4096, 1024], P(('ctx', 'fsdp'))
- grad_b_down: float32 [1024], P(('ctx', 'fsdp'))
The draws below stay inside these ranges and needn't reach their ends.
Inputs may be any that keep to these rules, and one draw needn't show every extreme that they name: Row i of block_order holds some j below 16 and 31 - j, in either order; each of the 32 block numbers appears once.
All inputs are finite; a program needn't handle non-finite values.
Results may differ from the reference program's by a relative error of at most 0.015.
Values may be sent and summed in bfloat16 or wider, within the bound.
No kernel may reach another device: no remote copies, remote signals or barrier semaphores. Data moves between devices by JAX's collectives and lax.ppermute only.
A program may use at most 320 MiB of HBM per device.

```python
import math
import jax
import jax.numpy as jnp
from jax import lax

D = 1024
HEADS = 16
HEAD_DIM = 64
FF = 4096
ROT = 16
HALF = 64
LENGTH = 2048
SEQS = 2
N_CTX = 16


def draw_block_order(key, part):
    perm_key, flip_key = jax.random.split(jax.random.fold_in(key, 11))
    chosen = jax.random.permutation(perm_key, jnp.arange(N_CTX, dtype=jnp.int32))
    mirror = 2 * N_CTX - 1 - chosen
    flipped = jax.random.randint(flip_key, (N_CTX,), 0, 2, dtype=jnp.int32)
    first_block = jnp.where(flipped == 1, mirror, chosen)
    second_block = jnp.where(flipped == 1, chosen, mirror)
    return jnp.stack([first_block, second_block], 1).astype(jnp.int32)


def draw_w_qkv(key, part):
    column = jnp.arange(3 * D)
    factor = jnp.where(column < 2 * D, 1.5, 1.0) / math.sqrt(D)
    raw_noise = jax.random.normal(jax.random.fold_in(key, 13), (D, 3 * D), jnp.float32)
    return (raw_noise * factor).astype(jnp.bfloat16)


def shard_levels(own_key, shape, cuts, low, largest):
    def one(position, parts):
        heights = jax.random.uniform(jax.random.fold_in(jax.random.fold_in(own_key, 6), position), (parts,), jnp.float32, low / len(cuts), largest / len(cuts))
        return jnp.repeat(jnp.exp(heights), shape[position] // parts).reshape((-1,) + (1,) * (len(shape) - position - 1))

    factor_of = one(*cuts[0])
    for cut in cuts[1:]:
        factor_of = factor_of * one(*cut)
    return factor_of


def bell_draw(key, dims, deviation, reach, pieces=(), kind=jnp.bfloat16):
    values = jax.random.normal(key, dims, jnp.float32) * deviation
    if len(pieces) > 0:
        values = shard_levels(key, dims, pieces, -0.22, 0.18) * values
    return jnp.clip(values, min=-reach, max=reach).astype(kind)


def setup_inputs(seed: int = 0) -> dict:
    key_of = jax.random.split(jax.random.key(seed), 14)
    tokens = bell_draw(key_of[0], (SEQS, LENGTH, D), 1.0, 6.0, ((0, 2), (1, 16)))
    block_order = draw_block_order(jax.random.fold_in(key_of[13], 71), 0)
    ln_gain = jnp.clip(1.0 + 0.15 * jax.random.normal(key_of[2], (D,), jnp.float32), 0.25, 1.75).astype(jnp.bfloat16)
    ln_bias = bell_draw(key_of[3], (D,), 0.3, 1.75, ((0, 2),))
    w_qkv = draw_w_qkv(jax.random.fold_in(key_of[13], 71), 0)
    qv_bias = bell_draw(key_of[5], (2, D), 0.5, 3.0, ((1, 2),))
    w_out = bell_draw(key_of[6], (D, D), 16 ** -0.5, 1.5, ((0, 2),))
    b_out = bell_draw(key_of[7], (D,), 0.5, 3.0, ((0, 2),))
    w_in = bell_draw(key_of[8], (D, FF), D ** -0.5, 0.1875, ((0, 2),))
    b_in = bell_draw(key_of[9], (FF,), 0.5, 3.0, ((0, 2),))
    w_down = bell_draw(key_of[10], (FF, D), FF ** -0.5, 0.09375, ((0, 2),))
    b_down = bell_draw(key_of[11], (D,), 0.5, 3.0, ((0, 2),))
    cotangent = bell_draw(key_of[12], (SEQS, LENGTH, D), 1.0, 6.0, ((0, 2), (1, 16)))
    return dict(tokens=tokens, block_order=block_order, ln_gain=ln_gain, ln_bias=ln_bias, w_qkv=w_qkv, qv_bias=qv_bias, w_out=w_out, b_out=b_out, w_in=w_in, b_in=b_in, w_down=w_down, b_down=b_down, cotangent=cotangent)


@jax.custom_vjp
def low(v):
    return lax.optimization_barrier(v.astype(jnp.bfloat16)).astype(jnp.float32)

@jax.custom_vjp
def low_back(v):
    return v

def low_keep(v):
    return (low(v), None)

def low_pass(kept, grad):
    return (grad,)

def back_keep(v):
    return (v, None)

def back_low(kept, grad):
    return (low(grad),)
low.defvjp(low_keep, low_pass)
low_back.defvjp(back_keep, back_low)
epsilon = 1e-05
exact_mode = lax.Precision.HIGHEST

def product(left_side, right_side):
    return jnp.dot(left_side, right_side, precision=exact_mode, preferred_element_type=jnp.float32)

def rotate(vectors, cosine, sine_part):
    half_rot = ROT // 2
    rotary_part = vectors[..., :ROT]
    turned = jnp.concatenate([-rotary_part[..., half_rot:], rotary_part[..., :half_rot]], -1)
    return jnp.concatenate([rotary_part * cosine + turned * sine_part, vectors[..., ROT:]], -1)

def tables(positions):
    freq_index = jnp.arange(ROT // 2, dtype=jnp.float32)
    inverse = 10000.0 ** (-2.0 * freq_index / ROT)
    angles = positions.astype(jnp.float32)[:, None] * inverse[None, :]
    angles = jnp.concatenate([angles, angles], -1)
    return (jnp.cos(angles), jnp.sin(angles))

def head_attention(queries, key_rows, value_rows, positions):
    seq_length = queries.shape[0]
    block_rows = min(512, seq_length)
    score_scale = HEAD_DIM ** (-0.5)

    def attend_rows(paired):
        query_rows, query_pos = paired
        scores = low_back(product(query_rows, key_rows.T) * score_scale)
        allowed = query_pos[:, None] >= positions[None, :]
        masked = jnp.where(allowed, scores, -1e+30)
        row_max = lax.optimization_barrier(jnp.max(masked, -1, keepdims=True))
        weights = jnp.where(allowed, jnp.exp(masked - row_max), 0.0)
        probs = weights / lax.optimization_barrier(jnp.sum(weights, -1, keepdims=True))
        return product(low(probs), value_rows)
    blocks = (queries.reshape(seq_length // block_rows, block_rows, HEAD_DIM), positions.reshape(seq_length // block_rows, block_rows))
    return lax.map(jax.checkpoint(attend_rows), blocks).reshape(seq_length, HEAD_DIM)

def forward(tokens, ln_gain, ln_bias, w_qkv, qv_bias, w_out, b_out, w_in, b_in, w_down, b_down, positions):
    seq_count, seq_length, model_width = tokens.shape
    row_mean = lax.optimization_barrier(jnp.mean(tokens, -1, keepdims=True))
    centered = tokens - row_mean
    inverse = lax.rsqrt(lax.optimization_barrier(jnp.mean(centered * centered, -1, keepdims=True)) + epsilon)
    ln_out = low(centered * inverse * ln_gain + ln_bias)
    flat_rows = ln_out.reshape(seq_count * seq_length, model_width)
    qkv_pre = product(flat_rows, w_qkv)
    query_pre = low_back(qkv_pre[:, :model_width] + qv_bias[0])
    key_pre = low_back(qkv_pre[:, model_width:2 * model_width])
    value_rows = low(low_back(qkv_pre[:, 2 * model_width:] + qv_bias[1]))
    cosine, sine_part = tables(positions)
    cosine = cosine[None, :, None, :]
    sine_part = sine_part[None, :, None, :]
    head_shape = (seq_count, seq_length, HEADS, HEAD_DIM)
    queries = low(rotate(query_pre.reshape(head_shape), cosine, sine_part))
    key_rows = low(rotate(key_pre.reshape(head_shape), cosine, sine_part))
    value_heads = value_rows.reshape(head_shape)

    def by_head(array):
        return array.transpose(0, 2, 1, 3).reshape(seq_count * HEADS, seq_length, HEAD_DIM)

    def one_head(triple):
        return head_attention(triple[0], triple[1], triple[2], positions)
    attended = lax.map(one_head, (by_head(queries), by_head(key_rows), by_head(value_heads)))
    attended = attended.reshape(seq_count, HEADS, seq_length, HEAD_DIM).transpose(0, 2, 1, 3)
    attended = low(low_back(attended.reshape(seq_count * seq_length, model_width)))
    branch = product(attended, w_out) + b_out
    hidden = low_back(product(flat_rows, w_in) + b_in)
    active = low(jax.nn.gelu(hidden, approximate=False))
    feed_out = product(active, w_down) + b_down
    return tokens + (branch + feed_out).reshape(seq_count, seq_length, model_width)

def reference(tokens, block_order, ln_gain, ln_bias, w_qkv, qv_bias, w_out, b_out, w_in, b_in, w_down, b_down, cotangent):
    offsets = jnp.arange(HALF, dtype=jnp.int32)
    positions = (block_order.astype(jnp.int32)[:, :, None] * HALF + offsets[None, None, :]).reshape(LENGTH)
    floats = tuple((array.astype(jnp.float32) for array in (tokens, ln_gain, ln_bias, w_qkv, qv_bias, w_out, b_out, w_in, b_in, w_down, b_down)))

    def wrapped(*params):
        return forward(*params, positions)
    layer_out, pullback = jax.vjp(wrapped, *floats)
    grads = pullback(cotangent.astype(jnp.float32))
    return (layer_out.astype(jnp.bfloat16), grads[0].astype(jnp.bfloat16), grads[1], grads[2], grads[3], grads[4], grads[5], grads[6], grads[7], grads[8], grads[9], grads[10])
```

```python
from functools import partial
import math

import jax
import jax.numpy as jnp
from jax import lax
from jax.experimental import pallas as pl
from jax.experimental.pallas import tpu as pltpu
from jax.sharding import PartitionSpec as P

HEADS = 16
HEAD_DIM = 64
ROT = 16


epsilon = 1e-05


def from_behind(block, axis, distance):
    devices = range(lax.axis_size(axis))
    route = [((i - distance) % len(devices), i) for i in devices]
    return lax.ppermute(block, axis, route)


def rotate(vectors, cosine, sine_part):
    half_rot = ROT // 2
    rotary_part = vectors[..., :ROT]
    turned = jnp.concatenate([-rotary_part[..., half_rot:], rotary_part[..., :half_rot]], -1)
    return jnp.concatenate([rotary_part * cosine + turned * sine_part, vectors[..., ROT:]], -1)


def tables(positions):
    freq_index = jnp.arange(ROT // 2, dtype=jnp.float32)
    inverse = 10000.0 ** (-2.0 * freq_index / ROT)
    angles = positions.astype(jnp.float32)[:, None] * inverse[None, :]
    angles = jnp.concatenate([angles, angles], -1)
    return (jnp.cos(angles), jnp.sin(angles))


def spread_positions(orders, half_rows):
    offsets = jnp.arange(half_rows, dtype=jnp.int32)
    return (orders[:, :, None] * half_rows + offsets[None, None, :]).reshape(-1)


def outer_sum(left_side, right_side):
    return lax.dot_general(
        left_side, right_side, (((0,), (0,)), ((), ())), preferred_element_type=jnp.float32
    )


def times_transposed(left_side, right_side):
    return lax.dot_general(
        left_side, right_side, (((1,), (1,)), ((), ())), preferred_element_type=jnp.float32
    )


def attend_block(carried, queries, query_pos, key_rows, value_rows, key_pos, score_scale):
    row_max, row_sum, weighted = carried
    scores = (
        jnp.einsum("qhd,khd->hqk", queries, key_rows, preferred_element_type=jnp.float32)
        * score_scale
    )
    allowed = (query_pos[:, None] >= key_pos[None, :])[None]
    new_max = jnp.maximum(row_max, jnp.max(jnp.where(allowed, scores, -1e30), -1))
    weights = jnp.where(allowed, jnp.exp(scores - new_max[:, :, None]), 0.0)
    rescale = jnp.exp(row_max - new_max)
    row_sum = row_sum * rescale + jnp.sum(weights, -1)
    weighted = weighted * rescale.T[:, :, None] + jnp.einsum(
        "hqk,khd->qhd", weights.astype(jnp.bfloat16), value_rows, preferred_element_type=jnp.float32
    )
    return (new_max, row_sum, weighted)


def block_grads(
    queries, grad_rows, log_sum, delta_rows, query_pos, key_rows, value_rows, key_pos, score_scale
):
    scores = (
        jnp.einsum("qhd,khd->hqk", queries, key_rows, preferred_element_type=jnp.float32)
        * score_scale
    )
    allowed = (query_pos[:, None] >= key_pos[None, :])[None]
    probs = jnp.where(allowed, jnp.exp(scores - log_sum[:, :, None]), 0.0)
    grad_values = jnp.einsum(
        "hqk,qhd->khd", probs.astype(jnp.bfloat16), grad_rows, preferred_element_type=jnp.float32
    )
    grad_probs = jnp.einsum(
        "qhd,khd->hqk", grad_rows, value_rows, preferred_element_type=jnp.float32
    )
    grad_scores = (probs * (grad_probs - delta_rows[:, :, None])).astype(jnp.bfloat16)
    grad_queries = (
        jnp.einsum("hqk,khd->qhd", grad_scores, key_rows, preferred_element_type=jnp.float32)
        * score_scale
    )
    grad_keys = (
        jnp.einsum("hqk,qhd->khd", grad_scores, queries, preferred_element_type=jnp.float32)
        * score_scale
    )
    return (grad_queries, grad_keys, grad_values)


def body(
    tokens,
    block_order,
    ln_gain,
    ln_bias,
    w_qkv,
    qv_bias,
    w_out,
    b_out,
    w_in,
    b_in,
    w_down,
    b_down,
    cotangent,
):
    gathered = (
        lax.all_gather(ln_gain, "fsdp", axis=0, tiled=True),
        lax.all_gather(ln_bias, "fsdp", axis=0, tiled=True),
        lax.all_gather(w_qkv, "fsdp", axis=0, tiled=True),
        lax.all_gather(qv_bias, "fsdp", axis=1, tiled=True),
        lax.all_gather(w_out, "fsdp", axis=0, tiled=True),
        lax.all_gather(b_out, "fsdp", axis=0, tiled=True),
        lax.all_gather(w_in, "fsdp", axis=0, tiled=True),
        lax.all_gather(b_in, "fsdp", axis=0, tiled=True),
        lax.all_gather(w_down, "fsdp", axis=0, tiled=True),
        lax.all_gather(b_down, "fsdp", axis=0, tiled=True),
    )
    (
        gain_full,
        shift_full,
        qkv_full,
        bias_full,
        out_full,
        out_bias,
        in_full,
        in_bias,
        down_full,
        down_bias,
    ) = gathered
    tok_rows = tokens.shape[1]
    model_width = tokens.shape[2]
    half_rows = tok_rows // 2
    score_scale = HEAD_DIM ** (-0.5)
    head_shape = (tok_rows, HEADS, HEAD_DIM)
    flat_shape = (tok_rows, model_width)
    inputs = tokens[0].astype(jnp.float32)
    row_mean = jnp.mean(inputs, -1, keepdims=True)
    centered = inputs - row_mean
    inverse = lax.rsqrt(jnp.mean(centered * centered, -1, keepdims=True) + epsilon)
    normed = centered * inverse
    ln_out = (normed * gain_full.astype(jnp.float32) + shift_full.astype(jnp.float32)).astype(
        jnp.bfloat16
    )
    qkv_pre = jnp.dot(ln_out, qkv_full, preferred_element_type=jnp.float32)
    positions = spread_positions(block_order, half_rows)
    cosine, sine_part = tables(positions)
    cosine = cosine[:, None, :]
    sine_part = sine_part[:, None, :]
    query_pre = qkv_pre[:, :model_width] + bias_full[0].astype(jnp.float32)
    query_rows = rotate(query_pre.reshape(head_shape), cosine, sine_part).astype(jnp.bfloat16)
    key_rows = rotate(
        qkv_pre[:, model_width : 2 * model_width].reshape(head_shape), cosine, sine_part
    ).astype(jnp.bfloat16)
    value_rows = (qkv_pre[:, 2 * model_width :] + bias_full[1].astype(jnp.float32)).astype(
        jnp.bfloat16
    )
    key_flat = key_rows.reshape(flat_shape)
    start_state = (
        jnp.full((HEADS, tok_rows), -1e30, jnp.float32),
        jnp.zeros((HEADS, tok_rows), jnp.float32),
        jnp.zeros(head_shape, jnp.float32),
    )
    carried = start_state
    piece_keys = lax.all_gather(key_flat, "ctx", axis=0, tiled=True)
    piece_values = lax.all_gather(value_rows, "ctx", axis=0, tiled=True)
    piece_orders = lax.all_gather(block_order, "ctx", axis=0, tiled=True)
    shard_count = piece_orders.shape[0]
    group_size = math.gcd(shard_count, max(1, 1024 // tok_rows))
    rounds = shard_count // group_size
    stacked = (
        piece_keys.reshape(rounds, group_size * tok_rows, HEADS, HEAD_DIM),
        piece_values.reshape(rounds, group_size * tok_rows, HEADS, HEAD_DIM),
        piece_orders.reshape(rounds, group_size, 2),
    )

    def one_round(inner_state, block_item):
        key_pos = spread_positions(block_item[2], half_rows)
        return (
            attend_block(
                inner_state,
                query_rows,
                positions,
                block_item[0],
                block_item[1],
                key_pos,
                score_scale,
            ),
            None,
        )

    carried, _ = lax.scan(one_round, carried, stacked)
    row_max, row_sum, weighted = carried
    attended_f32 = weighted / row_sum.T[:, :, None]
    log_sum = row_max + jnp.log(row_sum)
    attended = attended_f32.reshape(flat_shape).astype(jnp.bfloat16)
    branch = jnp.dot(attended, out_full, preferred_element_type=jnp.float32) + out_bias.astype(
        jnp.float32
    )
    hidden = jnp.dot(ln_out, in_full, preferred_element_type=jnp.float32) + in_bias.astype(
        jnp.float32
    )
    active = jax.nn.gelu(hidden, approximate=False).astype(jnp.bfloat16)
    feed_out = jnp.dot(active, down_full, preferred_element_type=jnp.float32) + down_bias.astype(
        jnp.float32
    )
    layer_out = (inputs + branch + feed_out).astype(jnp.bfloat16)[None]
    gain_back, qkv_back, out_back, in_back, down_back = (
        gain_full,
        qkv_full,
        out_full,
        in_full,
        down_full,
    )
    grad_out = cotangent[0]
    grad_f32 = grad_out.astype(jnp.float32)
    grad_attended = times_transposed(grad_out, out_back).astype(jnp.bfloat16).reshape(head_shape)
    grad_active = times_transposed(grad_out, down_back)
    _, gelu_pull = jax.vjp(partial(jax.nn.gelu, approximate=False), hidden)
    grad_hidden = gelu_pull(grad_active)[0].astype(jnp.bfloat16)
    delta_rows = jnp.sum(grad_attended.astype(jnp.float32) * attended_f32, -1).T
    cotangent_sum = jnp.sum(grad_f32, 0)
    term_out_w = outer_sum(attended, grad_out)
    term_in_w = outer_sum(ln_out, grad_hidden)
    term_in_b = jnp.sum(grad_hidden.astype(jnp.float32), 0)
    term_down_w = outer_sum(active, grad_out)
    cycle_size = lax.axis_size("ctx")
    zeros_flat = jnp.zeros(flat_shape, jnp.float32)
    zeros_heads = jnp.zeros(head_shape, jnp.float32)

    def send_home(grad_keys, grad_values):
        return (
            from_behind(grad_keys.astype(jnp.bfloat16), "ctx", 1).astype(grad_keys.dtype),
            from_behind(grad_values.astype(jnp.bfloat16), "ctx", 1).astype(grad_values.dtype),
        )

    def visit_keys(carried):
        visit_key, visit_value, visit_order, grad_keys, grad_values, grad_query = carried
        part_query, part_key, part_value = block_grads(
            query_rows,
            grad_attended,
            log_sum,
            delta_rows,
            positions,
            visit_key.reshape(head_shape),
            visit_value.reshape(head_shape),
            spread_positions(visit_order, half_rows),
            score_scale,
        )
        return (
            grad_keys + part_key.reshape(flat_shape),
            grad_values + part_value.reshape(flat_shape),
            grad_query + part_query,
        )

    def cycle_step(step_index, carried):
        grad_keys, grad_values, grad_query = visit_keys(carried)
        visit_key, visit_value, visit_order = from_behind(
            (carried[0], carried[1], carried[2]), "ctx", 1
        )
        grad_keys, grad_values = send_home(grad_keys, grad_values)
        return (visit_key, visit_value, visit_order, grad_keys, grad_values, grad_query)

    carried = lax.fori_loop(
        0,
        cycle_size - 1,
        cycle_step,
        (key_flat, value_rows, block_order, zeros_flat, zeros_flat, zeros_heads),
    )
    grad_keys, grad_values, grad_query = visit_keys(carried)
    grad_keys, grad_values = send_home(grad_keys, grad_values)
    grad_keys = grad_keys.reshape(head_shape)
    grad_values = grad_values.reshape(head_shape)
    grad_q_pre = rotate(grad_query, cosine, -sine_part).reshape(flat_shape).astype(jnp.bfloat16)
    grad_k_pre = rotate(grad_keys, cosine, -sine_part).reshape(flat_shape).astype(jnp.bfloat16)
    grad_v_pre = grad_values.reshape(flat_shape).astype(jnp.bfloat16)
    grad_qkv = jnp.concatenate([grad_q_pre, grad_k_pre, grad_v_pre], -1)
    grad_ln = times_transposed(grad_qkv, qkv_back) + times_transposed(grad_hidden, in_back)
    grad_normed = grad_ln * gain_back.astype(jnp.float32)
    grad_inputs = inverse * (
        grad_normed
        - jnp.mean(grad_normed, -1, keepdims=True)
        - normed * jnp.mean(grad_normed * normed, -1, keepdims=True)
    )
    grad_tokens = (grad_f32 + grad_inputs).astype(jnp.bfloat16)[None]
    term_gain = jnp.sum(grad_ln * normed, 0)
    term_bias = jnp.sum(grad_ln, 0)
    term_qkv = outer_sum(ln_out, grad_qkv)
    term_qv = jnp.stack(
        [jnp.sum(grad_q_pre.astype(jnp.float32), 0), jnp.sum(grad_v_pre.astype(jnp.float32), 0)], 0
    )
    (
        sum_gain,
        sum_bias,
        sum_qkv,
        sum_qv,
        sum_out_w,
        sum_out_b,
        sum_in_w,
        sum_in_b,
        sum_down_w,
        sum_down_b,
    ) = (
        lax.psum_scatter(term_gain, ("ctx", "fsdp"), scatter_dimension=0, tiled=True),
        lax.psum_scatter(term_bias, ("ctx", "fsdp"), scatter_dimension=0, tiled=True),
        lax.psum_scatter(term_qkv, ("ctx", "fsdp"), scatter_dimension=0, tiled=True),
        lax.psum_scatter(term_qv, ("ctx", "fsdp"), scatter_dimension=1, tiled=True),
        lax.psum_scatter(term_out_w, ("ctx", "fsdp"), scatter_dimension=0, tiled=True),
        lax.psum_scatter(cotangent_sum, ("ctx", "fsdp"), scatter_dimension=0, tiled=True),
        lax.psum_scatter(term_in_w, ("ctx", "fsdp"), scatter_dimension=0, tiled=True),
        lax.psum_scatter(term_in_b, ("ctx", "fsdp"), scatter_dimension=0, tiled=True),
        lax.psum_scatter(term_down_w, ("ctx", "fsdp"), scatter_dimension=0, tiled=True),
        lax.psum_scatter(cotangent_sum, ("ctx", "fsdp"), scatter_dimension=0, tiled=True),
    )
    return (
        layer_out,
        grad_tokens,
        sum_gain,
        sum_bias,
        sum_qkv,
        sum_qv,
        sum_out_w,
        sum_out_b,
        sum_in_w,
        sum_in_b,
        sum_down_w,
        sum_down_b,
    )


LINES = 4
ACROSS = HEADS // LINES
F32 = jnp.float32
BF16 = jnp.bfloat16
VMEM_LIMIT = 56 * 1024 * 1024
VEC = 16


def dot(left, right):
    return jnp.dot(left, right, preferred_element_type=F32)


def dot_nt(left, right):
    return lax.dot_general(left, right, (((1,), (1,)), ((), ())), preferred_element_type=F32)


def call(kernel, out_shapes, scratch, flops, *operands):
    specs = [
        pl.BlockSpec(memory_space=pltpu.SMEM if x.dtype == jnp.int32 else pltpu.VMEM)
        for x in operands
    ]
    outs = [jax.ShapeDtypeStruct(s, d) for s, d in out_shapes]
    moved = sum(x.size * x.dtype.itemsize for x in list(operands) + outs)
    return pl.pallas_call(
        kernel,
        out_shape=outs,
        in_specs=specs,
        out_specs=[pl.BlockSpec(memory_space=pltpu.VMEM) for _ in outs],
        scratch_shapes=scratch,
        compiler_params=pltpu.CompilerParams(vmem_limit_bytes=VMEM_LIMIT),
        cost_estimate=pl.CostEstimate(flops=flops, bytes_accessed=moved, transcendentals=0),
    )(*operands)


def reorder(x, place):
    upper, lower = x[:, :128], x[:, 128:]
    far = (place & 2) != 0
    near = (place & 1) != 0
    first = jnp.where(far, lower, upper)
    second = jnp.where(far, upper, lower)
    first = jnp.where(near, pltpu.roll(first, 64, 1), first)
    second = jnp.where(near, pltpu.roll(second, 64, 1), second)
    return first, second


def left_lanes(rows):
    return lax.broadcasted_iota(jnp.int32, (rows, 128), 1) < 64


def pair_heads(one, two, slot):
    keep = left_lanes(one.shape[0])
    if slot % 2 == 0:
        return jnp.where(keep, one, pltpu.roll(two, 64, 1))
    return jnp.where(keep, pltpu.roll(one, 64, 1), two)


def fold_rows(chunk, slot):
    rows = chunk.shape[0] // 2
    return pair_heads(chunk[:rows], chunk[rows:], slot)


def unfold_pair(even, odd):
    keep = left_lanes(even.shape[0])
    top = jnp.where(keep, even, pltpu.roll(odd, 64, 1))
    bottom = jnp.where(keep, pltpu.roll(even, 64, 1), odd)
    return jnp.concatenate([top, bottom], 0)


def normalise(rows):
    x = rows.astype(F32)
    centred = x - jnp.mean(x, -1, keepdims=True)
    inverse = lax.rsqrt(jnp.mean(centred * centred, -1, keepdims=True) + epsilon)
    return centred * inverse, inverse


def project_kernel(at, t0, t1, t2, t3, gain, shift, bias_q, bias_v, w_own, w_twin, *outs):
    slots, ln_ref, lnt_ref = outs[:4], outs[4], outs[5]
    place, core = at[1], at[2]
    rows = t0.shape[0]
    half = w_own.shape[0]
    for k, ref in enumerate((t0, t1, t2, t3)):
        normed, _ = normalise(ref[...])
        low = (normed * gain[...] + shift[...]).astype(BF16)
        ln_ref[rows * k : rows * (k + 1), :] = low
    mine = pl.ds(pl.multiple_of(core * half, half), half)
    other = pl.ds(pl.multiple_of((1 - core) * half, half), half)

    def part(index):
        cols = slice(256 * index, 256 * (index + 1))
        return dot(ln_ref[:, mine], w_own[:, cols]) + dot(ln_ref[:, other], w_twin[:, cols])

    q_chunks = reorder(part(0) + bias_q[...], place)
    k_chunks = reorder(part(1), place)
    v_chunks = reorder(part(2) + bias_v[...], place)
    total = ln_ref.shape[0]
    for slot in range(4):
        pair = slot // 2
        slots[slot][:total, :] = pair_heads(q_chunks[pair], k_chunks[pair], slot).astype(BF16)
        slots[slot][total:, :] = fold_rows(v_chunks[pair], slot).astype(BF16)
    lnt_ref[...] = ln_ref[...].T


def back_rows_kernel(at, c0, c1, c2, c3, w_out, s0, s1, s2, s3):
    cot = jnp.concatenate([c0[...], c1[...], c2[...], c3[...]], 0)
    chunks = reorder(dot_nt(cot, w_out[...]), at[1])
    for slot, ref in enumerate((s0, s1, s2, s3)):
        ref[...] = fold_rows(chunks[slot // 2], slot).astype(BF16)


def sort_rows(table, refs, target, rows, base, folded):
    for j in range(4):
        for i in range(8):
            dest = pl.ds(pl.multiple_of(table[j * 8 + i] * 64, 64), 64)
            if folded:
                source = base + 64 * (i % 4)
                lanes = slice(0, 64) if i < 4 else slice(64, 128)
                target[dest, :] = refs[j][source : source + 64, lanes]
            else:
                target[dest, :] = refs[j][base + 64 * i : base + 64 * (i + 1), :]


def turn(x, cosine, low_sine, high_sine):
    return x * cosine + pltpu.roll(x, 120, 1) * low_sine + pltpu.roll(x, 8, 1) * high_sine


TILE = 256


def scores_of(qk_ref, i):
    rows = slice(TILE * i, TILE * (i + 1))
    queries = jnp.where(left_lanes(TILE), qk_ref[rows, :], jnp.zeros((), BF16))
    queries = queries * jnp.asarray(HEAD_DIM ** (-0.5), BF16)
    return queries


def allowed_tile():
    row = lax.broadcasted_iota(jnp.int32, (TILE, TILE), 0)
    col = lax.broadcasted_iota(jnp.int32, (TILE, TILE), 1)
    return row >= col


def attend_kernel(table, r0, r1, r2, r3, cosine, low_sine, high_sine, *rest):
    a0, a1, a2, a3, qk_ref, kq_ref, v_ref, att_ref, lse_ref, raw = rest
    refs = (r0, r1, r2, r3)
    count = qk_ref.shape[0]
    lines = count // 4
    sort_rows(table, refs, raw, lines, 0, False)
    sort_rows(table, refs, v_ref, lines, lines, True)
    for i in range(count // TILE):
        rows = slice(TILE * i, TILE * (i + 1))
        turned = turn(
            raw[rows, :].astype(F32), cosine[rows, :], low_sine[rows, :], high_sine[rows, :]
        )
        qk_ref[rows, :] = turned.astype(BF16)
        kq_ref[rows, :] = pltpu.roll(turned, 64, 1).astype(BF16)
    mask = allowed_tile()
    for i in range(count // TILE):
        rows = slice(TILE * i, TILE * (i + 1))
        keys = TILE * (i + 1)
        scores = dot_nt(scores_of(qk_ref, i), kq_ref[:keys, :])
        last = jnp.where(mask, scores[:, keys - TILE :], -1e30)
        scores = last if i == 0 else jnp.concatenate([scores[:, : keys - TILE], last], 1)
        top = jnp.max(scores, -1, keepdims=True)
        weights = jnp.exp(scores - top)
        total = jnp.sum(weights, -1, keepdims=True)
        weighted = dot(weights.astype(BF16), v_ref[:keys, :])
        att_ref[rows, :] = weighted / total
        lse_ref[rows, :] = top + jnp.log(total)
    for j, out in enumerate((a0, a1, a2, a3)):
        for i in range(8):
            source = pl.ds(pl.multiple_of(table[j * 8 + i] * 64, 64), 64)
            lanes = slice(0, 64) if i < 4 else slice(64, 128)
            out[64 * (i % 4) : 64 * (i % 4) + 64, lanes] = att_ref[source, :].astype(BF16)


def attend_back_kernel(table, g0, g1, g2, g3, qk_ref, kq_ref, v_ref, att_ref, lse_ref, *rest):
    cosine, low_sine, high_sine, o0, o1, o2, o3, sums, ga_ref, kt_ref, vt_ref, gqk, gv = rest
    count = qk_ref.shape[0]
    lines = count // 4
    sort_rows(table, (g0, g1, g2, g3), ga_ref, lines, 0, True)
    mask = allowed_tile()
    kt_ref[...] = jnp.zeros_like(kt_ref)
    vt_ref[...] = jnp.zeros_like(vt_ref)
    for i in range(count // TILE):
        rows = slice(TILE * i, TILE * (i + 1))
        keys = TILE * (i + 1)
        queries = scores_of(qk_ref, i)
        scores = dot_nt(queries, kq_ref[:keys, :])
        last = jnp.where(mask, scores[:, keys - TILE :], -1e30)
        scores = last if i == 0 else jnp.concatenate([scores[:, : keys - TILE], last], 1)
        probs = jnp.exp(scores - lse_ref[rows, :])
        grad_rows = ga_ref[rows, :]
        delta = jnp.sum(grad_rows.astype(F32) * att_ref[rows, :], -1, keepdims=True)
        grad_probs = dot_nt(grad_rows, v_ref[:keys, :])
        grad_scores = (probs * (grad_probs - delta)).astype(BF16)
        gqk[rows, :] = dot(grad_scores, kq_ref[:keys, :]) * HEAD_DIM ** (-0.5)
        vt_ref[:, :keys] += dot(grad_rows.astype(F32).T.astype(BF16), probs.astype(BF16))
        kt_ref[:, :keys] += dot(queries.astype(F32).T.astype(BF16), grad_scores)
    sum_q = jnp.zeros((1, 128), F32)
    sum_v = jnp.zeros((1, 64), F32)
    for i in range(count // TILE):
        rows = slice(TILE * i, TILE * (i + 1))
        grad_keys = pltpu.roll(kt_ref[:, rows].T, 64, 1)
        both = jnp.where(left_lanes(TILE), gqk[rows, :], grad_keys)
        both = turn(both, cosine[rows, :], -low_sine[rows, :], -high_sine[rows, :])
        both = both.astype(BF16).astype(F32)
        values = vt_ref[:, rows].T.astype(BF16).astype(F32)
        gqk[rows, :] = both
        gv[rows, :] = values
        sum_q = sum_q + jnp.sum(both, 0, keepdims=True)
        sum_v = sum_v + jnp.sum(values, 0, keepdims=True)
    sums[...] = jnp.zeros_like(sums)
    sums[0:1, :64] = sum_q[:, :64]
    sums[1:2, :64] = sum_v
    for j, out in enumerate((o0, o1, o2, o3)):
        for i in range(8):
            source = pl.ds(pl.multiple_of(table[j * 8 + i] * 64, 64), 64)
            lanes = slice(0, 64) if i < 4 else slice(64, 128)
            out[64 * i : 64 * (i + 1), :] = gqk[source, :].astype(BF16)
            base = lines + 64 * (i % 4)
            out[base : base + 64, lanes] = gv[source, :].astype(BF16)


def feed_kernel(at, ln, w_own, w_twin, bias, w_down, hidden_ref, act_ref, actt_ref, low_ref):
    core = at[2]
    half = w_own.shape[0]
    mine = pl.ds(pl.multiple_of(core * half, half), half)
    other = pl.ds(pl.multiple_of((1 - core) * half, half), half)
    for f in range(4):
        cols = slice(256 * f, 256 * (f + 1))
        hidden = dot(ln[:, mine], w_own[:, cols]) + dot(ln[:, other], w_twin[:, cols])
        hidden = hidden + bias[:, cols]
        hidden_ref[:, cols] = hidden
        active = 0.5 * hidden * (1.0 + lax.erf(hidden * 0.7071067811865476))
        act_ref[:, cols] = active.astype(BF16)
        actt_ref[cols, :] = active.astype(BF16).T
    for f in range(4):
        cols = slice(256 * f, 256 * (f + 1))
        low_ref[:, cols] = dot(act_ref[...], w_down[:, cols])


def feed_back_kernel(at, c0, c1, c2, c3, hidden, actt, lnt, w_own, w_twin, w_down, *rest):
    send, keep, low_ref, gh_ref, chunk_ref = rest
    line, core = at[0], at[2]
    half = w_own.shape[0]
    cot = jnp.concatenate([c0[...], c1[...], c2[...], c3[...]], 0)
    block = send.shape[0] // 4
    sums = jnp.zeros((1, 1024), F32)
    cot_sum = jnp.sum(cot.astype(F32), 0, keepdims=True)
    bias_sums = []
    for f in range(4):
        cols = slice(256 * f, 256 * (f + 1))
        grad_active = dot_nt(cot, w_down[cols, :])
        h = hidden[:, cols]
        slope = 0.5 * (1.0 + lax.erf(h * 0.7071067811865476)) + h * jnp.exp(
            -0.5 * h * h
        ) * 0.3989422804014327
        grad_hidden = (slope * grad_active).astype(BF16)
        gh_ref[:, cols] = grad_hidden
        bias_sums.append(jnp.sum(grad_hidden.astype(F32), 0, keepdims=True))
    for f in range(4):
        chunk_ref[...] = dot(actt[256 * f : 256 * (f + 1), :], cot)
        base = block * f
        send[base : base + 128, :] = chunk_ref[
            pl.ds(pl.multiple_of((1 - core) * 128, 128), 128), :
        ].astype(BF16)
        keep[base : base + 128, :] = chunk_ref[pl.ds(pl.multiple_of(core * 128, 128), 128), :]
    for z in range(4):
        chunk_ref[...] = dot(lnt[256 * z : 256 * (z + 1), :], gh_ref[...])
        for f in range(4):
            base = block * f + 128 + 32 * z
            send[base : base + 32, :] = chunk_ref[
                pl.ds(pl.multiple_of(64 * f + 32 * (1 - core), 32), 32), :
            ].astype(BF16)
            keep[base : base + 32, :] = chunk_ref[
                pl.ds(pl.multiple_of(64 * f + 32 * core, 32), 32), :
            ]
    picked = jnp.where(
        line < 2,
        jnp.where(line == 0, cot_sum[:, 0:256], cot_sum[:, 256:512]),
        jnp.where(line == 2, cot_sum[:, 512:768], cot_sum[:, 768:1024]),
    )
    zero = jnp.zeros((1, 640), F32)
    for f in range(4):
        even, odd = bias_sums[f][:, :128], bias_sums[f][:, 128:]
        first = core == 0
        base = block * f + 256
        given = jnp.concatenate([jnp.where(first, odd, even), picked, zero], 1)
        kept = jnp.concatenate([jnp.where(first, even, odd), picked, zero], 1)
        send[base : base + VEC, :] = jnp.broadcast_to(given, (VEC, 1024)).astype(BF16)
        keep[base : base + VEC, :] = jnp.broadcast_to(kept, (VEC, 1024))
    mine = pl.ds(pl.multiple_of(core * half, half), half)
    other = pl.ds(pl.multiple_of((1 - core) * half, half), half)
    low_ref[:, mine] = dot_nt(gh_ref[...], w_own[...])
    low_ref[:, other] = dot_nt(gh_ref[...], w_twin[...])


def add_twin_kernel(at, keep, received, o0, o1, o2, o3):
    block = o0.shape[0]
    for slot, ref in enumerate((o0, o1, o2, o3)):
        rows = pl.ds(pl.multiple_of((at[1] ^ slot) * block, 16), block)
        ref[...] = (keep[rows, :] + received[rows, :].astype(F32)).astype(ref.dtype)


def feed_sum_kernel(at, own, r1, r2, r3, down_ref, vec_ref, i0, i1, i2, i3):
    def total(rows):
        return (
            own[rows, :]
            + r1[rows, :].astype(F32)
            + r2[rows, :].astype(F32)
            + r3[rows, :].astype(F32)
        )

    down_ref[...] = total(slice(0, 128))
    vec_ref[...] = total(slice(256, 264))
    for slot, ref in enumerate((i0, i1, i2, i3)):
        rows = pl.ds(pl.multiple_of(128 + 32 * (at[0] ^ slot), 16), 32)
        ref[...] = total(rows).astype(ref.dtype)


def branch_kernel(at, a0, a1, a2, a3, low, w_out, c0, c1, c2, c3, *rest):
    s0, s1, s2, s3, send, keep, chunk_ref = rest
    place, core = at[1], at[2]
    chunks = (
        unfold_pair(a0[...].astype(F32), a1[...].astype(F32)),
        unfold_pair(a2[...].astype(F32), a3[...].astype(F32)),
    )
    attended = jnp.concatenate(reorder(jnp.concatenate(chunks, 1), place), 1).astype(BF16)
    rows = s0.shape[0]
    for k, ref in enumerate((s0, s1, s2, s3)):
        part = slice(rows * k, rows * (k + 1))
        ref[...] = (low[part, :] + dot(attended[part, :], w_out[...])).astype(ref.dtype)
    cot = jnp.concatenate([c0[...], c1[...], c2[...], c3[...]], 0)
    chunk_ref[...] = dot(attended.T, cot)
    for f in range(4):
        send[32 * f : 32 * (f + 1), :] = chunk_ref[
            pl.ds(pl.multiple_of(64 * f + 32 * (1 - core), 32), 32), :
        ].astype(BF16)
        keep[32 * f : 32 * (f + 1), :] = chunk_ref[
            pl.ds(pl.multiple_of(64 * f + 32 * core, 32), 32), :
        ]


def grads_kernel(at, g0, g1, g2, g3, low, t0, t1, t2, t3, lnt, w_own, w_twin, *rest):
    s0, s1, s2, s3, send, keep, g_ref, low_ref, chunk_ref = rest
    place, core = at[1], at[2]
    half = w_own.shape[0]
    rows = t0.shape[0]
    total = 4 * rows
    parts = [ref[...].astype(F32) for ref in (g0, g1, g2, g3)]
    keep_left = left_lanes(total)
    q_chunks, k_chunks, v_chunks = [], [], []
    for pair in range(2):
        even, odd = parts[2 * pair][:total], parts[2 * pair + 1][:total]
        q_chunks.append(jnp.where(keep_left, even, pltpu.roll(odd, 64, 1)))
        k_chunks.append(jnp.where(keep_left, pltpu.roll(even, 64, 1), odd))
        v_chunks.append(unfold_pair(parts[2 * pair][total:], parts[2 * pair + 1][total:]))
    for index, chunks in enumerate((q_chunks, k_chunks, v_chunks)):
        first, second = reorder(jnp.concatenate(chunks, 1), place)
        g_ref[:, 256 * index : 256 * index + 128] = first.astype(BF16)
        g_ref[:, 256 * index + 128 : 256 * index + 256] = second.astype(BF16)
    mine = pl.ds(pl.multiple_of(core * half, half), half)
    other = pl.ds(pl.multiple_of((1 - core) * half, half), half)
    low_ref[:, mine] = low[:, mine] + dot_nt(g_ref[...], w_own[...])
    low_ref[:, other] = low[:, other] + dot_nt(g_ref[...], w_twin[...])
    sum_gain = jnp.zeros((1, 1024), F32)
    sum_bias = jnp.zeros((1, 1024), F32)
    for k, (ref, out) in enumerate(zip((t0, t1, t2, t3), (s0, s1, s2, s3))):
        grad = low_ref[rows * k : rows * (k + 1), :]
        out[...] = grad.astype(out.dtype)
        normed, _ = normalise(ref[...])
        sum_gain = sum_gain + jnp.sum(grad * normed, 0, keepdims=True)
        sum_bias = sum_bias + jnp.sum(grad, 0, keepdims=True)
    block = send.shape[0] // 4
    for z in range(4):
        chunk_ref[...] = dot(lnt[256 * z : 256 * (z + 1), :], g_ref[...])
        for f in range(4):
            base = block * f + 32 * z
            send[base : base + 32, :] = chunk_ref[
                pl.ds(pl.multiple_of(64 * f + 32 * (1 - core), 32), 32), :
            ].astype(BF16)
            keep[base : base + 32, :] = chunk_ref[
                pl.ds(pl.multiple_of(64 * f + 32 * core, 32), 32), :
            ]
    zero = jnp.zeros((1, 512), F32)
    vec = jnp.concatenate(
        [
            sum_gain[:, :768],
            sum_bias[:, :768],
            jnp.concatenate([sum_gain[:, 768:], zero], 1),
            jnp.concatenate([sum_bias[:, 768:], zero], 1),
            jnp.zeros((VEC - 4, 768), F32),
        ],
        0,
    )
    for f in range(4):
        base = block * f + 128
        send[base : base + VEC, :] = vec.astype(BF16)
        keep[base : base + VEC, :] = vec


def grad_sum_kernel(at, own, r1, r2, r3, i0, i1, i2, i3):
    def total(rows):
        return (
            own[rows, :]
            + r1[rows, :].astype(F32)
            + r2[rows, :].astype(F32)
            + r3[rows, :].astype(F32)
        )

    vec = total(slice(128, 128 + VEC))
    for slot, ref in enumerate((i0, i1, i2, i3)):
        rows = pl.ds(pl.multiple_of(32 * (at[0] ^ slot), 16), 32)
        ref[:32, :] = total(rows).astype(ref.dtype)
        ref[32:, :] = vec.astype(ref.dtype)


def out_sum_kernel(own, r1, r2, r3, out):
    out[...] = own[...] + r1[...].astype(F32) + r2[...].astype(F32) + r3[...].astype(F32)


def join_in_kernel(at, i0, i1, i2, i3, out):
    for slot, ref in enumerate((i0, i1, i2, i3)):
        cols = pl.ds(pl.multiple_of((at[0] ^ slot) * 1024, 1024), 1024)
        out[:, cols] = ref[...].astype(F32)


def join_qkv_kernel(at, i0, i1, i2, i3, out, vec_ref):
    vec = jnp.zeros((VEC, 768), F32)
    for slot, ref in enumerate((i0, i1, i2, i3)):
        for part in range(3):
            cols = pl.ds(pl.multiple_of(1024 * part + (at[0] ^ slot) * 256, 256), 256)
            out[:, cols] = ref[:32, 256 * part : 256 * (part + 1)].astype(F32)
        vec = vec + ref[32:, :].astype(F32)
    vec_ref[...] = vec


def layer_kernel(own, r1, r2, r3, tokens, b_out, b_down, out):
    total = own[...] + r1[...].astype(F32) + r2[...].astype(F32) + r3[...].astype(F32)
    total = total + tokens[...].astype(F32) + b_out[...] + b_down[...]
    out[...] = total.astype(BF16)


def tokens_kernel(own, r1, r2, r3, tokens, cot, gain, out):
    grad_ln = own[...] + r1[...].astype(F32) + r2[...].astype(F32) + r3[...].astype(F32)
    normed, inverse = normalise(tokens[...])
    g = grad_ln * gain[...]
    grad = inverse * (
        g - jnp.mean(g, -1, keepdims=True) - normed * jnp.mean(g * normed, -1, keepdims=True)
    )
    out[...] = (cot[...].astype(F32) + grad).astype(BF16)


def turn_tables(count):
    cosine, sine_part = tables(jnp.arange(count, dtype=jnp.int32))
    half_rot = ROT // 2
    cosine, sine_part = cosine[:, :half_rot], sine_part[:, :half_rot]
    rest = HEAD_DIM - ROT
    ones = jnp.ones((count, rest), F32)
    zeros = jnp.zeros((count, rest), F32)
    none = jnp.zeros((count, half_rot), F32)
    whole = jnp.concatenate([cosine, cosine, ones], -1)
    low_sine = jnp.concatenate([-sine_part, none, zeros], -1)
    high_sine = jnp.concatenate([none, sine_part, zeros], -1)
    return tuple(jnp.concatenate([t, t], -1) for t in (whole, low_sine, high_sine))


def head_body(
    tokens,
    block_order,
    ln_gain,
    ln_bias,
    w_qkv,
    qv_bias,
    w_out,
    b_out,
    w_in,
    b_in,
    w_down,
    b_down,
    cotangent,
):
    context = lax.axis_index("ctx")
    line, place = context // ACROSS, context % ACROSS
    core = lax.axis_index("fsdp")
    at = jnp.stack([line, place, core]).astype(jnp.int32)
    positions = range(LINES * ACROSS)

    def over_lines(x, k):
        return lax.ppermute(x, "ctx", [(i, i ^ (k * ACROSS)) for i in positions])

    def over_places(x, j):
        return lax.ppermute(x, "ctx", [(i, i ^ j) for i in positions])

    def twin(x):
        return lax.ppermute(x, "fsdp", [(0, 1), (1, 0)])

    def with_lines(x):
        return [x] + [over_lines(x, k) for k in range(1, LINES)]

    def with_places(x):
        return [x] + [over_places(x, j) for j in range(1, ACROSS)]

    rows, width = tokens.shape[1], tokens.shape[2]
    half = w_qkv.shape[0]
    feed = w_in.shape[1]
    owner = line // (LINES // 2)
    part = line % (LINES // 2)
    head_cols = width // LINES
    feed_cols = feed // LINES

    token_lines = with_lines(tokens[0])
    cot_lines = with_lines(cotangent[0])
    orders = jnp.stack(with_lines(block_order), 0).reshape(LINES, 2)
    table = jnp.stack(with_places(orders), 0).reshape(2 * LINES * ACROSS)

    cut = lax.dynamic_slice
    qkv_own = jnp.concatenate(
        [cut(w_qkv, (0, width * i + head_cols * line), (half, head_cols)) for i in range(3)], 1
    )
    qkv_twin = twin(qkv_own)
    in_own = cut(w_in, (0, feed_cols * line), (half, feed_cols))
    in_twin = twin(in_own)
    out_cut = cut(w_out, (head_cols * part, 0), (head_cols, width))
    out_rows = jnp.where(core == owner, out_cut, twin(out_cut))
    down_cut = cut(w_down, (feed_cols * part, 0), (feed_cols, width))
    down_rows = jnp.where(core == owner, down_cut, twin(down_cut))
    vectors = jnp.concatenate(
        [
            ln_gain,
            ln_bias,
            b_out,
            b_down,
            cut(qv_bias, (0, head_cols * part), (2, head_cols)).reshape(-1),
            cut(b_in, (feed_cols * part,), (feed_cols,)),
        ]
    )
    twin_vectors = twin(vectors)
    ours = vectors.astype(F32)
    theirs = twin_vectors.astype(F32)
    pair = jnp.where(core == 0, jnp.stack([ours, theirs]), jnp.stack([theirs, ours]))
    gain, shift, out_bias, down_bias = (
        pair[:, half * i : half * (i + 1)].reshape(1, width) for i in range(4)
    )
    chosen = jnp.where(core == owner, ours, theirs)[None, 4 * half :]
    bias_q = chosen[:, :head_cols]
    bias_v = chosen[:, head_cols : 2 * head_cols]
    bias_in = chosen[:, 2 * head_cols :]
    length = rows * LINES * ACROSS
    rotation = turn_tables(length)
    line_rows = rows * LINES
    slot_shape = (line_rows * 3 // 2, 128)
    fold_shape = (line_rows // 2, 128)

    *qkv_slots, ln_low, ln_turned = call(
        project_kernel,
        [(slot_shape, BF16)] * 4 + [((line_rows, width), BF16), ((width, line_rows), BF16)],
        [],
        2 * line_rows * width * 3 * head_cols,
        at, *token_lines, gain, shift, bias_q, bias_v, qkv_own, qkv_twin,
    )
    qkv_in = [qkv_slots[0]] + [over_places(qkv_slots[j], j) for j in range(1, 4)]
    back_slots = call(
        back_rows_kernel,
        [(fold_shape, BF16)] * 4,
        [],
        2 * line_rows * width * head_cols,
        at, *cot_lines, out_rows,
    )
    back_in = [back_slots[0]] + [over_places(back_slots[j], j) for j in range(1, 4)]
    hidden, _, active_turned, feed_low = call(
        feed_kernel,
        [
            ((line_rows, feed_cols), F32),
            ((line_rows, feed_cols), BF16),
            ((feed_cols, line_rows), BF16),
            ((line_rows, width), F32),
        ],
        [],
        4 * line_rows * width * feed_cols,
        at, ln_low, in_own, in_twin, bias_in, down_rows,
    )
    *att_slots, qk_rows, kq_rows, value_rows, attended, lse = call(
        attend_kernel,
        [(fold_shape, BF16)] * 4
        + [
            ((length, 128), BF16),
            ((length, 128), BF16),
            ((length, 64), BF16),
            ((length, 64), F32),
            ((length, 1), F32),
        ],
        [pltpu.VMEM((length, 128), BF16)],
        4 * length * length * 64,
        table, *qkv_in, *rotation,
    )
    att_in = [att_slots[0]] + [over_places(att_slots[j], j) for j in range(1, 4)]
    block = 128 + 128 + VEC
    feed_send, feed_keep, feed_grad_low = call(
        feed_back_kernel,
        [((4 * block, width), BF16), ((4 * block, width), F32), ((line_rows, width), F32)],
        [pltpu.VMEM((line_rows, feed_cols), BF16), pltpu.VMEM((256, 1024), F32)],
        8 * line_rows * width * feed_cols,
        at, *cot_lines, hidden, active_turned, ln_turned, in_own, in_twin, down_rows,
    )
    feed_blocks = call(
        add_twin_kernel,
        [((block, width), F32)] + [((block, width), BF16)] * 3,
        [],
        0,
        at, feed_keep, twin(feed_send),
    )
    feed_in = [feed_blocks[0]] + [over_places(feed_blocks[j], j) for j in range(1, 4)]
    grad_down, feed_vec, *in_slots = call(
        feed_sum_kernel,
        [((128, width), F32), ((8, width), F32), ((32, width), F32)] + [((32, width), BF16)] * 3,
        [],
        0,
        at, *feed_in,
    )
    in_parts = [in_slots[0]] + [over_lines(in_slots[k], k) for k in range(1, 4)]
    (grad_in,) = call(join_in_kernel, [((32, feed), F32)], [], 0, at, *in_parts)

    *low_slots, out_send, out_keep = call(
        branch_kernel,
        [((rows, width), F32)]
        + [((rows, width), BF16)] * 3
        + [((128, width), BF16), ((128, width), F32)],
        [pltpu.VMEM((256, 1024), F32)],
        4 * line_rows * width * head_cols,
        at, *att_in, feed_low, out_rows, *cot_lines,
    )
    low_in = [low_slots[0]] + [over_lines(low_slots[k], k) for k in range(1, 4)]
    (layer_out,) = call(
        layer_kernel, [((rows, width), BF16)], [], 0, *low_in, tokens[0], out_bias, down_bias
    )
    out_blocks = call(
        add_twin_kernel,
        [((32, width), F32)] + [((32, width), BF16)] * 3,
        [],
        0,
        at, out_keep, twin(out_send),
    )
    out_in = [out_blocks[0]] + [over_places(out_blocks[j], j) for j in range(1, 4)]
    (grad_out,) = call(out_sum_kernel, [((32, width), F32)], [], 0, *out_in)

    *grad_slots, bias_sums = call(
        attend_back_kernel,
        [(slot_shape, BF16)] * 4 + [((8, 128), F32)],
        [
            pltpu.VMEM((length, 64), BF16),
            pltpu.VMEM((128, length), F32),
            pltpu.VMEM((64, length), F32),
            pltpu.VMEM((length, 128), F32),
            pltpu.VMEM((length, 64), F32),
        ],
        10 * length * length * 64,
        table, *back_in, qk_rows, kq_rows, value_rows, attended, lse, *rotation,
    )
    bias_sums = bias_sums + twin(bias_sums)
    grad_in_slots = [grad_slots[0]] + [over_places(grad_slots[j], j) for j in range(1, 4)]
    qkv_cols = 3 * head_cols
    qkv_block = 128 + VEC
    *ln_slots, qkv_send, qkv_keep = call(
        grads_kernel,
        [((rows, width), F32)]
        + [((rows, width), BF16)] * 3
        + [((4 * qkv_block, qkv_cols), BF16), ((4 * qkv_block, qkv_cols), F32)],
        [
            pltpu.VMEM((line_rows, qkv_cols), BF16),
            pltpu.VMEM((line_rows, width), F32),
            pltpu.VMEM((256, qkv_cols), F32),
        ],
        4 * line_rows * width * qkv_cols,
        at, *grad_in_slots, feed_grad_low, *token_lines, ln_turned, qkv_own, qkv_twin,
    )
    ln_in = [ln_slots[0]] + [over_lines(ln_slots[k], k) for k in range(1, 4)]
    (grad_tokens,) = call(
        tokens_kernel, [((rows, width), BF16)], [], 0, *ln_in, tokens[0], cotangent[0], gain
    )
    qkv_blocks = call(
        add_twin_kernel,
        [((qkv_block, qkv_cols), F32)] + [((qkv_block, qkv_cols), BF16)] * 3,
        [],
        0,
        at, qkv_keep, twin(qkv_send),
    )
    qkv_sums = [qkv_blocks[0]] + [over_places(qkv_blocks[j], j) for j in range(1, 4)]
    qkv_parts = call(
        grad_sum_kernel,
        [((32 + VEC, qkv_cols), F32)] + [((32 + VEC, qkv_cols), BF16)] * 3,
        [],
        0,
        at, *qkv_sums,
    )
    qkv_parts = [qkv_parts[0]] + [over_lines(qkv_parts[k], k) for k in range(1, 4)]
    grad_qkv, ln_vec = call(
        join_qkv_kernel,
        [((32, 3 * width), F32), ((VEC, qkv_cols), F32)],
        [],
        0,
        at, *qkv_parts,
    )
    index = context * 2 + core
    gains = jnp.concatenate([ln_vec[0], ln_vec[2, :256]])
    shifts = jnp.concatenate([ln_vec[1], ln_vec[3, :256]])
    grad_gain = cut(gains, (32 * index,), (32,))
    grad_shift = cut(shifts, (32 * index,), (32,))
    grad_qv = cut(bias_sums, (0, 32 * core), (2, 32))
    grad_b_in = feed_vec[0, :128]
    grad_b = cut(feed_vec, (0, 128 + 64 * place + 32 * core), (1, 32))[0]
    return (
        layer_out[None],
        grad_tokens[None],
        grad_gain,
        grad_shift,
        grad_qkv,
        grad_qv,
        grad_out,
        grad_b,
        grad_in,
        grad_b_in,
        grad_down,
        grad_b,
    )


def solution(mesh):
    one_head_each = mesh.shape["ctx"] == HEADS and mesh.shape["fsdp"] == 2
    return jax.shard_map(
        head_body if one_head_each else body,
        mesh=mesh,
        in_specs=(
            P("fsdp", "ctx", None),
            P("ctx", None),
            P("fsdp"),
            P("fsdp"),
            P("fsdp", None),
            P(None, "fsdp"),
            P("fsdp", None),
            P("fsdp"),
            P("fsdp", None),
            P("fsdp"),
            P("fsdp", None),
            P("fsdp"),
            P("fsdp", "ctx", None),
        ),
        out_specs=(
            P("fsdp", "ctx", None),
            P("fsdp", "ctx", None),
            P(("ctx", "fsdp")),
            P(("ctx", "fsdp")),
            P(("ctx", "fsdp"), None),
            P(None, ("ctx", "fsdp")),
            P(("ctx", "fsdp"), None),
            P(("ctx", "fsdp")),
            P(("ctx", "fsdp"), None),
            P(("ctx", "fsdp")),
            P(("ctx", "fsdp"), None),
            P(("ctx", "fsdp")),
        ),
        check_vma=False,
    )
```

```python
from functools import partial
import math

import jax
import jax.numpy as jnp
import numpy as np
from jax import lax
from jax.experimental import pallas as pl
from jax.experimental.pallas import tpu as pltpu
from jax.sharding import PartitionSpec as P

HEADS = 16
HEAD_DIM = 64
ROT = 16


epsilon = 1e-05


def from_behind(block, axis, distance):
    devices = range(lax.axis_size(axis))
    route = [((i - distance) % len(devices), i) for i in devices]
    return lax.ppermute(block, axis, route)


def rotate(vectors, cosine, sine_part):
    half_rot = ROT // 2
    rotary_part = vectors[..., :ROT]
    turned = jnp.concatenate([-rotary_part[..., half_rot:], rotary_part[..., :half_rot]], -1)
    return jnp.concatenate([rotary_part * cosine + turned * sine_part, vectors[..., ROT:]], -1)


def tables(positions):
    freq_index = jnp.arange(ROT // 2, dtype=jnp.float32)
    inverse = 10000.0 ** (-2.0 * freq_index / ROT)
    angles = positions.astype(jnp.float32)[:, None] * inverse[None, :]
    angles = jnp.concatenate([angles, angles], -1)
    return (jnp.cos(angles), jnp.sin(angles))


def spread_positions(orders, half_rows):
    offsets = jnp.arange(half_rows, dtype=jnp.int32)
    return (orders[:, :, None] * half_rows + offsets[None, None, :]).reshape(-1)


def outer_sum(left_side, right_side):
    return lax.dot_general(
        left_side, right_side, (((0,), (0,)), ((), ())), preferred_element_type=jnp.float32
    )


def times_transposed(left_side, right_side):
    return lax.dot_general(
        left_side, right_side, (((1,), (1,)), ((), ())), preferred_element_type=jnp.float32
    )


def attend_block(carried, queries, query_pos, key_rows, value_rows, key_pos, score_scale):
    row_max, row_sum, weighted = carried
    scores = (
        jnp.einsum("qhd,khd->hqk", queries, key_rows, preferred_element_type=jnp.float32)
        * score_scale
    )
    allowed = (query_pos[:, None] >= key_pos[None, :])[None]
    new_max = jnp.maximum(row_max, jnp.max(jnp.where(allowed, scores, -1e30), -1))
    weights = jnp.where(allowed, jnp.exp(scores - new_max[:, :, None]), 0.0)
    rescale = jnp.exp(row_max - new_max)
    row_sum = row_sum * rescale + jnp.sum(weights, -1)
    weighted = weighted * rescale.T[:, :, None] + jnp.einsum(
        "hqk,khd->qhd", weights.astype(jnp.bfloat16), value_rows, preferred_element_type=jnp.float32
    )
    return (new_max, row_sum, weighted)


def block_grads(
    queries, grad_rows, log_sum, delta_rows, query_pos, key_rows, value_rows, key_pos, score_scale
):
    scores = (
        jnp.einsum("qhd,khd->hqk", queries, key_rows, preferred_element_type=jnp.float32)
        * score_scale
    )
    allowed = (query_pos[:, None] >= key_pos[None, :])[None]
    probs = jnp.where(allowed, jnp.exp(scores - log_sum[:, :, None]), 0.0)
    grad_values = jnp.einsum(
        "hqk,qhd->khd", probs.astype(jnp.bfloat16), grad_rows, preferred_element_type=jnp.float32
    )
    grad_probs = jnp.einsum(
        "qhd,khd->hqk", grad_rows, value_rows, preferred_element_type=jnp.float32
    )
    grad_scores = (probs * (grad_probs - delta_rows[:, :, None])).astype(jnp.bfloat16)
    grad_queries = (
        jnp.einsum("hqk,khd->qhd", grad_scores, key_rows, preferred_element_type=jnp.float32)
        * score_scale
    )
    grad_keys = (
        jnp.einsum("hqk,qhd->khd", grad_scores, queries, preferred_element_type=jnp.float32)
        * score_scale
    )
    return (grad_queries, grad_keys, grad_values)


def body(
    tokens,
    block_order,
    ln_gain,
    ln_bias,
    w_qkv,
    qv_bias,
    w_out,
    b_out,
    w_in,
    b_in,
    w_down,
    b_down,
    cotangent,
):
    gathered = (
        lax.all_gather(ln_gain, "fsdp", axis=0, tiled=True),
        lax.all_gather(ln_bias, "fsdp", axis=0, tiled=True),
        lax.all_gather(w_qkv, "fsdp", axis=0, tiled=True),
        lax.all_gather(qv_bias, "fsdp", axis=1, tiled=True),
        lax.all_gather(w_out, "fsdp", axis=0, tiled=True),
        lax.all_gather(b_out, "fsdp", axis=0, tiled=True),
        lax.all_gather(w_in, "fsdp", axis=0, tiled=True),
        lax.all_gather(b_in, "fsdp", axis=0, tiled=True),
        lax.all_gather(w_down, "fsdp", axis=0, tiled=True),
        lax.all_gather(b_down, "fsdp", axis=0, tiled=True),
    )
    (
        gain_full,
        shift_full,
        qkv_full,
        bias_full,
        out_full,
        out_bias,
        in_full,
        in_bias,
        down_full,
        down_bias,
    ) = gathered
    tok_rows = tokens.shape[1]
    model_width = tokens.shape[2]
    half_rows = tok_rows // 2
    score_scale = HEAD_DIM ** (-0.5)
    head_shape = (tok_rows, HEADS, HEAD_DIM)
    flat_shape = (tok_rows, model_width)
    inputs = tokens[0].astype(jnp.float32)
    row_mean = jnp.mean(inputs, -1, keepdims=True)
    centered = inputs - row_mean
    inverse = lax.rsqrt(jnp.mean(centered * centered, -1, keepdims=True) + epsilon)
    normed = centered * inverse
    ln_out = (normed * gain_full.astype(jnp.float32) + shift_full.astype(jnp.float32)).astype(
        jnp.bfloat16
    )
    qkv_pre = jnp.dot(ln_out, qkv_full, preferred_element_type=jnp.float32)
    positions = spread_positions(block_order, half_rows)
    cosine, sine_part = tables(positions)
    cosine = cosine[:, None, :]
    sine_part = sine_part[:, None, :]
    query_pre = qkv_pre[:, :model_width] + bias_full[0].astype(jnp.float32)
    query_rows = rotate(query_pre.reshape(head_shape), cosine, sine_part).astype(jnp.bfloat16)
    key_rows = rotate(
        qkv_pre[:, model_width : 2 * model_width].reshape(head_shape), cosine, sine_part
    ).astype(jnp.bfloat16)
    value_rows = (qkv_pre[:, 2 * model_width :] + bias_full[1].astype(jnp.float32)).astype(
        jnp.bfloat16
    )
    key_flat = key_rows.reshape(flat_shape)
    start_state = (
        jnp.full((HEADS, tok_rows), -1e30, jnp.float32),
        jnp.zeros((HEADS, tok_rows), jnp.float32),
        jnp.zeros(head_shape, jnp.float32),
    )
    carried = start_state
    piece_keys = lax.all_gather(key_flat, "ctx", axis=0, tiled=True)
    piece_values = lax.all_gather(value_rows, "ctx", axis=0, tiled=True)
    piece_orders = lax.all_gather(block_order, "ctx", axis=0, tiled=True)
    shard_count = piece_orders.shape[0]
    group_size = math.gcd(shard_count, max(1, 1024 // tok_rows))
    rounds = shard_count // group_size
    stacked = (
        piece_keys.reshape(rounds, group_size * tok_rows, HEADS, HEAD_DIM),
        piece_values.reshape(rounds, group_size * tok_rows, HEADS, HEAD_DIM),
        piece_orders.reshape(rounds, group_size, 2),
    )

    def one_round(inner_state, block_item):
        key_pos = spread_positions(block_item[2], half_rows)
        return (
            attend_block(
                inner_state,
                query_rows,
                positions,
                block_item[0],
                block_item[1],
                key_pos,
                score_scale,
            ),
            None,
        )

    carried, _ = lax.scan(one_round, carried, stacked)
    row_max, row_sum, weighted = carried
    attended_f32 = weighted / row_sum.T[:, :, None]
    log_sum = row_max + jnp.log(row_sum)
    attended = attended_f32.reshape(flat_shape).astype(jnp.bfloat16)
    branch = jnp.dot(attended, out_full, preferred_element_type=jnp.float32) + out_bias.astype(
        jnp.float32
    )
    hidden = jnp.dot(ln_out, in_full, preferred_element_type=jnp.float32) + in_bias.astype(
        jnp.float32
    )
    active = jax.nn.gelu(hidden, approximate=False).astype(jnp.bfloat16)
    feed_out = jnp.dot(active, down_full, preferred_element_type=jnp.float32) + down_bias.astype(
        jnp.float32
    )
    layer_out = (inputs + branch + feed_out).astype(jnp.bfloat16)[None]
    gain_back, qkv_back, out_back, in_back, down_back = (
        gain_full,
        qkv_full,
        out_full,
        in_full,
        down_full,
    )
    grad_out = cotangent[0]
    grad_f32 = grad_out.astype(jnp.float32)
    grad_attended = times_transposed(grad_out, out_back).astype(jnp.bfloat16).reshape(head_shape)
    grad_active = times_transposed(grad_out, down_back)
    _, gelu_pull = jax.vjp(partial(jax.nn.gelu, approximate=False), hidden)
    grad_hidden = gelu_pull(grad_active)[0].astype(jnp.bfloat16)
    delta_rows = jnp.sum(grad_attended.astype(jnp.float32) * attended_f32, -1).T
    cotangent_sum = jnp.sum(grad_f32, 0)
    term_out_w = outer_sum(attended, grad_out)
    term_in_w = outer_sum(ln_out, grad_hidden)
    term_in_b = jnp.sum(grad_hidden.astype(jnp.float32), 0)
    term_down_w = outer_sum(active, grad_out)
    cycle_size = lax.axis_size("ctx")
    zeros_flat = jnp.zeros(flat_shape, jnp.float32)
    zeros_heads = jnp.zeros(head_shape, jnp.float32)

    def send_home(grad_keys, grad_values):
        return (
            from_behind(grad_keys.astype(jnp.bfloat16), "ctx", 1).astype(grad_keys.dtype),
            from_behind(grad_values.astype(jnp.bfloat16), "ctx", 1).astype(grad_values.dtype),
        )

    def visit_keys(carried):
        visit_key, visit_value, visit_order, grad_keys, grad_values, grad_query = carried
        part_query, part_key, part_value = block_grads(
            query_rows,
            grad_attended,
            log_sum,
            delta_rows,
            positions,
            visit_key.reshape(head_shape),
            visit_value.reshape(head_shape),
            spread_positions(visit_order, half_rows),
            score_scale,
        )
        return (
            grad_keys + part_key.reshape(flat_shape),
            grad_values + part_value.reshape(flat_shape),
            grad_query + part_query,
        )

    def cycle_step(step_index, carried):
        grad_keys, grad_values, grad_query = visit_keys(carried)
        visit_key, visit_value, visit_order = from_behind(
            (carried[0], carried[1], carried[2]), "ctx", 1
        )
        grad_keys, grad_values = send_home(grad_keys, grad_values)
        return (visit_key, visit_value, visit_order, grad_keys, grad_values, grad_query)

    carried = lax.fori_loop(
        0,
        cycle_size - 1,
        cycle_step,
        (key_flat, value_rows, block_order, zeros_flat, zeros_flat, zeros_heads),
    )
    grad_keys, grad_values, grad_query = visit_keys(carried)
    grad_keys, grad_values = send_home(grad_keys, grad_values)
    grad_keys = grad_keys.reshape(head_shape)
    grad_values = grad_values.reshape(head_shape)
    grad_q_pre = rotate(grad_query, cosine, -sine_part).reshape(flat_shape).astype(jnp.bfloat16)
    grad_k_pre = rotate(grad_keys, cosine, -sine_part).reshape(flat_shape).astype(jnp.bfloat16)
    grad_v_pre = grad_values.reshape(flat_shape).astype(jnp.bfloat16)
    grad_qkv = jnp.concatenate([grad_q_pre, grad_k_pre, grad_v_pre], -1)
    grad_ln = times_transposed(grad_qkv, qkv_back) + times_transposed(grad_hidden, in_back)
    grad_normed = grad_ln * gain_back.astype(jnp.float32)
    grad_inputs = inverse * (
        grad_normed
        - jnp.mean(grad_normed, -1, keepdims=True)
        - normed * jnp.mean(grad_normed * normed, -1, keepdims=True)
    )
    grad_tokens = (grad_f32 + grad_inputs).astype(jnp.bfloat16)[None]
    term_gain = jnp.sum(grad_ln * normed, 0)
    term_bias = jnp.sum(grad_ln, 0)
    term_qkv = outer_sum(ln_out, grad_qkv)
    term_qv = jnp.stack(
        [jnp.sum(grad_q_pre.astype(jnp.float32), 0), jnp.sum(grad_v_pre.astype(jnp.float32), 0)], 0
    )
    (
        sum_gain,
        sum_bias,
        sum_qkv,
        sum_qv,
        sum_out_w,
        sum_out_b,
        sum_in_w,
        sum_in_b,
        sum_down_w,
        sum_down_b,
    ) = (
        lax.psum_scatter(term_gain, ("ctx", "fsdp"), scatter_dimension=0, tiled=True),
        lax.psum_scatter(term_bias, ("ctx", "fsdp"), scatter_dimension=0, tiled=True),
        lax.psum_scatter(term_qkv, ("ctx", "fsdp"), scatter_dimension=0, tiled=True),
        lax.psum_scatter(term_qv, ("ctx", "fsdp"), scatter_dimension=1, tiled=True),
        lax.psum_scatter(term_out_w, ("ctx", "fsdp"), scatter_dimension=0, tiled=True),
        lax.psum_scatter(cotangent_sum, ("ctx", "fsdp"), scatter_dimension=0, tiled=True),
        lax.psum_scatter(term_in_w, ("ctx", "fsdp"), scatter_dimension=0, tiled=True),
        lax.psum_scatter(term_in_b, ("ctx", "fsdp"), scatter_dimension=0, tiled=True),
        lax.psum_scatter(term_down_w, ("ctx", "fsdp"), scatter_dimension=0, tiled=True),
        lax.psum_scatter(cotangent_sum, ("ctx", "fsdp"), scatter_dimension=0, tiled=True),
    )
    return (
        layer_out,
        grad_tokens,
        sum_gain,
        sum_bias,
        sum_qkv,
        sum_qv,
        sum_out_w,
        sum_out_b,
        sum_in_w,
        sum_in_b,
        sum_down_w,
        sum_down_b,
    )


LINES = 4
ACROSS = HEADS // LINES
F32 = jnp.float32
BF16 = jnp.bfloat16
VMEM_LIMIT = 16 * 1024 * 1024
TIMES = {'branch': 500, 'layer': 500}

VEC = 16


def dot(left, right):
    return jnp.dot(left, right, preferred_element_type=F32)


def dot_nt(left, right):
    return lax.dot_general(left, right, (((1,), (1,)), ((), ())), preferred_element_type=F32)


class Far(tuple):
    pass


class Near(tuple):
    pass


def far(*x):
    return Far(x)


def near(*x):
    return Near(x)


def raw(x):
    return x[0] if isinstance(x, (Far, Near)) else x


def spot():
    context = lax.axis_index("ctx")
    return context // ACROSS, context % ACROSS, lax.axis_index("fsdp")


def call(kernel, out_shapes, scratch, *operands, after=(), loose_in=0):
    whole = pl.BlockSpec(memory_space=pltpu.VMEM)
    loose = pl.BlockSpec(memory_space=pl.ANY)
    arrays, specs = [], []
    for x in operands:
        if isinstance(x, Far):
            arrays.append(pltpu.with_memory_space_constraint(x[0], pltpu.HBM))
        elif isinstance(x, Near):
            arrays.append(pltpu.with_memory_space_constraint(x[0], pltpu.VMEM))
        else:
            arrays.append(x)
        if arrays[-1].dtype == jnp.int32 and arrays[-1].ndim == 1:
            specs.append(pl.BlockSpec(memory_space=pltpu.SMEM))
        else:
            specs.append(loose if len(specs) < loose_in else whole)
    outs = []
    for shape in out_shapes:
        if isinstance(shape, Far):
            outs.append(pltpu.HBM(*shape))
        elif isinstance(shape, Near):
            outs.append(pltpu.VMEM(*shape))
        else:
            outs.append(jax.ShapeDtypeStruct(*shape))
    count = len(arrays)

    def body(*refs):
        kernel(*refs[:count], *refs[count + len(after) :])

    name = kernel.__name__.removesuffix("_kernel")
    results = pl.pallas_call(
        body,
        name=name,
        out_shape=outs,
        in_specs=specs + [loose] * len(after),
        out_specs=[whole for _ in outs],
        scratch_shapes=scratch,
        compiler_params=pltpu.CompilerParams(vmem_limit_bytes=VMEM_LIMIT),
        cost_estimate=pl.CostEstimate(
            flops=TIMES.get(name, 0) * 115_000_000, bytes_accessed=0, transcendentals=0
        ),
    )(*arrays, *map(raw, after))
    return [
        near(x) if isinstance(shape, Near) else x for x, shape in zip(results, out_shapes)
    ]


def run_copies(pairs, sems):
    copies = [pltpu.make_async_copy(x, y, sems.at[i]) for i, (x, y) in enumerate(pairs)]
    for copy in copies:
        copy.start()
    for copy in copies:
        copy.wait()


def prepare_kernel(qkv, w_in, w_out, w_down, gain, shift, b_out, b_down, qv, b_in, packed, sems):
    line, _, _ = spot()
    heads, feed = qkv.shape[1] // 12, w_in.shape[1] // LINES
    part = line % (LINES // 2)
    row = 0
    pairs = []
    for source in (
        w_in.at[:, pl.ds(pl.multiple_of(feed * line, 128), feed)],
        w_out.at[pl.ds(pl.multiple_of(heads * part, 16), heads), :],
        w_down.at[pl.ds(pl.multiple_of(feed * part, 16), feed), :],
    ):
        pairs.append((source, packed.at[row : row + source.shape[0], :]))
        row += source.shape[0]
    half = qkv.shape[0]
    for i in range(3):
        columns = pl.ds(pl.multiple_of(heads * (LINES * i + line), 128), heads)
        pairs.append(
            (qkv.at[:, columns], packed.at[row : row + half, heads * i : heads * (i + 1)])
        )
    row += half
    rows = [x[...].astype(F32).reshape(1, half) for x in (gain, shift, b_out, b_down)]
    rows += [qv[...].astype(F32), b_in[...].astype(F32).reshape(4, half)]
    rows.append(jnp.zeros((VEC - 10, half), F32))
    packed[row : row + VEC, :half] = jnp.concatenate(rows, 0).astype(BF16)
    run_copies(pairs, sems)


def assemble_kernel(own, twin, qkv, w_in, w_out, w_down, vectors, low, sems):
    line, _, core = spot()
    half = qkv.shape[0] // 2
    heads, feed = w_out.shape[0], w_down.shape[0]
    qkv_row = half + heads + feed
    vec_row = qkv_row + half
    pairs = []
    for source, side in ((own, core), (twin, 1 - core)):
        rows = pl.ds(pl.multiple_of(half * side, half), half)
        pairs.append((source.at[:half, :], w_in.at[rows, :]))
        pairs.append((source.at[qkv_row:vec_row, : 3 * heads], qkv.at[rows, :]))
        spare = pl.ds(pl.multiple_of(VEC * side, VEC), VEC)
        pairs.append((source.at[vec_row:, :half], low.at[spare, :]))
    holds = core == line // (LINES // 2)

    @pl.when(holds)
    def _():
        rest = [
            (own.at[half : half + heads, :], w_out),
            (own.at[half + heads : qkv_row, :], w_down),
        ]
        run_copies(pairs + rest, sems)

    @pl.when(jnp.logical_not(holds))
    def _():
        rest = [
            (twin.at[half : half + heads, :], w_out),
            (twin.at[half + heads : qkv_row, :], w_down),
        ]
        run_copies(pairs + rest, sems)

    vectors[...] = low[...].astype(F32)


def full_row(vectors, index):
    return jnp.concatenate(
        [vectors[index : index + 1, :], vectors[VEC + index : VEC + index + 1, :]], 1
    )


def pack_kernel(order, tokens, packed):
    rows = tokens.shape[0]
    packed[:rows, :] = tokens[...]
    lane = lax.broadcasted_iota(jnp.int32, (VEC, 128), 1)
    numbers = jnp.where(lane == 0, order[0], jnp.where(lane == 1, order[1], 0))
    packed[rows:, :128] = numbers.astype(F32).astype(BF16)
    packed[rows:, 128:] = jnp.zeros((VEC, tokens.shape[1] - 128), BF16)


def hold_kernel(x, y):
    y[...] = x[...]


def reorder(chunks, place):
    upper, lower = chunks
    turned = (place & 2) != 0
    near_by = (place & 1) != 0
    first = jnp.where(turned, lower, upper)
    second = jnp.where(turned, upper, lower)
    first = jnp.where(near_by, pltpu.roll(first, 64, 1), first)
    second = jnp.where(near_by, pltpu.roll(second, 64, 1), second)
    return first, second


def left_lanes(rows):
    return lax.broadcasted_iota(jnp.int32, (rows, 128), 1) < 64


def pair_heads(one, two, slot):
    keep = left_lanes(one.shape[0])
    if slot % 2 == 0:
        return jnp.where(keep, one, pltpu.roll(two, 64, 1))
    return jnp.where(keep, pltpu.roll(one, 64, 1), two)


def fold_rows(chunk, slot):
    rows = chunk.shape[0] // 2
    return pair_heads(chunk[:rows], chunk[rows:], slot)


def unfold_pair(even, odd):
    keep = left_lanes(even.shape[0])
    top = jnp.where(keep, even, pltpu.roll(odd, 64, 1))
    bottom = jnp.where(keep, pltpu.roll(even, 64, 1), odd)
    return jnp.concatenate([top, bottom], 0)


def normalise(rows):
    x = rows.astype(F32)
    centred = x - jnp.mean(x, -1, keepdims=True)
    inverse = lax.rsqrt(jnp.mean(centred * centred, -1, keepdims=True) + epsilon)
    return centred * inverse, inverse


def two_chunks(x):
    return x[:, :128], x[:, 128:256]


def two_chunks(x):
    return x[:, :128], x[:, 128:256]


def project_kernel(t0, t1, t2, t3, vectors, qkv, s0, s1, s2, s3, ln_ref, lnt_ref, normed_ref):
    line, place, _ = spot()
    rows = t0.shape[0] - VEC
    gain, shift = full_row(vectors, 0), full_row(vectors, 1)
    numbers = jnp.zeros((VEC, 128), F32)
    for k, ref in enumerate((t0, t1, t2, t3)):
        source = line ^ k
        part = pl.ds(pl.multiple_of(rows * source, rows), rows)
        normed, _ = normalise(ref[:rows, :])
        normed_ref[part, :] = normed
        ln_ref[part, :] = (normed * gain + shift).astype(BF16)
        numbers = numbers + pltpu.roll(ref[rows:, :128].astype(F32), 2 * source, 1)
    side = VEC * (line // (LINES // 2))
    lanes = pl.ds(pl.multiple_of(256 * (line % (LINES // 2)), 256), 256)
    bias_q = vectors[pl.ds(side + 4, 1), lanes]
    bias_v = vectors[pl.ds(side + 5, 1), lanes]
    q_chunks = reorder(two_chunks(dot(ln_ref[...], qkv[:, :256]) + bias_q), place)
    k_chunks = reorder(two_chunks(dot(ln_ref[...], qkv[:, 256:512])), place)
    v_chunks = reorder(two_chunks(dot(ln_ref[...], qkv[:, 512:]) + bias_v), place)
    total = ln_ref.shape[0]
    end = total * 3 // 2
    for slot, ref in enumerate((s0, s1, s2, s3)):
        pair = slot // 2
        ref[:total, :] = pair_heads(q_chunks[pair], k_chunks[pair], slot).astype(BF16)
        ref[total:end, :] = fold_rows(v_chunks[pair], slot).astype(BF16)
        ref[end:, :] = numbers.astype(BF16)
    lnt_ref[...] = ln_ref[...].T


def back_rows_kernel(c0, c1, c2, c3, w_out, att, s0, s1, s2, s3, cot):
    line, place, _ = spot()
    rows = c0.shape[0]
    for k, ref in enumerate((c0, c1, c2, c3)):
        cot[pl.ds(pl.multiple_of(rows * (line ^ k), rows), rows), :] = ref[...]
    chunks = reorder(two_chunks(dot_nt(cot[...], w_out[...])), place)
    fold = att.shape[0] // 4
    for slot, ref in enumerate((s0, s1, s2, s3)):
        ref[:fold, :] = att[fold * slot : fold * (slot + 1), :]
        ref[fold:, :] = fold_rows(chunks[slot // 2], slot).astype(BF16)


def block_rows(table):
    for j in range(4):
        for i in range(8):
            yield j, i, pl.ds(pl.multiple_of(table[8 * j, i] * 64, 64), 64)


def sort_rows(table, slots, target, base, folded):
    for j, i, dest in block_rows(table):
        if folded:
            start = base + 64 * (i % 4)
            lanes = slice(0, 64) if i < 4 else slice(64, 128)
            target[dest, :] = slots[j][start : start + 64, lanes]
        else:
            target[dest, :] = slots[j][base + 64 * i : base + 64 * (i + 1), :]


def turn(x, cosine, sine):
    lane = lax.broadcasted_iota(jnp.int32, x.shape, 1) & (HEAD_DIM - 1)
    other = jnp.where(lane < ROT // 2, pltpu.roll(x, 120, 1), pltpu.roll(x, 8, 1))
    return x * cosine + other * sine


TILE = 256


def scores_of(qk_ref, i):
    rows = slice(TILE * i, TILE * (i + 1))
    queries = jnp.where(left_lanes(TILE), qk_ref[rows, :], jnp.zeros((), BF16))
    queries = queries * jnp.asarray(HEAD_DIM ** (-0.5), BF16)
    return queries


def allowed_tile():
    row = lax.broadcasted_iota(jnp.int32, (TILE, TILE), 0)
    col = lax.broadcasted_iota(jnp.int32, (TILE, TILE), 1)
    return row >= col


def attend_kernel(r0, r1, r2, r3, cosine, sine, *rest):
    att_slots, qk_ref, kq_ref, v_ref, att_ref, lse_ref, table_ref, raw, table, sem = rest
    refs = (r0, r1, r2, r3)
    count = qk_ref.shape[0]
    lines = count // 4
    for j, ref in enumerate(refs):
        numbers = ref[lines * 3 // 2 :, :].astype(F32)[:8, :]
        table_ref[8 * j : 8 * (j + 1), :] = numbers.astype(jnp.int32)
    run_copies([(table_ref, table)], sem)
    sort_rows(table, refs, raw, 0, False)
    sort_rows(table, refs, v_ref, lines, True)
    for i in range(count // TILE):
        rows = slice(TILE * i, TILE * (i + 1))
        turned = turn(raw[rows, :].astype(F32), cosine[rows, :], sine[rows, :])
        qk_ref[rows, :] = turned.astype(BF16)
        kq_ref[rows, :] = pltpu.roll(turned, 64, 1).astype(BF16)
    mask = allowed_tile()
    for i in range(count // TILE):
        rows = slice(TILE * i, TILE * (i + 1))
        keys = TILE * (i + 1)
        scores = dot_nt(scores_of(qk_ref, i), kq_ref[:keys, :])
        last = jnp.where(mask, scores[:, keys - TILE :], -1e30)
        scores = last if i == 0 else jnp.concatenate([scores[:, : keys - TILE], last], 1)
        top = jnp.max(scores, -1, keepdims=True)
        weights = jnp.exp(scores - top)
        total = jnp.sum(weights, -1, keepdims=True)
        weighted = dot(weights.astype(BF16), v_ref[:keys, :])
        att_ref[rows, :] = weighted / total
        lse_ref[rows, :] = top + jnp.log(total)
    for j, i, source in block_rows(table):
        start = lines // 2 * j + 64 * (i % 4)
        lanes = slice(0, 64) if i < 4 else slice(64, 128)
        att_slots[start : start + 64, lanes] = att_ref[source, :].astype(BF16)


def attend_back_kernel(r0, r1, r2, r3, table_ref, qk_ref, kq_ref, v_ref, att_ref, *rest):
    lse_ref, cosine, sine, o0, o1, o2, o3, sums, ga_ref, kt_ref, vt_ref, gqk, gv = rest[:13]
    table, sem = rest[13:]
    refs = (r0, r1, r2, r3)
    count = qk_ref.shape[0]
    lines = count // 4
    run_copies([(table_ref, table)], sem)
    sort_rows(table, refs, ga_ref, lines // 2, True)
    mask = allowed_tile()
    kt_ref[...] = jnp.zeros_like(kt_ref)
    vt_ref[...] = jnp.zeros_like(vt_ref)
    for i in range(count // TILE):
        rows = slice(TILE * i, TILE * (i + 1))
        keys = TILE * (i + 1)
        queries = scores_of(qk_ref, i)
        scores = dot_nt(queries, kq_ref[:keys, :])
        last = jnp.where(mask, scores[:, keys - TILE :], -1e30)
        scores = last if i == 0 else jnp.concatenate([scores[:, : keys - TILE], last], 1)
        probs = jnp.exp(scores - lse_ref[rows, :])
        grad_rows = ga_ref[rows, :]
        delta = jnp.sum(grad_rows.astype(F32) * att_ref[rows, :], -1, keepdims=True)
        grad_probs = dot_nt(grad_rows, v_ref[:keys, :])
        grad_scores = (probs * (grad_probs - delta)).astype(BF16)
        gqk[rows, :] = dot(grad_scores, kq_ref[:keys, :]) * HEAD_DIM ** (-0.5)
        vt_ref[:, :keys] += dot(grad_rows.astype(F32).T.astype(BF16), probs.astype(BF16))
        kt_ref[:, :keys] += dot(queries.astype(F32).T.astype(BF16), grad_scores)
    sum_q = jnp.zeros((1, 128), F32)
    sum_v = jnp.zeros((1, 64), F32)
    for i in range(count // TILE):
        rows = slice(TILE * i, TILE * (i + 1))
        grad_keys = pltpu.roll(kt_ref[:, rows].T, 64, 1)
        both = jnp.where(left_lanes(TILE), gqk[rows, :], grad_keys)
        both = turn(both, cosine[rows, :], -sine[rows, :])
        both = both.astype(BF16).astype(F32)
        values = vt_ref[:, rows].T.astype(BF16).astype(F32)
        gqk[rows, :] = both
        gv[rows, :] = values
        sum_q = sum_q + jnp.sum(both, 0, keepdims=True)
        sum_v = sum_v + jnp.sum(values, 0, keepdims=True)
    sums[...] = jnp.zeros_like(sums)
    sums[0:1, :64] = sum_q[:, :64]
    sums[1:2, :64] = sum_v
    outs = (o0, o1, o2, o3)
    for j, i, source in block_rows(table):
        lanes = slice(0, 64) if i < 4 else slice(64, 128)
        outs[j][64 * i : 64 * (i + 1), :] = gqk[source, :].astype(BF16)
        start = lines + 64 * (i % 4)
        outs[j][start : start + 64, lanes] = gv[source, :].astype(BF16)


def feed_kernel(ln, w_in, vectors, w_down, hidden_ref, actt_ref, low_ref, act_ref):
    line, _, _ = spot()
    row = VEC * (line // (LINES // 2)) + 6 + 2 * (line % (LINES // 2))
    bias = jnp.concatenate([vectors[pl.ds(row, 1), :], vectors[pl.ds(row + 1, 1), :]], 1)
    for f in range(4):
        cols = slice(256 * f, 256 * (f + 1))
        hidden = dot(ln[...], w_in[:, cols]) + bias[:, cols]
        hidden_ref[:, cols] = hidden
        active = 0.5 * hidden * (1.0 + lax.erf(hidden * 0.7071067811865476))
        act_ref[:, cols] = active.astype(BF16)
        actt_ref[cols, :] = active.astype(BF16).T
    for f in range(4):
        cols = slice(256 * f, 256 * (f + 1))
        low_ref[:, cols] = dot(act_ref[...], w_down[:, cols])


def feed_back_kernel(cot_ref, hidden, actt, lnt, w_in, w_down, *rest):
    send, keep, low_ref, gh_ref, chunk_ref = rest
    line, _, core = spot()
    cot = cot_ref[...]
    block = send.shape[0] // 4
    sums = jnp.zeros((1, 1024), F32)
    cot_sum = jnp.sum(cot.astype(F32), 0, keepdims=True)
    bias_sums = []
    for f in range(4):
        cols = slice(256 * f, 256 * (f + 1))
        grad_active = dot_nt(cot, w_down[cols, :])
        h = hidden[:, cols]
        slope = 0.5 * (1.0 + lax.erf(h * 0.7071067811865476)) + h * jnp.exp(
            -0.5 * h * h
        ) * 0.3989422804014327
        grad_hidden = (slope * grad_active).astype(BF16)
        gh_ref[:, cols] = grad_hidden
        bias_sums.append(jnp.sum(grad_hidden.astype(F32), 0, keepdims=True))
    for f in range(4):
        chunk_ref[...] = dot(actt[256 * f : 256 * (f + 1), :], cot)
        base = block * f
        send[base : base + 128, :] = chunk_ref[
            pl.ds(pl.multiple_of((1 - core) * 128, 128), 128), :
        ].astype(BF16)
        keep[base : base + 128, :] = chunk_ref[pl.ds(pl.multiple_of(core * 128, 128), 128), :]
    for z in range(4):
        chunk_ref[...] = dot(lnt[256 * z : 256 * (z + 1), :], gh_ref[...])
        for f in range(4):
            base = block * f + 128 + 32 * z
            send[base : base + 32, :] = chunk_ref[
                pl.ds(pl.multiple_of(64 * f + 32 * (1 - core), 32), 32), :
            ].astype(BF16)
            keep[base : base + 32, :] = chunk_ref[
                pl.ds(pl.multiple_of(64 * f + 32 * core, 32), 32), :
            ]
    picked = jnp.where(
        line < 2,
        jnp.where(line == 0, cot_sum[:, 0:256], cot_sum[:, 256:512]),
        jnp.where(line == 2, cot_sum[:, 512:768], cot_sum[:, 768:1024]),
    )
    zero = jnp.zeros((1, 640), F32)
    for f in range(4):
        even, odd = bias_sums[f][:, :128], bias_sums[f][:, 128:]
        first = core == 0
        base = block * f + 256
        given = jnp.concatenate([jnp.where(first, odd, even), picked, zero], 1)
        kept = jnp.concatenate([jnp.where(first, even, odd), picked, zero], 1)
        send[base : base + VEC, :] = jnp.broadcast_to(given, (VEC, 1024)).astype(BF16)
        keep[base : base + VEC, :] = jnp.broadcast_to(kept, (VEC, 1024))
    for i in range(4):
        low_ref[:, 256 * i : 256 * (i + 1)] = dot_nt(gh_ref[...], w_in[256 * i : 256 * (i + 1), :])


def share_twin_kernel(keep, received, o0, o1, o2, o3):
    _, place, _ = spot()
    block = o0.shape[0]
    for slot, ref in enumerate((o0, o1, o2, o3)):
        rows = pl.ds(pl.multiple_of((place ^ slot) * block, 16), block)
        ref[...] = (keep[rows, :] + received[rows, :].astype(F32)).astype(ref.dtype)


def adder(own, r1, r2, r3):
    def total(rows, cols=slice(None)):
        return (own[rows, cols].astype(F32) + r1[rows, cols].astype(F32)) + (
            r2[rows, cols].astype(F32) + r3[rows, cols].astype(F32)
        )

    return total


def owned_lanes(rows):
    _, place, core = spot()
    return pltpu.roll(rows, lax.rem(256 - (64 * place + 32 * core), 256), 1)[:, :32]


def feed_sum_kernel(own, r1, r2, r3, down_ref, bias_in, bias_out, i0, i1, i2, i3):
    line, _, _ = spot()
    total = adder(own, r1, r2, r3)
    down_ref[...] = total(slice(0, 128))
    bias_in[...] = total(slice(256, 264), slice(0, 128))[:1]
    bias_out[...] = owned_lanes(total(slice(256, 264), slice(128, 384)))[:1]
    for slot, ref in enumerate((i0, i1, i2, i3)):
        rows = pl.ds(pl.multiple_of(128 + 32 * (line ^ slot), 32), 32)
        ref[...] = total(rows).astype(ref.dtype)


def branch_kernel(r0, r1, r2, r3, low, w_out, keep, send, att_t, low_ref):
    line, place, _ = spot()
    fold = r0.shape[0] // 2
    parts = [ref[:fold, :].astype(F32) for ref in (r0, r1, r2, r3)]
    chunks = reorder((unfold_pair(parts[0], parts[1]), unfold_pair(parts[2], parts[3])), place)
    attended = jnp.concatenate(chunks, 1).astype(BF16)
    att_t[...] = attended.T
    low_ref[...] = low[...] + dot(attended, w_out[...])
    rows = low_ref.shape[0] // 4
    for k, (ref, base) in enumerate(((keep, 0), (send, 0), (keep, rows), (send, rows))):
        part = pl.ds(pl.multiple_of(rows * (line ^ k), rows), rows)
        ref[base : base + rows, :] = low_ref[part, :].astype(ref.dtype)


def halve_kernel(keep, received, own, send):
    rows = own.shape[0]
    own[...] = keep[:rows, :] + received[:rows, :].astype(F32)
    send[...] = (keep[rows:, :] + received[rows:, :].astype(F32)).astype(BF16)


def grads_kernel(r0, r1, r2, r3, low, normed, lnt, qkv, att_t, cot, head_sums, *rest):
    s0, s1, s2, s3, send, keep, g_ref, low_ref, chunk_ref, out_ref = rest
    line, place, core = spot()
    rows = s0.shape[0]
    total = 4 * rows
    parts = [ref[...].astype(F32) for ref in (r0, r1, r2, r3)]
    keep_left = left_lanes(total)
    queries, keys, values = [], [], []
    for pair in range(2):
        even, odd = parts[2 * pair][:total], parts[2 * pair + 1][:total]
        queries.append(jnp.where(keep_left, even, pltpu.roll(odd, 64, 1)))
        keys.append(jnp.where(keep_left, pltpu.roll(even, 64, 1), odd))
        values.append(unfold_pair(parts[2 * pair][total:], parts[2 * pair + 1][total:]))
    for index, chunks in enumerate((queries, keys, values)):
        for pair, chunk in enumerate(reorder(chunks, place)):
            base = 256 * index + 128 * pair
            g_ref[:, base : base + 128] = chunk.astype(BF16)
    for i in range(4):
        cols = slice(256 * i, 256 * (i + 1))
        low_ref[:, cols] = low[:, cols] + dot_nt(g_ref[...], qkv[cols, :])
    sum_gain = jnp.zeros((1, 1024), F32)
    sum_bias = jnp.zeros((1, 1024), F32)
    for k, out in enumerate((s0, s1, s2, s3)):
        part = pl.ds(pl.multiple_of(rows * (line ^ k), rows), rows)
        grad = low_ref[part, :]
        out[...] = grad.astype(out.dtype)
        sum_gain = sum_gain + jnp.sum(grad * normed[part, :], 0, keepdims=True)
        sum_bias = sum_bias + jnp.sum(grad, 0, keepdims=True)
    block = send.shape[0] // 4
    for z in range(4):
        chunk_ref[...] = dot(lnt[256 * z : 256 * (z + 1), :], g_ref[...])
        for f in range(4):
            base = block * f + 32 * z
            send[base : base + 32, :] = chunk_ref[
                pl.ds(pl.multiple_of(64 * f + 32 * (1 - core), 32), 32), :
            ].astype(BF16)
            keep[base : base + 32, :] = chunk_ref[
                pl.ds(pl.multiple_of(64 * f + 32 * core, 32), 32), :
            ]
    out_ref[...] = dot(att_t[...], cot[...])
    sums = [sum_gain[:, 256 * i : 256 * (i + 1)] for i in range(4)]
    sums += [sum_bias[:, 256 * i : 256 * (i + 1)] for i in range(4)]
    spare = jnp.concatenate([head_sums[...], jnp.zeros((8, 128), F32)], 1)
    for f in range(4):
        base = block * f + 128
        vec = jnp.concatenate(sums + [jnp.where(place == f, spare, 0.0)], 0)
        for ref, side in ((send, 1 - core), (keep, core)):
            rows = out_ref[pl.ds(pl.multiple_of(64 * f + 32 * side, 32), 32), :]
            tail = jnp.concatenate([rows[:16, 768:], rows[16:, 768:], vec], 1)
            ref[base : base + 32, :] = rows[:, :768].astype(ref.dtype)
            ref[base + 32 : base + 48, :] = tail.astype(ref.dtype)


def grad_sum_kernel(own, r1, r2, r3, grad_out, qv, i0, i1, i2, i3):
    line, _, core = spot()
    total = adder(own, r1, r2, r3)
    tail = total(slice(160, 176))
    grad_out[:, :768] = total(slice(128, 160))
    grad_out[:16, 768:] = tail[:, :256]
    grad_out[16:, 768:] = tail[:, 256:512]
    qv[...] = jnp.where(core == 0, tail[8:10, 512:544], tail[8:10, 544:576])
    for slot, ref in enumerate((i0, i1, i2, i3)):
        rows = pl.ds(pl.multiple_of(32 * (line ^ slot), 32), 32)
        ref[:32, :] = total(rows).astype(ref.dtype)
        ref[32:, :] = tail.astype(ref.dtype)


def join_in_kernel(i0, i1, i2, i3, out):
    line, _, _ = spot()
    for slot, ref in enumerate((i0, i1, i2, i3)):
        cols = pl.ds(pl.multiple_of((line ^ slot) * 1024, 1024), 1024)
        out[:, cols] = ref[...].astype(F32)


def join_qkv_kernel(i0, i1, i2, i3, out, gain, bias, vec_ref):
    line, _, _ = spot()
    vec = jnp.zeros((VEC, 256), F32)
    for slot, ref in enumerate((i0, i1, i2, i3)):
        for part in range(3):
            cols = pl.ds(pl.multiple_of(1024 * part + (line ^ slot) * 256, 256), 256)
            out[:, cols] = ref[:32, 256 * part : 256 * (part + 1)].astype(F32)
        vec = vec + ref[32:, 512:768].astype(F32)
    vec_ref[...] = owned_lanes(vec)
    gain[...] = vec_ref[pl.ds(line, 1), :]
    bias[...] = vec_ref[pl.ds(4 + line, 1), :]


def layer_kernel(own, received, tokens, vectors, out):
    total = own[...] + received[...].astype(F32) + tokens[: own.shape[0], :].astype(F32)
    out[...] = (total + full_row(vectors, 2) + full_row(vectors, 3)).astype(BF16)


def tokens_kernel(own, r1, r2, r3, tokens, cot, vectors, out):
    grad_ln = own[...] + r1[...].astype(F32) + r2[...].astype(F32) + r3[...].astype(F32)
    line, _, _ = spot()
    rows = own.shape[0]
    normed, inverse = normalise(tokens[:rows, :])
    g = grad_ln * full_row(vectors, 0)
    grad = inverse * (
        g - jnp.mean(g, -1, keepdims=True) - normed * jnp.mean(g * normed, -1, keepdims=True)
    )
    mine = cot[pl.ds(pl.multiple_of(rows * line, rows), rows), :]
    out[...] = (mine.astype(F32) + grad).astype(BF16)


def turn_tables(count):
    half_rot = ROT // 2
    inverse = 10000.0 ** (-2.0 * np.arange(half_rot) / ROT)
    angles = np.arange(count)[:, None] * inverse[None, :]
    cosine = np.ones((count, HEAD_DIM), np.float32)
    sine = np.zeros((count, HEAD_DIM), np.float32)
    cosine[:, :half_rot] = cosine[:, half_rot:ROT] = np.cos(angles)
    sine[:, :half_rot] = -np.sin(angles)
    sine[:, half_rot:ROT] = np.sin(angles)
    return tuple(np.concatenate([t, t], -1) for t in (cosine, sine))


def head_body(
    tokens,
    block_order,
    ln_gain,
    ln_bias,
    w_qkv,
    qv_bias,
    w_out,
    b_out,
    w_in,
    b_in,
    w_down,
    b_down,
    cotangent,
):
    positions = range(LINES * ACROSS)

    def over_lines(x, k):
        return lax.ppermute(x, "ctx", [(i, i ^ (k * ACROSS)) for i in positions])

    def over_places(x, j):
        return lax.ppermute(x, "ctx", [(i, i ^ j) for i in positions])

    def twin(x):
        return near(lax.ppermute(raw(x), "fsdp", [(0, 1), (1, 0)]))

    def with_lines(blocks):
        return [blocks[0]] + [near(over_lines(raw(blocks[k]), k)) for k in range(1, LINES)]

    def with_places(blocks):
        return [blocks[0]] + [near(over_places(raw(blocks[j]), j)) for j in range(1, ACROSS)]

    rows, width = tokens.shape[1], tokens.shape[2]
    half = w_qkv.shape[0]
    feed = w_in.shape[1]
    head_cols = width // LINES
    feed_cols = feed // LINES
    qkv_cols = 3 * head_cols
    length = rows * LINES * ACROSS
    line_rows = rows * LINES
    slot_rows = line_rows * 3 // 2
    rotation = turn_tables(length)
    packed_rows = half + head_cols + feed_cols + half + VEC
    table = pltpu.SMEM((32, 128), jnp.int32)
    one_copy = pltpu.SemaphoreType.DMA((1,))
    block = 128 + 128 + VEC
    qkv_block = 128 + 32 + VEC

    last = []

    def run(kernel, out_shapes, scratch, *operands, after=(), loose_in=0):
        results = call(
            kernel, out_shapes, scratch, *operands, after=(*after, *last), loose_in=loose_in
        )
        last[:] = results[:1]
        return results

    (packed,) = run(
        prepare_kernel,
        [near((packed_rows, width), BF16)],
        [pltpu.SemaphoreType.DMA((6,))],
        far(w_qkv), far(w_in), far(w_out), far(w_down),
        *map(far, (ln_gain, ln_bias, b_out, b_down, qv_bias, b_in)),
        loose_in=4,
    )
    (token_block,) = run(
        pack_kernel,
        [near((rows + VEC, width), BF16)],
        [],
        block_order.reshape(2), far(tokens[0]),
    )
    token_lines = with_lines([token_block] * LINES)
    qkv, in_rows, out_rows, down_rows, vectors = run(
        assemble_kernel,
        [
            near((width, qkv_cols), BF16),
            near((width, feed_cols), BF16),
            near((head_cols, width), BF16),
            near((feed_cols, width), BF16),
            near((2 * VEC, half), F32),
        ],
        [pltpu.VMEM((2 * VEC, half), BF16), pltpu.SemaphoreType.DMA((8,))],
        packed, twin(packed),
        loose_in=2,
    )
    first_cot = near(over_lines(cotangent[0], 1))
    (held,) = run(
        hold_kernel,
        [((rows, width), BF16)],
        [],
        cotangent[0],
        after=token_lines[1:] + [first_cot],
    )
    cot_lines = [cotangent[0], first_cot] + [near(over_lines(held, k)) for k in (2, 3)]
    *slots, ln_low, ln_turned, normed = run(
        project_kernel,
        [near((slot_rows + VEC, 128), BF16)]
        + [near((slot_rows + VEC, 128), BF16)] * 3
        + [
            near((line_rows, width), BF16),
            near((width, line_rows), BF16),
            near((line_rows, width), F32),
        ],
        [],
        *token_lines, vectors, qkv,
    )
    slots_in = with_places(slots)
    hidden, active_turned, feed_low = run(
        feed_kernel,
        [
            near((line_rows, feed_cols), F32),
            near((feed_cols, line_rows), BF16),
            near((line_rows, width), F32),
        ],
        [pltpu.VMEM((line_rows, feed_cols), BF16)],
        ln_low, in_rows, vectors, down_rows,
    )
    att_slots, qk_rows, kq_rows, value_rows, attended, lse, numbers = run(
        attend_kernel,
        [
            near((line_rows * 2, 128), BF16),
            near((length, 128), BF16),
            near((length, 128), BF16),
            near((length, 64), BF16),
            near((length, 64), F32),
            near((length, 1), F32),
            near((32, 128), jnp.int32),
        ],
        [pltpu.VMEM((length, 128), BF16), table, one_copy],
        *slots_in, *rotation,
    )
    *mixed, cot_rows = run(
        back_rows_kernel,
        [near((line_rows, 128), BF16)]
        + [near((line_rows, 128), BF16)] * 3
        + [near((line_rows, width), BF16)],
        [],
        *cot_lines, out_rows, att_slots,
    )
    mixed_in = with_places(mixed)
    feed_send, feed_keep, feed_grad_low = run(
        feed_back_kernel,
        [
            near((4 * block, width), BF16),
            near((4 * block, width), F32),
            near((line_rows, width), F32),
        ],
        [pltpu.VMEM((line_rows, feed_cols), BF16), pltpu.VMEM((256, 1024), F32)],
        cot_rows, hidden, active_turned, ln_turned, in_rows, down_rows,
    )
    feed_twin = twin(feed_send)
    low_keep, low_send, att_turned = run(
        branch_kernel,
        [
            near((2 * rows, width), F32),
            near((2 * rows, width), BF16),
            near((head_cols, line_rows), BF16),
        ],
        [pltpu.VMEM((line_rows, width), F32)],
        *mixed_in, feed_low, out_rows,
    )
    low_received = near(over_lines(raw(low_send), 1))
    *grad_slots, bias_sums = run(
        attend_back_kernel,
        [near((slot_rows, 128), BF16)] + [near((slot_rows, 128), BF16)] * 3 + [near((8, 128), F32)],
        [
            pltpu.VMEM((length, 64), BF16),
            pltpu.VMEM((128, length), F32),
            pltpu.VMEM((64, length), F32),
            pltpu.VMEM((length, 128), F32),
            pltpu.VMEM((length, 64), F32),
            table,
            one_copy,
        ],
        *mixed_in, numbers, qk_rows, kq_rows, value_rows, attended, lse, *rotation,
    )
    grad_slots_in = with_places(grad_slots)
    low_own, low_half = run(
        halve_kernel,
        [near((rows, width), F32), near((rows, width), BF16)],
        [],
        low_keep, low_received,
    )
    low_rest = near(over_lines(raw(low_half), 2))
    feed_blocks = run(
        share_twin_kernel,
        [near((block, width), F32)] + [near((block, width), BF16)] * 3,
        [],
        feed_keep, feed_twin,
    )
    feed_in = with_places(feed_blocks)
    *ln_slots, qkv_send, qkv_keep = run(
        grads_kernel,
        [near((rows, width), F32)]
        + [near((rows, width), BF16)] * 3
        + [near((4 * qkv_block, qkv_cols), BF16), near((4 * qkv_block, qkv_cols), F32)],
        [
            pltpu.VMEM((line_rows, qkv_cols), BF16),
            pltpu.VMEM((line_rows, width), F32),
            pltpu.VMEM((256, qkv_cols), F32),
            pltpu.VMEM((head_cols, width), F32),
        ],
        *grad_slots_in, feed_grad_low, normed, ln_turned, qkv, att_turned, cot_rows,
        bias_sums,
    )
    ln_in = with_lines(ln_slots)
    (layer_out,) = run(
        layer_kernel,
        [((rows, width), BF16)],
        [],
        low_own, low_rest, token_block, vectors,
    )
    qkv_blocks = run(
        share_twin_kernel,
        [near((qkv_block, qkv_cols), F32)] + [near((qkv_block, qkv_cols), BF16)] * 3,
        [],
        qkv_keep, twin(qkv_send),
    )
    qkv_sums = with_places(qkv_blocks)
    grad_down, grad_b_in, grad_b, *in_slots = run(
        feed_sum_kernel,
        [((128, width), F32), ((1, 128), F32), ((1, 32), F32), near((32, width), F32)]
        + [near((32, width), BF16)] * 3,
        [],
        *feed_in,
    )
    in_parts = with_lines(in_slots)
    grad_out, grad_qv, *qkv_parts = run(
        grad_sum_kernel,
        [((32, width), F32), ((2, 32), F32), near((32 + VEC, qkv_cols), F32)]
        + [near((32 + VEC, qkv_cols), BF16)] * 3,
        [],
        *qkv_sums,
    )
    qkv_parts = with_lines(qkv_parts)
    (grad_tokens,) = run(
        tokens_kernel,
        [((rows, width), BF16)],
        [],
        *ln_in, token_block, cot_rows, vectors,
    )
    (grad_in,) = run(join_in_kernel, [((32, feed), F32)], [], *in_parts)
    grad_qkv, grad_gain, grad_shift = run(
        join_qkv_kernel,
        [((32, 3 * width), F32), ((1, 32), F32), ((1, 32), F32)],
        [pltpu.VMEM((VEC, 32), F32)],
        *qkv_parts,
    )
    return (
        layer_out[None],
        grad_tokens[None],
        grad_gain[0],
        grad_shift[0],
        grad_qkv,
        grad_qv,
        grad_out,
        grad_b[0],
        grad_in,
        grad_b_in[0],
        grad_down,
        grad_b[0],
    )


def solution(mesh):
    one_head_each = mesh.shape["ctx"] == HEADS and mesh.shape["fsdp"] == 2
    return jax.shard_map(
        head_body if one_head_each else body,
        mesh=mesh,
        in_specs=(
            P("fsdp", "ctx", None),
            P("ctx", None),
            P("fsdp"),
            P("fsdp"),
            P("fsdp", None),
            P(None, "fsdp"),
            P("fsdp", None),
            P("fsdp"),
            P("fsdp", None),
            P("fsdp"),
            P("fsdp", None),
            P("fsdp"),
            P("fsdp", "ctx", None),
        ),
        out_specs=(
            P("fsdp", "ctx", None),
            P("fsdp", "ctx", None),
            P(("ctx", "fsdp")),
            P(("ctx", "fsdp")),
            P(("ctx", "fsdp"), None),
            P(None, ("ctx", "fsdp")),
            P(("ctx", "fsdp"), None),
            P(("ctx", "fsdp")),
            P(("ctx", "fsdp"), None),
            P(("ctx", "fsdp")),
            P(("ctx", "fsdp"), None),
            P(("ctx", "fsdp")),
        ),
        check_vma=False,
    )
```

```python
from functools import partial
import math

import jax
import jax.numpy as jnp
import numpy as np
from jax import lax
from jax.experimental import pallas as pl
from jax.experimental.pallas import tpu as pltpu
from jax.sharding import PartitionSpec as P

HEADS = 16
HEAD_DIM = 64
ROT = 16


epsilon = 1e-05


def from_behind(block, axis, distance):
    devices = range(lax.axis_size(axis))
    route = [((i - distance) % len(devices), i) for i in devices]
    return lax.ppermute(block, axis, route)


def rotate(vectors, cosine, sine_part):
    half_rot = ROT // 2
    rotary_part = vectors[..., :ROT]
    turned = jnp.concatenate([-rotary_part[..., half_rot:], rotary_part[..., :half_rot]], -1)
    return jnp.concatenate([rotary_part * cosine + turned * sine_part, vectors[..., ROT:]], -1)


def tables(positions):
    freq_index = jnp.arange(ROT // 2, dtype=jnp.float32)
    inverse = 10000.0 ** (-2.0 * freq_index / ROT)
    angles = positions.astype(jnp.float32)[:, None] * inverse[None, :]
    angles = jnp.concatenate([angles, angles], -1)
    return (jnp.cos(angles), jnp.sin(angles))


def spread_positions(orders, half_rows):
    offsets = jnp.arange(half_rows, dtype=jnp.int32)
    return (orders[:, :, None] * half_rows + offsets[None, None, :]).reshape(-1)


def outer_sum(left_side, right_side):
    return lax.dot_general(
        left_side, right_side, (((0,), (0,)), ((), ())), preferred_element_type=jnp.float32
    )


def times_transposed(left_side, right_side):
    return lax.dot_general(
        left_side, right_side, (((1,), (1,)), ((), ())), preferred_element_type=jnp.float32
    )


def attend_block(carried, queries, query_pos, key_rows, value_rows, key_pos, score_scale):
    row_max, row_sum, weighted = carried
    scores = (
        jnp.einsum("qhd,khd->hqk", queries, key_rows, preferred_element_type=jnp.float32)
        * score_scale
    )
    allowed = (query_pos[:, None] >= key_pos[None, :])[None]
    new_max = jnp.maximum(row_max, jnp.max(jnp.where(allowed, scores, -1e30), -1))
    weights = jnp.where(allowed, jnp.exp(scores - new_max[:, :, None]), 0.0)
    rescale = jnp.exp(row_max - new_max)
    row_sum = row_sum * rescale + jnp.sum(weights, -1)
    weighted = weighted * rescale.T[:, :, None] + jnp.einsum(
        "hqk,khd->qhd", weights.astype(jnp.bfloat16), value_rows, preferred_element_type=jnp.float32
    )
    return (new_max, row_sum, weighted)


def block_grads(
    queries, grad_rows, log_sum, delta_rows, query_pos, key_rows, value_rows, key_pos, score_scale
):
    scores = (
        jnp.einsum("qhd,khd->hqk", queries, key_rows, preferred_element_type=jnp.float32)
        * score_scale
    )
    allowed = (query_pos[:, None] >= key_pos[None, :])[None]
    probs = jnp.where(allowed, jnp.exp(scores - log_sum[:, :, None]), 0.0)
    grad_values = jnp.einsum(
        "hqk,qhd->khd", probs.astype(jnp.bfloat16), grad_rows, preferred_element_type=jnp.float32
    )
    grad_probs = jnp.einsum(
        "qhd,khd->hqk", grad_rows, value_rows, preferred_element_type=jnp.float32
    )
    grad_scores = (probs * (grad_probs - delta_rows[:, :, None])).astype(jnp.bfloat16)
    grad_queries = (
        jnp.einsum("hqk,khd->qhd", grad_scores, key_rows, preferred_element_type=jnp.float32)
        * score_scale
    )
    grad_keys = (
        jnp.einsum("hqk,qhd->khd", grad_scores, queries, preferred_element_type=jnp.float32)
        * score_scale
    )
    return (grad_queries, grad_keys, grad_values)


def body(
    tokens,
    block_order,
    ln_gain,
    ln_bias,
    w_qkv,
    qv_bias,
    w_out,
    b_out,
    w_in,
    b_in,
    w_down,
    b_down,
    cotangent,
):
    gathered = (
        lax.all_gather(ln_gain, "fsdp", axis=0, tiled=True),
        lax.all_gather(ln_bias, "fsdp", axis=0, tiled=True),
        lax.all_gather(w_qkv, "fsdp", axis=0, tiled=True),
        lax.all_gather(qv_bias, "fsdp", axis=1, tiled=True),
        lax.all_gather(w_out, "fsdp", axis=0, tiled=True),
        lax.all_gather(b_out, "fsdp", axis=0, tiled=True),
        lax.all_gather(w_in, "fsdp", axis=0, tiled=True),
        lax.all_gather(b_in, "fsdp", axis=0, tiled=True),
        lax.all_gather(w_down, "fsdp", axis=0, tiled=True),
        lax.all_gather(b_down, "fsdp", axis=0, tiled=True),
    )
    (
        gain_full,
        shift_full,
        qkv_full,
        bias_full,
        out_full,
        out_bias,
        in_full,
        in_bias,
        down_full,
        down_bias,
    ) = gathered
    tok_rows = tokens.shape[1]
    model_width = tokens.shape[2]
    half_rows = tok_rows // 2
    score_scale = HEAD_DIM ** (-0.5)
    head_shape = (tok_rows, HEADS, HEAD_DIM)
    flat_shape = (tok_rows, model_width)
    inputs = tokens[0].astype(jnp.float32)
    row_mean = jnp.mean(inputs, -1, keepdims=True)
    centered = inputs - row_mean
    inverse = lax.rsqrt(jnp.mean(centered * centered, -1, keepdims=True) + epsilon)
    normed = centered * inverse
    ln_out = (normed * gain_full.astype(jnp.float32) + shift_full.astype(jnp.float32)).astype(
        jnp.bfloat16
    )
    qkv_pre = jnp.dot(ln_out, qkv_full, preferred_element_type=jnp.float32)
    positions = spread_positions(block_order, half_rows)
    cosine, sine_part = tables(positions)
    cosine = cosine[:, None, :]
    sine_part = sine_part[:, None, :]
    query_pre = qkv_pre[:, :model_width] + bias_full[0].astype(jnp.float32)
    query_rows = rotate(query_pre.reshape(head_shape), cosine, sine_part).astype(jnp.bfloat16)
    key_rows = rotate(
        qkv_pre[:, model_width : 2 * model_width].reshape(head_shape), cosine, sine_part
    ).astype(jnp.bfloat16)
    value_rows = (qkv_pre[:, 2 * model_width :] + bias_full[1].astype(jnp.float32)).astype(
        jnp.bfloat16
    )
    key_flat = key_rows.reshape(flat_shape)
    start_state = (
        jnp.full((HEADS, tok_rows), -1e30, jnp.float32),
        jnp.zeros((HEADS, tok_rows), jnp.float32),
        jnp.zeros(head_shape, jnp.float32),
    )
    carried = start_state
    piece_keys = lax.all_gather(key_flat, "ctx", axis=0, tiled=True)
    piece_values = lax.all_gather(value_rows, "ctx", axis=0, tiled=True)
    piece_orders = lax.all_gather(block_order, "ctx", axis=0, tiled=True)
    shard_count = piece_orders.shape[0]
    group_size = math.gcd(shard_count, max(1, 1024 // tok_rows))
    rounds = shard_count // group_size
    stacked = (
        piece_keys.reshape(rounds, group_size * tok_rows, HEADS, HEAD_DIM),
        piece_values.reshape(rounds, group_size * tok_rows, HEADS, HEAD_DIM),
        piece_orders.reshape(rounds, group_size, 2),
    )

    def one_round(inner_state, block_item):
        key_pos = spread_positions(block_item[2], half_rows)
        return (
            attend_block(
                inner_state,
                query_rows,
                positions,
                block_item[0],
                block_item[1],
                key_pos,
                score_scale,
            ),
            None,
        )

    carried, _ = lax.scan(one_round, carried, stacked)
    row_max, row_sum, weighted = carried
    attended_f32 = weighted / row_sum.T[:, :, None]
    log_sum = row_max + jnp.log(row_sum)
    attended = attended_f32.reshape(flat_shape).astype(jnp.bfloat16)
    branch = jnp.dot(attended, out_full, preferred_element_type=jnp.float32) + out_bias.astype(
        jnp.float32
    )
    hidden = jnp.dot(ln_out, in_full, preferred_element_type=jnp.float32) + in_bias.astype(
        jnp.float32
    )
    active = jax.nn.gelu(hidden, approximate=False).astype(jnp.bfloat16)
    feed_out = jnp.dot(active, down_full, preferred_element_type=jnp.float32) + down_bias.astype(
        jnp.float32
    )
    layer_out = (inputs + branch + feed_out).astype(jnp.bfloat16)[None]
    gain_back, qkv_back, out_back, in_back, down_back = (
        gain_full,
        qkv_full,
        out_full,
        in_full,
        down_full,
    )
    grad_out = cotangent[0]
    grad_f32 = grad_out.astype(jnp.float32)
    grad_attended = times_transposed(grad_out, out_back).astype(jnp.bfloat16).reshape(head_shape)
    grad_active = times_transposed(grad_out, down_back)
    _, gelu_pull = jax.vjp(partial(jax.nn.gelu, approximate=False), hidden)
    grad_hidden = gelu_pull(grad_active)[0].astype(jnp.bfloat16)
    delta_rows = jnp.sum(grad_attended.astype(jnp.float32) * attended_f32, -1).T
    cotangent_sum = jnp.sum(grad_f32, 0)
    term_out_w = outer_sum(attended, grad_out)
    term_in_w = outer_sum(ln_out, grad_hidden)
    term_in_b = jnp.sum(grad_hidden.astype(jnp.float32), 0)
    term_down_w = outer_sum(active, grad_out)
    cycle_size = lax.axis_size("ctx")
    zeros_flat = jnp.zeros(flat_shape, jnp.float32)
    zeros_heads = jnp.zeros(head_shape, jnp.float32)

    def send_home(grad_keys, grad_values):
        return (
            from_behind(grad_keys.astype(jnp.bfloat16), "ctx", 1).astype(grad_keys.dtype),
            from_behind(grad_values.astype(jnp.bfloat16), "ctx", 1).astype(grad_values.dtype),
        )

    def visit_keys(carried):
        visit_key, visit_value, visit_order, grad_keys, grad_values, grad_query = carried
        part_query, part_key, part_value = block_grads(
            query_rows,
            grad_attended,
            log_sum,
            delta_rows,
            positions,
            visit_key.reshape(head_shape),
            visit_value.reshape(head_shape),
            spread_positions(visit_order, half_rows),
            score_scale,
        )
        return (
            grad_keys + part_key.reshape(flat_shape),
            grad_values + part_value.reshape(flat_shape),
            grad_query + part_query,
        )

    def cycle_step(step_index, carried):
        grad_keys, grad_values, grad_query = visit_keys(carried)
        visit_key, visit_value, visit_order = from_behind(
            (carried[0], carried[1], carried[2]), "ctx", 1
        )
        grad_keys, grad_values = send_home(grad_keys, grad_values)
        return (visit_key, visit_value, visit_order, grad_keys, grad_values, grad_query)

    carried = lax.fori_loop(
        0,
        cycle_size - 1,
        cycle_step,
        (key_flat, value_rows, block_order, zeros_flat, zeros_flat, zeros_heads),
    )
    grad_keys, grad_values, grad_query = visit_keys(carried)
    grad_keys, grad_values = send_home(grad_keys, grad_values)
    grad_keys = grad_keys.reshape(head_shape)
    grad_values = grad_values.reshape(head_shape)
    grad_q_pre = rotate(grad_query, cosine, -sine_part).reshape(flat_shape).astype(jnp.bfloat16)
    grad_k_pre = rotate(grad_keys, cosine, -sine_part).reshape(flat_shape).astype(jnp.bfloat16)
    grad_v_pre = grad_values.reshape(flat_shape).astype(jnp.bfloat16)
    grad_qkv = jnp.concatenate([grad_q_pre, grad_k_pre, grad_v_pre], -1)
    grad_ln = times_transposed(grad_qkv, qkv_back) + times_transposed(grad_hidden, in_back)
    grad_normed = grad_ln * gain_back.astype(jnp.float32)
    grad_inputs = inverse * (
        grad_normed
        - jnp.mean(grad_normed, -1, keepdims=True)
        - normed * jnp.mean(grad_normed * normed, -1, keepdims=True)
    )
    grad_tokens = (grad_f32 + grad_inputs).astype(jnp.bfloat16)[None]
    term_gain = jnp.sum(grad_ln * normed, 0)
    term_bias = jnp.sum(grad_ln, 0)
    term_qkv = outer_sum(ln_out, grad_qkv)
    term_qv = jnp.stack(
        [jnp.sum(grad_q_pre.astype(jnp.float32), 0), jnp.sum(grad_v_pre.astype(jnp.float32), 0)], 0
    )
    (
        sum_gain,
        sum_bias,
        sum_qkv,
        sum_qv,
        sum_out_w,
        sum_out_b,
        sum_in_w,
        sum_in_b,
        sum_down_w,
        sum_down_b,
    ) = (
        lax.psum_scatter(term_gain, ("ctx", "fsdp"), scatter_dimension=0, tiled=True),
        lax.psum_scatter(term_bias, ("ctx", "fsdp"), scatter_dimension=0, tiled=True),
        lax.psum_scatter(term_qkv, ("ctx", "fsdp"), scatter_dimension=0, tiled=True),
        lax.psum_scatter(term_qv, ("ctx", "fsdp"), scatter_dimension=1, tiled=True),
        lax.psum_scatter(term_out_w, ("ctx", "fsdp"), scatter_dimension=0, tiled=True),
        lax.psum_scatter(cotangent_sum, ("ctx", "fsdp"), scatter_dimension=0, tiled=True),
        lax.psum_scatter(term_in_w, ("ctx", "fsdp"), scatter_dimension=0, tiled=True),
        lax.psum_scatter(term_in_b, ("ctx", "fsdp"), scatter_dimension=0, tiled=True),
        lax.psum_scatter(term_down_w, ("ctx", "fsdp"), scatter_dimension=0, tiled=True),
        lax.psum_scatter(cotangent_sum, ("ctx", "fsdp"), scatter_dimension=0, tiled=True),
    )
    return (
        layer_out,
        grad_tokens,
        sum_gain,
        sum_bias,
        sum_qkv,
        sum_qv,
        sum_out_w,
        sum_out_b,
        sum_in_w,
        sum_in_b,
        sum_down_w,
        sum_down_b,
    )


LINES = 4
ACROSS = HEADS // LINES
F32 = jnp.float32
BF16 = jnp.bfloat16
VMEM_LIMIT = 16 * 1024 * 1024
TIMES = {'wait': 5, 'project': 80, 'feed_grad': 40, 'halve': 400, 'unpack': 20, 'feed_sum': 150, 'prepare': 150, 'back_rows': 80, 'feed_terms': 5, 'share_twin': 400, 'join_in': 5}

VEC = 16


def dot(left, right):
    return jnp.dot(left, right, preferred_element_type=F32)


def dot_nt(left, right):
    return lax.dot_general(left, right, (((1,), (1,)), ((), ())), preferred_element_type=F32)


class Far(tuple):
    pass


class Near(tuple):
    pass


def far(*x):
    return Far(x)


def near(*x):
    return Near(x)


def raw(x):
    return x[0] if isinstance(x, (Far, Near)) else x


def spot():
    context = lax.axis_index("ctx")
    return context // ACROSS, context % ACROSS, lax.axis_index("fsdp")


def call(kernel, out_shapes, scratch, *operands, after=(), loose_in=0):
    whole = pl.BlockSpec(memory_space=pltpu.VMEM)
    loose = pl.BlockSpec(memory_space=pl.ANY)
    arrays, specs = [], []
    for x in operands:
        if isinstance(x, Far):
            arrays.append(pltpu.with_memory_space_constraint(x[0], pltpu.HBM))
        elif isinstance(x, Near):
            arrays.append(pltpu.with_memory_space_constraint(x[0], pltpu.VMEM))
        else:
            arrays.append(x)
        if arrays[-1].dtype == jnp.int32 and arrays[-1].ndim == 1:
            specs.append(pl.BlockSpec(memory_space=pltpu.SMEM))
        else:
            specs.append(loose if len(specs) < loose_in else whole)
    outs = []
    for shape in out_shapes:
        if isinstance(shape, Far):
            outs.append(pltpu.HBM(*shape))
        elif isinstance(shape, Near):
            outs.append(pltpu.VMEM(*shape))
        else:
            outs.append(jax.ShapeDtypeStruct(*shape))
    count = len(arrays)

    def body(*refs):
        kernel(*refs[:count], *refs[count + len(after) :])

    name = kernel.__name__.removesuffix("_kernel")
    results = pl.pallas_call(
        body,
        name=name,
        out_shape=outs,
        in_specs=specs + [loose] * len(after),
        out_specs=[whole for _ in outs],
        scratch_shapes=scratch,
        compiler_params=pltpu.CompilerParams(vmem_limit_bytes=VMEM_LIMIT),
        cost_estimate=pl.CostEstimate(
            flops=TIMES.get(name, 0) * 115_000_000, bytes_accessed=0, transcendentals=0
        ),
    )(*arrays, *map(raw, after))
    return [
        near(x) if isinstance(shape, Near) else x for x, shape in zip(results, out_shapes)
    ]


def run_copies(pairs, sems):
    copies = [pltpu.make_async_copy(x, y, sems.at[i]) for i, (x, y) in enumerate(pairs)]
    for copy in copies:
        copy.start()
    for copy in copies:
        copy.wait()


def prepare_kernel(qkv, w_in, w_out, w_down, gain, shift, b_out, b_down, qv, b_in, packed, sems):
    line, _, _ = spot()
    feed = w_in.shape[1] // LINES
    half, width = w_out.shape
    part = line % (LINES // 2)
    row = 0
    pairs = []
    sources = [
        w_in.at[:, pl.ds(pl.multiple_of(feed * line, 128), feed)],
        w_out,
        w_down.at[pl.ds(pl.multiple_of(feed * part, 16), feed), :],
    ]
    for source in sources + [qkv.at[:, width * i : width * (i + 1)] for i in range(3)]:
        pairs.append((source, packed.at[row : row + source.shape[0], :]))
        row += source.shape[0]
    rows = [x[...].astype(F32).reshape(1, half) for x in (gain, shift, b_out, b_down)]
    rows += [qv[...].astype(F32), b_in[...].astype(F32).reshape(4, half)]
    rows.append(jnp.zeros((VEC - 10, half), F32))
    packed[row : row + VEC, :half] = jnp.concatenate(rows, 0).astype(BF16)
    run_copies(pairs, sems)


def assemble_kernel(own, twin, qkv, w_in, w_out, w_down, vectors, low, sems):
    line, _, core = spot()
    width = w_out.shape[1]
    half = width // 2
    feed = w_down.shape[0]
    down_row = 2 * half
    qkv_row = down_row + feed
    vec_row = qkv_row + 3 * half
    pairs = []
    for source, side in ((own, core), (twin, 1 - core)):
        rows = pl.ds(pl.multiple_of(half * side, half), half)
        pairs.append((source.at[:half, :], w_in.at[rows, :]))
        pairs.append((source.at[half:down_row, :], w_out.at[rows, :]))
        for i in range(3):
            base = qkv_row + half * i
            pairs.append(
                (source.at[base : base + half, :], qkv.at[rows, width * i : width * (i + 1)])
            )
        spare = pl.ds(pl.multiple_of(VEC * side, VEC), VEC)
        pairs.append((source.at[vec_row:, :half], low.at[spare, :]))
    holds = core == line // (LINES // 2)

    @pl.when(holds)
    def _():
        run_copies(pairs + [(own.at[down_row:qkv_row, :], w_down)], sems)

    @pl.when(jnp.logical_not(holds))
    def _():
        run_copies(pairs + [(twin.at[down_row:qkv_row, :], w_down)], sems)

    vectors[...] = low[...].astype(F32)


def line_columns(qkv, part):
    line, _, _ = spot()
    width = qkv.shape[1] // 3
    base = width * part + width // LINES * line
    return qkv[:, pl.ds(pl.multiple_of(base, 128), width // LINES)]


def line_rows_of(w_out):
    line, _, _ = spot()
    count = w_out.shape[0] // LINES
    return w_out[pl.ds(pl.multiple_of(count * line, 16), count), :]


def full_row(vectors, index):
    return jnp.concatenate(
        [vectors[index : index + 1, :], vectors[VEC + index : VEC + index + 1, :]], 1
    )


def pack_kernel(order, tokens, packed):
    rows = tokens.shape[0]
    packed[:rows, :] = tokens[...]
    lane = lax.broadcasted_iota(jnp.int32, (VEC, 128), 1)
    numbers = jnp.where(lane == 0, order[0], jnp.where(lane == 1, order[1], 0))
    packed[rows:, :128] = numbers.astype(F32).astype(BF16)
    packed[rows:, 128:] = jnp.zeros((VEC, tokens.shape[1] - 128), BF16)


def reorder(chunks, place):
    upper, lower = chunks
    turned = (place & 2) != 0
    near_by = (place & 1) != 0
    first = jnp.where(turned, lower, upper)
    second = jnp.where(turned, upper, lower)
    first = jnp.where(near_by, pltpu.roll(first, 64, 1), first)
    second = jnp.where(near_by, pltpu.roll(second, 64, 1), second)
    return first, second


def left_lanes(rows):
    return lax.broadcasted_iota(jnp.int32, (rows, 128), 1) < 64


def pair_heads(one, two, slot):
    keep = left_lanes(one.shape[0])
    if slot % 2 == 0:
        return jnp.where(keep, one, pltpu.roll(two, 64, 1))
    return jnp.where(keep, pltpu.roll(one, 64, 1), two)


def fold_rows(chunk, slot):
    rows = chunk.shape[0] // 2
    return pair_heads(chunk[:rows], chunk[rows:], slot)


def unfold_pair(even, odd):
    keep = left_lanes(even.shape[0])
    top = jnp.where(keep, even, pltpu.roll(odd, 64, 1))
    bottom = jnp.where(keep, pltpu.roll(even, 64, 1), odd)
    return jnp.concatenate([top, bottom], 0)


def normalise(rows):
    x = rows.astype(F32)
    centred = x - jnp.mean(x, -1, keepdims=True)
    inverse = lax.rsqrt(jnp.mean(centred * centred, -1, keepdims=True) + epsilon)
    return centred * inverse, inverse


def two_chunks(x):
    return x[:, :128], x[:, 128:256]


def two_chunks(x):
    return x[:, :128], x[:, 128:256]


def project_kernel(t0, t1, t2, t3, vectors, qkv, s0, s1, s2, s3, ln_ref, lnt_ref, normed_ref):
    line, place, _ = spot()
    rows = t0.shape[0] - VEC
    gain, shift = full_row(vectors, 0), full_row(vectors, 1)
    numbers = jnp.zeros((VEC, 128), F32)
    for k, ref in enumerate((t0, t1, t2, t3)):
        source = line ^ k
        part = pl.ds(pl.multiple_of(rows * source, rows), rows)
        normed, _ = normalise(ref[:rows, :])
        normed_ref[part, :] = normed
        ln_ref[part, :] = (normed * gain + shift).astype(BF16)
        numbers = numbers + pltpu.roll(ref[rows:, :128].astype(F32), 2 * source, 1)
    side = VEC * (line // (LINES // 2))
    lanes = pl.ds(pl.multiple_of(256 * (line % (LINES // 2)), 256), 256)
    bias_q = vectors[pl.ds(side + 4, 1), lanes]
    bias_v = vectors[pl.ds(side + 5, 1), lanes]
    q_chunks = reorder(two_chunks(dot(ln_ref[...], line_columns(qkv, 0)) + bias_q), place)
    k_chunks = reorder(two_chunks(dot(ln_ref[...], line_columns(qkv, 1))), place)
    v_chunks = reorder(two_chunks(dot(ln_ref[...], line_columns(qkv, 2)) + bias_v), place)
    total = ln_ref.shape[0]
    end = total * 3 // 2
    for slot, ref in enumerate((s0, s1, s2, s3)):
        pair = slot // 2
        ref[:total, :] = pair_heads(q_chunks[pair], k_chunks[pair], slot).astype(BF16)
        ref[total:end, :] = fold_rows(v_chunks[pair], slot).astype(BF16)
        ref[end:, :] = numbers.astype(BF16)
    lnt_ref[...] = ln_ref[...].T


def back_rows_kernel(c0, c1, c2, c3, w_out, s0, s1, s2, s3, cot):
    line, place, _ = spot()
    rows = c0.shape[0]
    for k, ref in enumerate((c0, c1, c2, c3)):
        cot[pl.ds(pl.multiple_of(rows * (line ^ k), rows), rows), :] = ref[...]
    chunks = reorder(two_chunks(dot_nt(cot[...], line_rows_of(w_out))), place)
    for slot, ref in enumerate((s0, s1, s2, s3)):
        ref[...] = fold_rows(chunks[slot // 2], slot).astype(BF16)


def block_rows(table):
    for j in range(4):
        for i in range(8):
            yield j, i, pl.ds(pl.multiple_of(table[8 * j, i] * 64, 64), 64)


def sort_rows(table, slots, target, base, folded):
    for j, i, dest in block_rows(table):
        if folded:
            start = base + 64 * (i % 4)
            lanes = slice(0, 64) if i < 4 else slice(64, 128)
            target[dest, :] = slots[j][start : start + 64, lanes]
        else:
            target[dest, :] = slots[j][base + 64 * i : base + 64 * (i + 1), :]


def turn(x, cosine, sine):
    lane = lax.broadcasted_iota(jnp.int32, x.shape, 1) & (HEAD_DIM - 1)
    other = jnp.where(lane < ROT // 2, pltpu.roll(x, 120, 1), pltpu.roll(x, 8, 1))
    return x * cosine + other * sine


TILE = 256


def scores_of(qk_ref, i):
    rows = slice(TILE * i, TILE * (i + 1))
    queries = jnp.where(left_lanes(TILE), qk_ref[rows, :], jnp.zeros((), BF16))
    queries = queries * jnp.asarray(HEAD_DIM ** (-0.5), BF16)
    return queries


def allowed_tile():
    row = lax.broadcasted_iota(jnp.int32, (TILE, TILE), 0)
    col = lax.broadcasted_iota(jnp.int32, (TILE, TILE), 1)
    return row >= col


def attend_kernel(r0, r1, r2, r3, cosine, sine, *rest):
    qk_ref, kq_ref, v_ref, att_ref, lse_ref, table_ref, raw, table, sem = rest
    refs = (r0, r1, r2, r3)
    count = qk_ref.shape[0]
    lines = count // 4
    for j, ref in enumerate(refs):
        numbers = ref[lines * 3 // 2 :, :].astype(F32)[:8, :]
        table_ref[8 * j : 8 * (j + 1), :] = numbers.astype(jnp.int32)
    run_copies([(table_ref, table)], sem)
    sort_rows(table, refs, raw, 0, False)
    sort_rows(table, refs, v_ref, lines, True)
    for i in range(count // TILE):
        rows = slice(TILE * i, TILE * (i + 1))
        turned = turn(raw[rows, :].astype(F32), cosine[rows, :], sine[rows, :])
        qk_ref[rows, :] = turned.astype(BF16)
        kq_ref[rows, :] = pltpu.roll(turned, 64, 1).astype(BF16)
    mask = allowed_tile()
    for i in range(count // TILE):
        rows = slice(TILE * i, TILE * (i + 1))
        keys = TILE * (i + 1)
        scores = dot_nt(scores_of(qk_ref, i), kq_ref[:keys, :])
        last = jnp.where(mask, scores[:, keys - TILE :], -1e30)
        scores = last if i == 0 else jnp.concatenate([scores[:, : keys - TILE], last], 1)
        top = jnp.max(scores, -1, keepdims=True)
        weights = jnp.exp(scores - top)
        total = jnp.sum(weights, -1, keepdims=True)
        weighted = dot(weights.astype(BF16), v_ref[:keys, :])
        att_ref[rows, :] = weighted / total
        lse_ref[rows, :] = top + jnp.log(total)


def attend_back_kernel(r0, r1, r2, r3, table_ref, qk_ref, kq_ref, v_ref, att_ref, *rest):
    lse_ref, cosine, sine, o0, o1, o2, o3, sums, ga_ref, kt_ref, vt_ref, gqk, gv = rest[:13]
    table, sem = rest[13:]
    refs = (r0, r1, r2, r3)
    count = qk_ref.shape[0]
    lines = count // 4
    run_copies([(table_ref, table)], sem)
    sort_rows(table, refs, ga_ref, 0, True)
    mask = allowed_tile()
    kt_ref[...] = jnp.zeros_like(kt_ref)
    vt_ref[...] = jnp.zeros_like(vt_ref)
    for i in range(count // TILE):
        rows = slice(TILE * i, TILE * (i + 1))
        keys = TILE * (i + 1)
        queries = scores_of(qk_ref, i)
        scores = dot_nt(queries, kq_ref[:keys, :])
        last = jnp.where(mask, scores[:, keys - TILE :], -1e30)
        scores = last if i == 0 else jnp.concatenate([scores[:, : keys - TILE], last], 1)
        probs = jnp.exp(scores - lse_ref[rows, :])
        grad_rows = ga_ref[rows, :]
        delta = jnp.sum(grad_rows.astype(F32) * att_ref[rows, :], -1, keepdims=True)
        grad_probs = dot_nt(grad_rows, v_ref[:keys, :])
        grad_scores = (probs * (grad_probs - delta)).astype(BF16)
        gqk[rows, :] = dot(grad_scores, kq_ref[:keys, :]) * HEAD_DIM ** (-0.5)
        vt_ref[:, :keys] += dot(grad_rows.astype(F32).T.astype(BF16), probs.astype(BF16))
        kt_ref[:, :keys] += dot(queries.astype(F32).T.astype(BF16), grad_scores)
    sum_q = jnp.zeros((1, 128), F32)
    sum_v = jnp.zeros((1, 64), F32)
    for i in range(count // TILE):
        rows = slice(TILE * i, TILE * (i + 1))
        grad_keys = pltpu.roll(kt_ref[:, rows].T, 64, 1)
        both = jnp.where(left_lanes(TILE), gqk[rows, :], grad_keys)
        both = turn(both, cosine[rows, :], -sine[rows, :])
        both = both.astype(BF16).astype(F32)
        values = vt_ref[:, rows].T.astype(BF16).astype(F32)
        gqk[rows, :] = both
        gv[rows, :] = values
        sum_q = sum_q + jnp.sum(both, 0, keepdims=True)
        sum_v = sum_v + jnp.sum(values, 0, keepdims=True)
    sums[...] = jnp.zeros_like(sums)
    sums[0:1, :64] = sum_q[:, :64]
    sums[1:2, :64] = sum_v
    outs = (o0, o1, o2, o3)
    for j, i, source in block_rows(table):
        lanes = slice(0, 64) if i < 4 else slice(64, 128)
        outs[j][64 * i : 64 * (i + 1), :] = gqk[source, :].astype(BF16)
        start = lines + 64 * (i % 4)
        outs[j][start : start + 64, lanes] = gv[source, :].astype(BF16)
        start += lines // 2
        outs[j][start : start + 64, lanes] = att_ref[source, :].astype(BF16)


def split_lines(low, keep, send):
    line, _, _ = spot()
    rows = low.shape[0] // LINES
    for k, (ref, base) in enumerate(((keep, 0), (send, 0), (keep, rows), (send, rows))):
        part = pl.ds(pl.multiple_of(rows * (line ^ k), rows), rows)
        ref[base : base + rows, :] = low[part, :].astype(ref.dtype)


def feed_kernel(ln, w_in, vectors, w_down, hidden_ref, actt_ref, keep, send, act_ref, low_ref):
    line, _, _ = spot()
    row = VEC * (line // (LINES // 2)) + 6 + 2 * (line % (LINES // 2))
    bias = jnp.concatenate([vectors[pl.ds(row, 1), :], vectors[pl.ds(row + 1, 1), :]], 1)
    for f in range(4):
        cols = slice(256 * f, 256 * (f + 1))
        hidden = dot(ln[...], w_in[:, cols]) + bias[:, cols]
        hidden_ref[:, cols] = hidden
        active = 0.5 * hidden * (1.0 + lax.erf(hidden * 0.7071067811865476))
        act_ref[:, cols] = active.astype(BF16)
        actt_ref[cols, :] = active.astype(BF16).T
    for f in range(4):
        cols = slice(256 * f, 256 * (f + 1))
        low_ref[:, cols] = dot(act_ref[...], w_down[:, cols])
    split_lines(low_ref, keep, send)


def feed_grad_kernel(cot, hidden, w_in, w_down, gh_ref, sums, low_ref, keep, send):
    for f in range(4):
        cols = slice(256 * f, 256 * (f + 1))
        grad_active = dot_nt(cot[...], w_down[cols, :])
        h = hidden[:, cols]
        slope = 0.5 * (1.0 + lax.erf(h * 0.7071067811865476)) + h * jnp.exp(
            -0.5 * h * h
        ) * 0.3989422804014327
        grad_hidden = (slope * grad_active).astype(BF16)
        gh_ref[:, cols] = grad_hidden
        total = jnp.sum(grad_hidden.astype(F32), 0, keepdims=True)
        sums[:, cols] = jnp.broadcast_to(total, (8, 256))
    for i in range(4):
        low_ref[:, 256 * i : 256 * (i + 1)] = dot_nt(gh_ref[...], w_in[256 * i : 256 * (i + 1), :])
    split_lines(low_ref, keep, send)


def feed_terms_kernel(cot_ref, actt, lnt, gh, sums, send, keep, chunk_ref):
    line, _, core = spot()
    cot = cot_ref[...]
    block = send.shape[0] // 4
    for f in range(4):
        chunk_ref[...] = dot(actt[256 * f : 256 * (f + 1), :], cot)
        base = block * f
        send[base : base + 128, :] = chunk_ref[
            pl.ds(pl.multiple_of((1 - core) * 128, 128), 128), :
        ].astype(BF16)
        keep[base : base + 128, :] = chunk_ref[pl.ds(pl.multiple_of(core * 128, 128), 128), :]
    for z in range(4):
        chunk_ref[...] = dot(lnt[256 * z : 256 * (z + 1), :], gh[...])
        for f in range(4):
            base = block * f + 128 + 32 * z
            send[base : base + 32, :] = chunk_ref[
                pl.ds(pl.multiple_of(64 * f + 32 * (1 - core), 32), 32), :
            ].astype(BF16)
            keep[base : base + 32, :] = chunk_ref[
                pl.ds(pl.multiple_of(64 * f + 32 * core, 32), 32), :
            ]
    cot_sum = jnp.sum(cot.astype(F32), 0, keepdims=True)
    picked = jnp.where(
        line < 2,
        jnp.where(line == 0, cot_sum[:, 0:256], cot_sum[:, 256:512]),
        jnp.where(line == 2, cot_sum[:, 512:768], cot_sum[:, 768:1024]),
    )
    zero = jnp.zeros((1, 640), F32)
    for f in range(4):
        even, odd = sums[:1, 256 * f : 256 * f + 128], sums[:1, 256 * f + 128 : 256 * f + 256]
        first = core == 0
        base = block * f + 256
        given = jnp.concatenate([jnp.where(first, odd, even), picked, zero], 1)
        kept = jnp.concatenate([jnp.where(first, even, odd), picked, zero], 1)
        send[base : base + VEC, :] = jnp.broadcast_to(given, (VEC, 1024)).astype(BF16)
        keep[base : base + VEC, :] = jnp.broadcast_to(kept, (VEC, 1024))


def share_twin_kernel(keep, received, o0, o1, o2, o3):
    _, place, _ = spot()
    block = o0.shape[0]
    for slot, ref in enumerate((o0, o1, o2, o3)):
        rows = pl.ds(pl.multiple_of((place ^ slot) * block, 16), block)
        ref[...] = (keep[rows, :] + received[rows, :].astype(F32)).astype(ref.dtype)


def adder(own, r1, r2, r3):
    def total(rows, cols=slice(None)):
        return (own[rows, cols].astype(F32) + r1[rows, cols].astype(F32)) + (
            r2[rows, cols].astype(F32) + r3[rows, cols].astype(F32)
        )

    return total


def owned_lanes(rows):
    _, place, core = spot()
    return pltpu.roll(rows, lax.rem(256 - (64 * place + 32 * core), 256), 1)[:, :32]


def feed_sum_kernel(own, r1, r2, r3, down_ref, bias_in, bias_out, i0, i1, i2, i3):
    line, _, _ = spot()
    total = adder(own, r1, r2, r3)
    down_ref[...] = total(slice(0, 128))
    bias_in[...] = total(slice(256, 264), slice(0, 128))[:1]
    bias_out[...] = owned_lanes(total(slice(256, 264), slice(128, 384)))[:1]
    for slot, ref in enumerate((i0, i1, i2, i3)):
        rows = pl.ds(pl.multiple_of(128 + 32 * (line ^ slot), 32), 32)
        ref[...] = total(rows).astype(ref.dtype)


def halve_kernel(keep, received, own, send):
    rows = own.shape[0]
    own[...] = keep[:rows, :] + received[:rows, :].astype(F32)
    send[...] = (keep[rows:, :] + received[rows:, :].astype(F32)).astype(BF16)


def unpack_kernel(r0, r1, r2, r3, mixed, att_t, s1, s2, s3):
    line, place, _ = spot()
    rows = s1.shape[0]
    total = LINES * rows
    fold = total // 2
    parts = [ref[...].astype(F32) for ref in (r0, r1, r2, r3)]
    keep_left = left_lanes(total)
    chunks = [[], [], [], []]
    for pair in range(2):
        one, two = parts[2 * pair], parts[2 * pair + 1]
        even, odd = one[:total], two[:total]
        values, attended = slice(total, total + fold), slice(total + fold, total + 2 * fold)
        chunks[0].append(unfold_pair(one[attended], two[attended]))
        chunks[1].append(jnp.where(keep_left, even, pltpu.roll(odd, 64, 1)))
        chunks[2].append(jnp.where(keep_left, pltpu.roll(even, 64, 1), odd))
        chunks[3].append(unfold_pair(one[values], two[values]))
    for index, both in enumerate(chunks):
        for pair, chunk in enumerate(reorder(both, place)):
            base = 256 * index + 128 * pair
            mixed[:, base : base + 128] = chunk.astype(BF16)
    for k, ref in ((1, s1), (2, s2), (3, s3)):
        ref[...] = mixed[pl.ds(pl.multiple_of(rows * (line ^ k), rows), rows), :]
    att_t[...] = mixed[:, :256].T


def grads_kernel(mixed, low, normed, lnt, qkv, att_t, cot, head_sums, *rest):
    send, keep, low_ref, chunk_ref, out_ref = rest
    _, place, core = spot()
    low_ref[...] = low[...]
    for i in range(3):
        cols = slice(256 * (i + 1), 256 * (i + 2))
        low_ref[...] += dot_nt(mixed[:, cols], line_columns(qkv, i))
    grad = low_ref[...]
    sum_gain = jnp.sum(grad * normed[...], 0, keepdims=True)
    sum_bias = jnp.sum(grad, 0, keepdims=True)
    block = send.shape[0] // 4
    for z in range(4):
        chunk_ref[...] = dot(lnt[256 * z : 256 * (z + 1), :], mixed[:, 256:])
        for f in range(4):
            base = block * f + 32 * z
            send[base : base + 32, :] = chunk_ref[
                pl.ds(pl.multiple_of(64 * f + 32 * (1 - core), 32), 32), :
            ].astype(BF16)
            keep[base : base + 32, :] = chunk_ref[
                pl.ds(pl.multiple_of(64 * f + 32 * core, 32), 32), :
            ]
    out_ref[...] = dot(att_t[...], cot[...])
    sums = [sum_gain[:, 256 * i : 256 * (i + 1)] for i in range(4)]
    sums += [sum_bias[:, 256 * i : 256 * (i + 1)] for i in range(4)]
    spare = jnp.concatenate([head_sums[...], jnp.zeros((8, 128), F32)], 1)
    for f in range(4):
        base = block * f + 128
        vec = jnp.concatenate(sums + [jnp.where(place == f, spare, 0.0)], 0)
        for ref, side in ((send, 1 - core), (keep, core)):
            rows = out_ref[pl.ds(pl.multiple_of(64 * f + 32 * side, 32), 32), :]
            tail = jnp.concatenate([rows[:16, 768:], rows[16:, 768:], vec], 1)
            ref[base : base + 32, :] = rows[:, :768].astype(ref.dtype)
            ref[base + 32 : base + 48, :] = tail.astype(ref.dtype)


def grad_sum_kernel(own, r1, r2, r3, grad_out, qv, i0, i1, i2, i3):
    line, _, core = spot()
    total = adder(own, r1, r2, r3)
    tail = total(slice(160, 176))
    grad_out[:, :768] = total(slice(128, 160))
    grad_out[:16, 768:] = tail[:, :256]
    grad_out[16:, 768:] = tail[:, 256:512]
    qv[...] = jnp.where(core == 0, tail[8:10, 512:544], tail[8:10, 544:576])
    for slot, ref in enumerate((i0, i1, i2, i3)):
        rows = pl.ds(pl.multiple_of(32 * (line ^ slot), 32), 32)
        ref[:32, :] = total(rows).astype(ref.dtype)
        ref[32:, :] = tail.astype(ref.dtype)


def join_in_kernel(i0, i1, i2, i3, out):
    line, _, _ = spot()
    for slot, ref in enumerate((i0, i1, i2, i3)):
        cols = pl.ds(pl.multiple_of((line ^ slot) * 1024, 1024), 1024)
        out[:, cols] = ref[...].astype(F32)


def join_qkv_kernel(i0, i1, i2, i3, out, gain, bias, vec_ref):
    line, _, _ = spot()
    vec = jnp.zeros((VEC, 256), F32)
    for slot, ref in enumerate((i0, i1, i2, i3)):
        for part in range(3):
            cols = pl.ds(pl.multiple_of(1024 * part + (line ^ slot) * 256, 256), 256)
            out[:, cols] = ref[:32, 256 * part : 256 * (part + 1)].astype(F32)
        vec = vec + ref[32:, 512:768].astype(F32)
    vec_ref[...] = owned_lanes(vec)
    gain[...] = vec_ref[pl.ds(line, 1), :]
    bias[...] = vec_ref[pl.ds(4 + line, 1), :]


def wait_kernel(out):
    out[...] = jnp.zeros_like(out)


def tokens_kernel(mixed, r1, r2, r3, qkv, w_out, *rest):
    low, low_rest, grad, grad_rest, tokens, cot, vectors, layer_out, grad_tokens = rest
    line, _, _ = spot()
    rows = low.shape[0]
    mine = pl.ds(pl.multiple_of(rows * line, rows), rows)
    branch = low[...] + low_rest[...].astype(F32)
    grad_ln = grad[...] + grad_rest[...].astype(F32)
    for k, ref in enumerate((mixed.at[mine, :], r1, r2, r3)):
        base = 256 * (line ^ k)
        part = pl.ds(pl.multiple_of(base, 256), 256)
        branch = branch + dot(ref[:, :256], w_out[part, :])
        for i in range(3):
            part = pl.ds(pl.multiple_of(base + 1024 * i, 256), 256)
            grad_ln = grad_ln + dot_nt(ref[:, 256 * (i + 1) : 256 * (i + 2)], qkv[:, part])
    own = tokens[:rows, :]
    branch = branch + own.astype(F32)
    layer_out[...] = (branch + full_row(vectors, 2) + full_row(vectors, 3)).astype(BF16)
    normed, inverse = normalise(own)
    g = grad_ln * full_row(vectors, 0)
    back = inverse * (
        g - jnp.mean(g, -1, keepdims=True) - normed * jnp.mean(g * normed, -1, keepdims=True)
    )
    grad_tokens[...] = (cot[mine, :].astype(F32) + back).astype(BF16)


def turn_tables(count):
    half_rot = ROT // 2
    inverse = 10000.0 ** (-2.0 * np.arange(half_rot) / ROT)
    angles = np.arange(count)[:, None] * inverse[None, :]
    cosine = np.ones((count, HEAD_DIM), np.float32)
    sine = np.zeros((count, HEAD_DIM), np.float32)
    cosine[:, :half_rot] = cosine[:, half_rot:ROT] = np.cos(angles)
    sine[:, :half_rot] = -np.sin(angles)
    sine[:, half_rot:ROT] = np.sin(angles)
    return tuple(np.concatenate([t, t], -1) for t in (cosine, sine))


def head_body(
    tokens,
    block_order,
    ln_gain,
    ln_bias,
    w_qkv,
    qv_bias,
    w_out,
    b_out,
    w_in,
    b_in,
    w_down,
    b_down,
    cotangent,
):
    positions = range(LINES * ACROSS)

    def over_lines(x, k):
        return lax.ppermute(x, "ctx", [(i, i ^ (k * ACROSS)) for i in positions])

    def over_places(x, j):
        return lax.ppermute(x, "ctx", [(i, i ^ j) for i in positions])

    def twin(x):
        return near(lax.ppermute(raw(x), "fsdp", [(0, 1), (1, 0)]))

    def with_lines(blocks):
        return [blocks[0]] + [near(over_lines(raw(blocks[k]), k)) for k in range(1, LINES)]

    def from_lines(x):
        far_one = over_lines(raw(x), 2)
        return [near(over_lines(raw(x), 1)), near(far_one), near(over_lines(far_one, 1))]

    def with_places(blocks):
        return [blocks[0]] + [near(over_places(raw(blocks[j]), j)) for j in range(1, ACROSS)]

    rows, width = tokens.shape[1], tokens.shape[2]
    half = w_qkv.shape[0]
    feed = w_in.shape[1]
    head_cols = width // LINES
    feed_cols = feed // LINES
    qkv_cols = 3 * head_cols
    length = rows * LINES * ACROSS
    line_rows = rows * LINES
    slot_rows = line_rows * 3 // 2
    rotation = turn_tables(length)
    packed_rows = 5 * half + feed_cols + VEC
    table = pltpu.SMEM((32, 128), jnp.int32)
    one_copy = pltpu.SemaphoreType.DMA((1,))
    block = 128 + 128 + VEC
    qkv_block = 128 + 32 + VEC

    last = []

    def run(kernel, out_shapes, scratch, *operands, after=(), loose_in=0):
        results = call(
            kernel, out_shapes, scratch, *operands, after=(*after, *last), loose_in=loose_in
        )
        last[:] = results[:1]
        return results
    (packed,) = run(
        prepare_kernel,
        [near((packed_rows, width), BF16)],
        [pltpu.SemaphoreType.DMA((6,))],
        far(w_qkv), far(w_in), far(w_out), far(w_down),
        *map(far, (ln_gain, ln_bias, b_out, b_down, qv_bias, b_in)),
        loose_in=4,
    )
    (token_block,) = run(
        pack_kernel,
        [near((rows + VEC, width), BF16)],
        [],
        block_order.reshape(2), far(tokens[0]),
    )
    from_two = over_lines(raw(token_block), 2)
    token_lines = [
        token_block,
        near(over_lines(raw(token_block), 1)),
        near(from_two),
        near(over_lines(from_two, 1)),
    ]
    cot_lines = [near(cotangent[0]), *from_lines(cotangent[0])]
    run(wait_kernel, [near((8, 128), F32)], [], after=[near(from_two)])
    qkv, in_rows, w_out_full, down_rows, vectors = run(
        assemble_kernel,
        [
            near((width, 3 * width), BF16),
            near((width, feed_cols), BF16),
            near((width, width), BF16),
            near((feed_cols, width), BF16),
            near((2 * VEC, half), F32),
        ],
        [pltpu.VMEM((2 * VEC, half), BF16), pltpu.SemaphoreType.DMA((13,))],
        packed, twin(packed),
        loose_in=2,
    )
    *slots, ln_low, ln_turned, normed = run(
        project_kernel,
        [near((slot_rows + VEC, 128), BF16)] * 4
        + [
            near((line_rows, width), BF16),
            near((width, line_rows), BF16),
            near((line_rows, width), F32),
        ],
        [],
        *token_lines, vectors, qkv,
    )
    slots_in = with_places(slots)
    hidden, active_turned, low_keep, low_send = run(
        feed_kernel,
        [
            near((line_rows, feed_cols), F32),
            near((feed_cols, line_rows), BF16),
            near((2 * rows, width), F32),
            near((2 * rows, width), BF16),
        ],
        [pltpu.VMEM((line_rows, feed_cols), BF16), pltpu.VMEM((line_rows, width), F32)],
        ln_low, in_rows, vectors, down_rows,
    )
    low_received = near(over_lines(raw(low_send), 1))
    *back_slots, cot_rows = run(
        back_rows_kernel,
        [near((line_rows // 2, 128), BF16)] * 4 + [near((line_rows, width), BF16)],
        [],
        *cot_lines, w_out_full,
    )
    back_in = with_places(back_slots)
    grad_hidden, hidden_sums, feed_grad_low, grad_keep, grad_send = run(
        feed_grad_kernel,
        [
            near((line_rows, feed_cols), BF16),
            near((8, feed_cols), F32),
            near((line_rows, width), F32),
            near((2 * rows, width), F32),
            near((2 * rows, width), BF16),
        ],
        [],
        cot_rows, hidden, in_rows, down_rows,
    )
    grad_received = near(over_lines(raw(grad_send), 1))
    qk_rows, kq_rows, value_rows, attended, lse, numbers = run(
        attend_kernel,
        [
            near((length, 128), BF16),
            near((length, 128), BF16),
            near((length, 64), BF16),
            near((length, 64), F32),
            near((length, 1), F32),
            near((32, 128), jnp.int32),
        ],
        [pltpu.VMEM((length, 128), BF16), table, one_copy],
        *slots_in, *rotation,
    )
    feed_send, feed_keep = run(
        feed_terms_kernel,
        [near((4 * block, width), BF16), near((4 * block, width), F32)],
        [pltpu.VMEM((256, 1024), F32)],
        cot_rows, active_turned, ln_turned, grad_hidden, hidden_sums,
    )
    feed_twin = twin(feed_send)
    *grad_slots, bias_sums = run(
        attend_back_kernel,
        [near((line_rows * 2, 128), BF16)] * 4 + [near((8, 128), F32)],
        [
            pltpu.VMEM((length, 64), BF16),
            pltpu.VMEM((128, length), F32),
            pltpu.VMEM((64, length), F32),
            pltpu.VMEM((length, 128), F32),
            pltpu.VMEM((length, 64), F32),
            table,
            one_copy,
        ],
        *back_in, numbers, qk_rows, kq_rows, value_rows, attended, lse, *rotation,
    )
    grad_slots_in = with_places(grad_slots)
    low_own, low_half = run(
        halve_kernel,
        [near((rows, width), F32), near((rows, width), BF16)],
        [],
        low_keep, low_received,
    )
    low_rest = near(over_lines(raw(low_half), 2))
    feed_blocks = run(
        share_twin_kernel,
        [near((block, width), F32)] + [near((block, width), BF16)] * 3,
        [],
        feed_keep, feed_twin,
    )
    feed_in = with_places(feed_blocks)
    mixed, att_turned, *mixed_slots = run(
        unpack_kernel,
        [near((line_rows, width), BF16), near((head_cols, line_rows), BF16)]
        + [near((rows, width), BF16)] * 3,
        [],
        *grad_slots_in,
    )
    _, *mixed_in = with_lines([mixed, *mixed_slots])
    qkv_send, qkv_keep = run(
        grads_kernel,
        [near((4 * qkv_block, qkv_cols), BF16), near((4 * qkv_block, qkv_cols), F32)],
        [
            pltpu.VMEM((line_rows, width), F32),
            pltpu.VMEM((256, qkv_cols), F32),
            pltpu.VMEM((head_cols, width), F32),
        ],
        mixed, feed_grad_low, normed, ln_turned, qkv, att_turned, cot_rows, bias_sums,
    )
    qkv_terms = twin(qkv_send)
    grad_own, grad_half = run(
        halve_kernel,
        [near((rows, width), F32), near((rows, width), BF16)],
        [],
        grad_keep, grad_received,
    )
    grad_rest = near(over_lines(raw(grad_half), 2))
    qkv_blocks = run(
        share_twin_kernel,
        [near((qkv_block, qkv_cols), F32)] + [near((qkv_block, qkv_cols), BF16)] * 3,
        [],
        qkv_keep, qkv_terms,
    )
    qkv_sums = with_places(qkv_blocks)
    grad_down, grad_b_in, grad_b, *in_slots = run(
        feed_sum_kernel,
        [((128, width), F32), ((1, 128), F32), ((1, 32), F32), near((32, width), F32)]
        + [near((32, width), BF16)] * 3,
        [],
        *feed_in,
    )
    in_parts = with_lines(in_slots)
    grad_out, grad_qv, *qkv_parts = run(
        grad_sum_kernel,
        [((32, width), F32), ((2, 32), F32), near((32 + VEC, qkv_cols), F32)]
        + [near((32 + VEC, qkv_cols), BF16)] * 3,
        [],
        *qkv_sums,
    )
    qkv_parts = with_lines(qkv_parts)
    layer_out, grad_tokens = run(
        tokens_kernel,
        [((rows, width), BF16), ((rows, width), BF16)],
        [],
        mixed, *mixed_in, qkv, w_out_full, low_own, low_rest, grad_own, grad_rest,
        token_block, cot_rows, vectors,
    )
    (grad_in,) = run(join_in_kernel, [((32, feed), F32)], [], *in_parts)
    grad_qkv, grad_gain, grad_shift = run(
        join_qkv_kernel,
        [((32, 3 * width), F32), ((1, 32), F32), ((1, 32), F32)],
        [pltpu.VMEM((VEC, 32), F32)],
        *qkv_parts,
    )
    return (
        layer_out[None],
        grad_tokens[None],
        grad_gain[0],
        grad_shift[0],
        grad_qkv,
        grad_qv,
        grad_out,
        grad_b[0],
        grad_in,
        grad_b_in[0],
        grad_down,
        grad_b[0],
    )


def solution(mesh):
    one_head_each = mesh.shape["ctx"] == HEADS and mesh.shape["fsdp"] == 2
    return jax.shard_map(
        head_body if one_head_each else body,
        mesh=mesh,
        in_specs=(
            P("fsdp", "ctx", None),
            P("ctx", None),
            P("fsdp"),
            P("fsdp"),
            P("fsdp", None),
            P(None, "fsdp"),
            P("fsdp", None),
            P("fsdp"),
            P("fsdp", None),
            P("fsdp"),
            P("fsdp", None),
            P("fsdp"),
            P("fsdp", "ctx", None),
        ),
        out_specs=(
            P("fsdp", "ctx", None),
            P("fsdp", "ctx", None),
            P(("ctx", "fsdp")),
            P(("ctx", "fsdp")),
            P(("ctx", "fsdp"), None),
            P(None, ("ctx", "fsdp")),
            P(("ctx", "fsdp"), None),
            P(("ctx", "fsdp")),
            P(("ctx", "fsdp"), None),
            P(("ctx", "fsdp")),
            P(("ctx", "fsdp"), None),
            P(("ctx", "fsdp")),
        ),
        check_vma=False,
    )
```

```python
from functools import partial
import math

import jax
import jax.numpy as jnp
import numpy as np
from jax import lax
from jax.experimental import pallas as pl
from jax.experimental.pallas import tpu as pltpu
from jax.sharding import PartitionSpec as P

HEADS = 16
HEAD_DIM = 64
ROT = 16


epsilon = 1e-05


def from_behind(block, axis, distance):
    devices = range(lax.axis_size(axis))
    route = [((i - distance) % len(devices), i) for i in devices]
    return lax.ppermute(block, axis, route)


def rotate(vectors, cosine, sine_part):
    half_rot = ROT // 2
    rotary_part = vectors[..., :ROT]
    turned = jnp.concatenate([-rotary_part[..., half_rot:], rotary_part[..., :half_rot]], -1)
    return jnp.concatenate([rotary_part * cosine + turned * sine_part, vectors[..., ROT:]], -1)


def tables(positions):
    freq_index = jnp.arange(ROT // 2, dtype=jnp.float32)
    inverse = 10000.0 ** (-2.0 * freq_index / ROT)
    angles = positions.astype(jnp.float32)[:, None] * inverse[None, :]
    angles = jnp.concatenate([angles, angles], -1)
    return (jnp.cos(angles), jnp.sin(angles))


def spread_positions(orders, half_rows):
    offsets = jnp.arange(half_rows, dtype=jnp.int32)
    return (orders[:, :, None] * half_rows + offsets[None, None, :]).reshape(-1)


def outer_sum(left_side, right_side):
    return lax.dot_general(
        left_side, right_side, (((0,), (0,)), ((), ())), preferred_element_type=jnp.float32
    )


def times_transposed(left_side, right_side):
    return lax.dot_general(
        left_side, right_side, (((1,), (1,)), ((), ())), preferred_element_type=jnp.float32
    )


def attend_block(carried, queries, query_pos, key_rows, value_rows, key_pos, score_scale):
    row_max, row_sum, weighted = carried
    scores = (
        jnp.einsum("qhd,khd->hqk", queries, key_rows, preferred_element_type=jnp.float32)
        * score_scale
    )
    allowed = (query_pos[:, None] >= key_pos[None, :])[None]
    new_max = jnp.maximum(row_max, jnp.max(jnp.where(allowed, scores, -1e30), -1))
    weights = jnp.where(allowed, jnp.exp(scores - new_max[:, :, None]), 0.0)
    rescale = jnp.exp(row_max - new_max)
    row_sum = row_sum * rescale + jnp.sum(weights, -1)
    weighted = weighted * rescale.T[:, :, None] + jnp.einsum(
        "hqk,khd->qhd", weights.astype(jnp.bfloat16), value_rows, preferred_element_type=jnp.float32
    )
    return (new_max, row_sum, weighted)


def block_grads(
    queries, grad_rows, log_sum, delta_rows, query_pos, key_rows, value_rows, key_pos, score_scale
):
    scores = (
        jnp.einsum("qhd,khd->hqk", queries, key_rows, preferred_element_type=jnp.float32)
        * score_scale
    )
    allowed = (query_pos[:, None] >= key_pos[None, :])[None]
    probs = jnp.where(allowed, jnp.exp(scores - log_sum[:, :, None]), 0.0)
    grad_values = jnp.einsum(
        "hqk,qhd->khd", probs.astype(jnp.bfloat16), grad_rows, preferred_element_type=jnp.float32
    )
    grad_probs = jnp.einsum(
        "qhd,khd->hqk", grad_rows, value_rows, preferred_element_type=jnp.float32
    )
    grad_scores = (probs * (grad_probs - delta_rows[:, :, None])).astype(jnp.bfloat16)
    grad_queries = (
        jnp.einsum("hqk,khd->qhd", grad_scores, key_rows, preferred_element_type=jnp.float32)
        * score_scale
    )
    grad_keys = (
        jnp.einsum("hqk,qhd->khd", grad_scores, queries, preferred_element_type=jnp.float32)
        * score_scale
    )
    return (grad_queries, grad_keys, grad_values)


def body(
    tokens,
    block_order,
    ln_gain,
    ln_bias,
    w_qkv,
    qv_bias,
    w_out,
    b_out,
    w_in,
    b_in,
    w_down,
    b_down,
    cotangent,
):
    gathered = (
        lax.all_gather(ln_gain, "fsdp", axis=0, tiled=True),
        lax.all_gather(ln_bias, "fsdp", axis=0, tiled=True),
        lax.all_gather(w_qkv, "fsdp", axis=0, tiled=True),
        lax.all_gather(qv_bias, "fsdp", axis=1, tiled=True),
        lax.all_gather(w_out, "fsdp", axis=0, tiled=True),
        lax.all_gather(b_out, "fsdp", axis=0, tiled=True),
        lax.all_gather(w_in, "fsdp", axis=0, tiled=True),
        lax.all_gather(b_in, "fsdp", axis=0, tiled=True),
        lax.all_gather(w_down, "fsdp", axis=0, tiled=True),
        lax.all_gather(b_down, "fsdp", axis=0, tiled=True),
    )
    (
        gain_full,
        shift_full,
        qkv_full,
        bias_full,
        out_full,
        out_bias,
        in_full,
        in_bias,
        down_full,
        down_bias,
    ) = gathered
    tok_rows = tokens.shape[1]
    model_width = tokens.shape[2]
    half_rows = tok_rows // 2
    score_scale = HEAD_DIM ** (-0.5)
    head_shape = (tok_rows, HEADS, HEAD_DIM)
    flat_shape = (tok_rows, model_width)
    inputs = tokens[0].astype(jnp.float32)
    row_mean = jnp.mean(inputs, -1, keepdims=True)
    centered = inputs - row_mean
    inverse = lax.rsqrt(jnp.mean(centered * centered, -1, keepdims=True) + epsilon)
    normed = centered * inverse
    ln_out = (normed * gain_full.astype(jnp.float32) + shift_full.astype(jnp.float32)).astype(
        jnp.bfloat16
    )
    qkv_pre = jnp.dot(ln_out, qkv_full, preferred_element_type=jnp.float32)
    positions = spread_positions(block_order, half_rows)
    cosine, sine_part = tables(positions)
    cosine = cosine[:, None, :]
    sine_part = sine_part[:, None, :]
    query_pre = qkv_pre[:, :model_width] + bias_full[0].astype(jnp.float32)
    query_rows = rotate(query_pre.reshape(head_shape), cosine, sine_part).astype(jnp.bfloat16)
    key_rows = rotate(
        qkv_pre[:, model_width : 2 * model_width].reshape(head_shape), cosine, sine_part
    ).astype(jnp.bfloat16)
    value_rows = (qkv_pre[:, 2 * model_width :] + bias_full[1].astype(jnp.float32)).astype(
        jnp.bfloat16
    )
    key_flat = key_rows.reshape(flat_shape)
    start_state = (
        jnp.full((HEADS, tok_rows), -1e30, jnp.float32),
        jnp.zeros((HEADS, tok_rows), jnp.float32),
        jnp.zeros(head_shape, jnp.float32),
    )
    carried = start_state
    piece_keys = lax.all_gather(key_flat, "ctx", axis=0, tiled=True)
    piece_values = lax.all_gather(value_rows, "ctx", axis=0, tiled=True)
    piece_orders = lax.all_gather(block_order, "ctx", axis=0, tiled=True)
    shard_count = piece_orders.shape[0]
    group_size = math.gcd(shard_count, max(1, 1024 // tok_rows))
    rounds = shard_count // group_size
    stacked = (
        piece_keys.reshape(rounds, group_size * tok_rows, HEADS, HEAD_DIM),
        piece_values.reshape(rounds, group_size * tok_rows, HEADS, HEAD_DIM),
        piece_orders.reshape(rounds, group_size, 2),
    )

    def one_round(inner_state, block_item):
        key_pos = spread_positions(block_item[2], half_rows)
        return (
            attend_block(
                inner_state,
                query_rows,
                positions,
                block_item[0],
                block_item[1],
                key_pos,
                score_scale,
            ),
            None,
        )

    carried, _ = lax.scan(one_round, carried, stacked)
    row_max, row_sum, weighted = carried
    attended_f32 = weighted / row_sum.T[:, :, None]
    log_sum = row_max + jnp.log(row_sum)
    attended = attended_f32.reshape(flat_shape).astype(jnp.bfloat16)
    branch = jnp.dot(attended, out_full, preferred_element_type=jnp.float32) + out_bias.astype(
        jnp.float32
    )
    hidden = jnp.dot(ln_out, in_full, preferred_element_type=jnp.float32) + in_bias.astype(
        jnp.float32
    )
    active = jax.nn.gelu(hidden, approximate=False).astype(jnp.bfloat16)
    feed_out = jnp.dot(active, down_full, preferred_element_type=jnp.float32) + down_bias.astype(
        jnp.float32
    )
    layer_out = (inputs + branch + feed_out).astype(jnp.bfloat16)[None]
    gain_back, qkv_back, out_back, in_back, down_back = (
        gain_full,
        qkv_full,
        out_full,
        in_full,
        down_full,
    )
    grad_out = cotangent[0]
    grad_f32 = grad_out.astype(jnp.float32)
    grad_attended = times_transposed(grad_out, out_back).astype(jnp.bfloat16).reshape(head_shape)
    grad_active = times_transposed(grad_out, down_back)
    _, gelu_pull = jax.vjp(partial(jax.nn.gelu, approximate=False), hidden)
    grad_hidden = gelu_pull(grad_active)[0].astype(jnp.bfloat16)
    delta_rows = jnp.sum(grad_attended.astype(jnp.float32) * attended_f32, -1).T
    cotangent_sum = jnp.sum(grad_f32, 0)
    term_out_w = outer_sum(attended, grad_out)
    term_in_w = outer_sum(ln_out, grad_hidden)
    term_in_b = jnp.sum(grad_hidden.astype(jnp.float32), 0)
    term_down_w = outer_sum(active, grad_out)
    cycle_size = lax.axis_size("ctx")
    zeros_flat = jnp.zeros(flat_shape, jnp.float32)
    zeros_heads = jnp.zeros(head_shape, jnp.float32)

    def send_home(grad_keys, grad_values):
        return (
            from_behind(grad_keys.astype(jnp.bfloat16), "ctx", 1).astype(grad_keys.dtype),
            from_behind(grad_values.astype(jnp.bfloat16), "ctx", 1).astype(grad_values.dtype),
        )

    def visit_keys(carried):
        visit_key, visit_value, visit_order, grad_keys, grad_values, grad_query = carried
        part_query, part_key, part_value = block_grads(
            query_rows,
            grad_attended,
            log_sum,
            delta_rows,
            positions,
            visit_key.reshape(head_shape),
            visit_value.reshape(head_shape),
            spread_positions(visit_order, half_rows),
            score_scale,
        )
        return (
            grad_keys + part_key.reshape(flat_shape),
            grad_values + part_value.reshape(flat_shape),
            grad_query + part_query,
        )

    def cycle_step(step_index, carried):
        grad_keys, grad_values, grad_query = visit_keys(carried)
        visit_key, visit_value, visit_order = from_behind(
            (carried[0], carried[1], carried[2]), "ctx", 1
        )
        grad_keys, grad_values = send_home(grad_keys, grad_values)
        return (visit_key, visit_value, visit_order, grad_keys, grad_values, grad_query)

    carried = lax.fori_loop(
        0,
        cycle_size - 1,
        cycle_step,
        (key_flat, value_rows, block_order, zeros_flat, zeros_flat, zeros_heads),
    )
    grad_keys, grad_values, grad_query = visit_keys(carried)
    grad_keys, grad_values = send_home(grad_keys, grad_values)
    grad_keys = grad_keys.reshape(head_shape)
    grad_values = grad_values.reshape(head_shape)
    grad_q_pre = rotate(grad_query, cosine, -sine_part).reshape(flat_shape).astype(jnp.bfloat16)
    grad_k_pre = rotate(grad_keys, cosine, -sine_part).reshape(flat_shape).astype(jnp.bfloat16)
    grad_v_pre = grad_values.reshape(flat_shape).astype(jnp.bfloat16)
    grad_qkv = jnp.concatenate([grad_q_pre, grad_k_pre, grad_v_pre], -1)
    grad_ln = times_transposed(grad_qkv, qkv_back) + times_transposed(grad_hidden, in_back)
    grad_normed = grad_ln * gain_back.astype(jnp.float32)
    grad_inputs = inverse * (
        grad_normed
        - jnp.mean(grad_normed, -1, keepdims=True)
        - normed * jnp.mean(grad_normed * normed, -1, keepdims=True)
    )
    grad_tokens = (grad_f32 + grad_inputs).astype(jnp.bfloat16)[None]
    term_gain = jnp.sum(grad_ln * normed, 0)
    term_bias = jnp.sum(grad_ln, 0)
    term_qkv = outer_sum(ln_out, grad_qkv)
    term_qv = jnp.stack(
        [jnp.sum(grad_q_pre.astype(jnp.float32), 0), jnp.sum(grad_v_pre.astype(jnp.float32), 0)], 0
    )
    (
        sum_gain,
        sum_bias,
        sum_qkv,
        sum_qv,
        sum_out_w,
        sum_out_b,
        sum_in_w,
        sum_in_b,
        sum_down_w,
        sum_down_b,
    ) = (
        lax.psum_scatter(term_gain, ("ctx", "fsdp"), scatter_dimension=0, tiled=True),
        lax.psum_scatter(term_bias, ("ctx", "fsdp"), scatter_dimension=0, tiled=True),
        lax.psum_scatter(term_qkv, ("ctx", "fsdp"), scatter_dimension=0, tiled=True),
        lax.psum_scatter(term_qv, ("ctx", "fsdp"), scatter_dimension=1, tiled=True),
        lax.psum_scatter(term_out_w, ("ctx", "fsdp"), scatter_dimension=0, tiled=True),
        lax.psum_scatter(cotangent_sum, ("ctx", "fsdp"), scatter_dimension=0, tiled=True),
        lax.psum_scatter(term_in_w, ("ctx", "fsdp"), scatter_dimension=0, tiled=True),
        lax.psum_scatter(term_in_b, ("ctx", "fsdp"), scatter_dimension=0, tiled=True),
        lax.psum_scatter(term_down_w, ("ctx", "fsdp"), scatter_dimension=0, tiled=True),
        lax.psum_scatter(cotangent_sum, ("ctx", "fsdp"), scatter_dimension=0, tiled=True),
    )
    return (
        layer_out,
        grad_tokens,
        sum_gain,
        sum_bias,
        sum_qkv,
        sum_qv,
        sum_out_w,
        sum_out_b,
        sum_in_w,
        sum_in_b,
        sum_down_w,
        sum_down_b,
    )


LINES = 4
ACROSS = HEADS // LINES
F32 = jnp.float32
BF16 = jnp.bfloat16
VMEM_LIMIT = 16 * 1024 * 1024
TIMES = {'hold': 5000, 'project': 80, 'feed_grad': 40, 'halve': 400, 'unpack': 150, 'feed_sum': 150, 'back_rows': 80, 'feed_terms': 5, 'share_twin': 400, 'join_in': 5}

VEC = 16


def dot(left, right):
    return jnp.dot(left, right, preferred_element_type=F32)


def dot_nt(left, right):
    return lax.dot_general(left, right, (((1,), (1,)), ((), ())), preferred_element_type=F32)


class Far(tuple):
    pass


class Near(tuple):
    pass


def far(*x):
    return Far(x)


def near(*x):
    return Near(x)


def raw(x):
    return x[0] if isinstance(x, (Far, Near)) else x


def spot():
    context = lax.axis_index("ctx")
    return context // ACROSS, context % ACROSS, lax.axis_index("fsdp")


def call(kernel, out_shapes, scratch, *operands, after=(), loose_in=0):
    whole = pl.BlockSpec(memory_space=pltpu.VMEM)
    loose = pl.BlockSpec(memory_space=pl.ANY)
    arrays, specs = [], []
    for x in operands:
        if isinstance(x, Far):
            arrays.append(pltpu.with_memory_space_constraint(x[0], pltpu.HBM))
        elif isinstance(x, Near):
            arrays.append(pltpu.with_memory_space_constraint(x[0], pltpu.VMEM))
        else:
            arrays.append(x)
        if arrays[-1].dtype == jnp.int32 and arrays[-1].ndim == 1:
            specs.append(pl.BlockSpec(memory_space=pltpu.SMEM))
        else:
            specs.append(loose if len(specs) < loose_in else whole)
    outs = []
    for shape in out_shapes:
        if isinstance(shape, Far):
            outs.append(pltpu.HBM(*shape))
        elif isinstance(shape, Near):
            outs.append(pltpu.VMEM(*shape))
        else:
            outs.append(jax.ShapeDtypeStruct(*shape))
    count = len(arrays)

    def body(*refs):
        kernel(*refs[:count], *refs[count + len(after) :])

    name = kernel.__name__.removesuffix("_kernel")
    results = pl.pallas_call(
        body,
        name=name,
        out_shape=outs,
        in_specs=specs + [loose] * len(after),
        out_specs=[whole for _ in outs],
        scratch_shapes=scratch,
        compiler_params=pltpu.CompilerParams(vmem_limit_bytes=VMEM_LIMIT),
        cost_estimate=pl.CostEstimate(
            flops=TIMES.get(name, 0) * 115_000_000, bytes_accessed=0, transcendentals=0
        ),
    )(*arrays, *map(raw, after))
    return [
        near(x) if isinstance(shape, Near) else x for x, shape in zip(results, out_shapes)
    ]


def run_copies(pairs, sems):
    copies = [pltpu.make_async_copy(x, y, sems.at[i]) for i, (x, y) in enumerate(pairs)]
    for copy in copies:
        copy.start()
    for copy in copies:
        copy.wait()


def prepare_kernel(qkv, w_in, w_out, w_down, gain, shift, b_out, b_down, qv, b_in, packed, sems):
    line, _, _ = spot()
    feed = w_in.shape[1] // LINES
    half, width = w_out.shape
    part = line % (LINES // 2)
    row = 0
    pairs = []
    sources = [
        w_in.at[:, pl.ds(pl.multiple_of(feed * line, 128), feed)],
        w_out,
        w_down.at[pl.ds(pl.multiple_of(feed * part, 16), feed), :],
    ]
    for source in sources + [qkv.at[:, width * i : width * (i + 1)] for i in range(3)]:
        pairs.append((source, packed.at[row : row + source.shape[0], :]))
        row += source.shape[0]
    rows = [x[...].astype(F32).reshape(1, half) for x in (gain, shift, b_out, b_down)]
    rows += [qv[...].astype(F32), b_in[...].astype(F32).reshape(4, half)]
    rows.append(jnp.zeros((VEC - 10, half), F32))
    packed[row : row + VEC, :half] = jnp.concatenate(rows, 0).astype(BF16)
    run_copies(pairs, sems)


def assemble_kernel(own, twin, qkv, w_in, w_out, w_down, vectors, low, sems):
    line, _, core = spot()
    width = w_out.shape[1]
    half = width // 2
    feed = w_down.shape[0]
    down_row = 2 * half
    qkv_row = down_row + feed
    vec_row = qkv_row + 3 * half
    pairs = []
    for source, side in ((own, core), (twin, 1 - core)):
        rows = pl.ds(pl.multiple_of(half * side, half), half)
        pairs.append((source.at[:half, :], w_in.at[rows, :]))
        pairs.append((source.at[half:down_row, :], w_out.at[rows, :]))
        for i in range(3):
            base = qkv_row + half * i
            pairs.append(
                (source.at[base : base + half, :], qkv.at[rows, width * i : width * (i + 1)])
            )
        spare = pl.ds(pl.multiple_of(VEC * side, VEC), VEC)
        pairs.append((source.at[vec_row:, :half], low.at[spare, :]))
    holds = core == line // (LINES // 2)

    @pl.when(holds)
    def _():
        run_copies(pairs + [(own.at[down_row:qkv_row, :], w_down)], sems)

    @pl.when(jnp.logical_not(holds))
    def _():
        run_copies(pairs + [(twin.at[down_row:qkv_row, :], w_down)], sems)

    vectors[...] = low[...].astype(F32)


def line_columns(qkv, part):
    line, _, _ = spot()
    width = qkv.shape[1] // 3
    base = width * part + width // LINES * line
    return qkv[:, pl.ds(pl.multiple_of(base, 128), width // LINES)]


def line_rows_of(w_out):
    line, _, _ = spot()
    count = w_out.shape[0] // LINES
    return w_out[pl.ds(pl.multiple_of(count * line, 16), count), :]


def full_row(vectors, index):
    return jnp.concatenate(
        [vectors[index : index + 1, :], vectors[VEC + index : VEC + index + 1, :]], 1
    )


def pack_kernel(order, tokens, packed):
    rows = tokens.shape[0]
    packed[:rows, :] = tokens[...]
    lane = lax.broadcasted_iota(jnp.int32, (VEC, 128), 1)
    numbers = jnp.where(lane == 0, order[0], jnp.where(lane == 1, order[1], 0))
    packed[rows:, :128] = numbers.astype(F32).astype(BF16)
    packed[rows:, 128:] = jnp.zeros((VEC, tokens.shape[1] - 128), BF16)


def reorder(chunks, place):
    upper, lower = chunks
    turned = (place & 2) != 0
    near_by = (place & 1) != 0
    first = jnp.where(turned, lower, upper)
    second = jnp.where(turned, upper, lower)
    first = jnp.where(near_by, pltpu.roll(first, 64, 1), first)
    second = jnp.where(near_by, pltpu.roll(second, 64, 1), second)
    return first, second


def left_lanes(rows):
    return lax.broadcasted_iota(jnp.int32, (rows, 128), 1) < 64


def pair_heads(one, two, slot):
    keep = left_lanes(one.shape[0])
    if slot % 2 == 0:
        return jnp.where(keep, one, pltpu.roll(two, 64, 1))
    return jnp.where(keep, pltpu.roll(one, 64, 1), two)


def fold_rows(chunk, slot):
    rows = chunk.shape[0] // 2
    return pair_heads(chunk[:rows], chunk[rows:], slot)


def unfold_pair(even, odd):
    keep = left_lanes(even.shape[0])
    top = jnp.where(keep, even, pltpu.roll(odd, 64, 1))
    bottom = jnp.where(keep, pltpu.roll(even, 64, 1), odd)
    return jnp.concatenate([top, bottom], 0)


def normalise(rows):
    x = rows.astype(F32)
    centred = x - jnp.mean(x, -1, keepdims=True)
    inverse = lax.rsqrt(jnp.mean(centred * centred, -1, keepdims=True) + epsilon)
    return centred * inverse, inverse


def two_chunks(x):
    return x[:, :128], x[:, 128:256]


def two_chunks(x):
    return x[:, :128], x[:, 128:256]


def project_kernel(t0, t1, t2, t3, vectors, qkv, s0, s1, s2, s3, ln_ref, lnt_ref, normed_ref):
    line, place, _ = spot()
    rows = t0.shape[0] - VEC
    gain, shift = full_row(vectors, 0), full_row(vectors, 1)
    numbers = jnp.zeros((VEC, 128), F32)
    for k, ref in enumerate((t0, t1, t2, t3)):
        source = line ^ k
        part = pl.ds(pl.multiple_of(rows * source, rows), rows)
        normed, _ = normalise(ref[:rows, :])
        normed_ref[part, :] = normed
        ln_ref[part, :] = (normed * gain + shift).astype(BF16)
        numbers = numbers + pltpu.roll(ref[rows:, :128].astype(F32), 2 * source, 1)
    side = VEC * (line // (LINES // 2))
    lanes = pl.ds(pl.multiple_of(256 * (line % (LINES // 2)), 256), 256)
    bias_q = vectors[pl.ds(side + 4, 1), lanes]
    bias_v = vectors[pl.ds(side + 5, 1), lanes]
    q_chunks = reorder(two_chunks(dot(ln_ref[...], line_columns(qkv, 0)) + bias_q), place)
    k_chunks = reorder(two_chunks(dot(ln_ref[...], line_columns(qkv, 1))), place)
    v_chunks = reorder(two_chunks(dot(ln_ref[...], line_columns(qkv, 2)) + bias_v), place)
    total = ln_ref.shape[0]
    end = total * 3 // 2
    for slot, ref in enumerate((s0, s1, s2, s3)):
        pair = slot // 2
        ref[:total, :] = pair_heads(q_chunks[pair], k_chunks[pair], slot).astype(BF16)
        ref[total:end, :] = fold_rows(v_chunks[pair], slot).astype(BF16)
        ref[end:, :] = numbers.astype(BF16)
    lnt_ref[...] = ln_ref[...].T


def back_rows_kernel(c0, c1, c2, c3, w_out, s0, s1, s2, s3, cot):
    line, place, _ = spot()
    rows = c0.shape[0]
    for k, ref in enumerate((c0, c1, c2, c3)):
        cot[pl.ds(pl.multiple_of(rows * (line ^ k), rows), rows), :] = ref[...]
    chunks = reorder(two_chunks(dot_nt(cot[...], line_rows_of(w_out))), place)
    for slot, ref in enumerate((s0, s1, s2, s3)):
        ref[...] = fold_rows(chunks[slot // 2], slot).astype(BF16)


def block_rows(table):
    for j in range(4):
        for i in range(8):
            yield j, i, pl.ds(pl.multiple_of(table[8 * j, i] * 64, 64), 64)


def sort_rows(table, slots, target, base, folded):
    for j, i, dest in block_rows(table):
        if folded:
            start = base + 64 * (i % 4)
            lanes = slice(0, 64) if i < 4 else slice(64, 128)
            target[dest, :] = slots[j][start : start + 64, lanes]
        else:
            target[dest, :] = slots[j][base + 64 * i : base + 64 * (i + 1), :]


def turn(x, cosine, sine):
    lane = lax.broadcasted_iota(jnp.int32, x.shape, 1) & (HEAD_DIM - 1)
    other = jnp.where(lane < ROT // 2, pltpu.roll(x, 120, 1), pltpu.roll(x, 8, 1))
    return x * cosine + other * sine


TILE = 256


def scores_of(qk_ref, i):
    rows = slice(TILE * i, TILE * (i + 1))
    queries = jnp.where(left_lanes(TILE), qk_ref[rows, :], jnp.zeros((), BF16))
    queries = queries * jnp.asarray(HEAD_DIM ** (-0.5), BF16)
    return queries


def allowed_tile():
    row = lax.broadcasted_iota(jnp.int32, (TILE, TILE), 0)
    col = lax.broadcasted_iota(jnp.int32, (TILE, TILE), 1)
    return row >= col


def attend_kernel(r0, r1, r2, r3, cosine, sine, *rest):
    qk_ref, kq_ref, v_ref, att_ref, lse_ref, table_ref, raw, table, sem = rest
    refs = (r0, r1, r2, r3)
    count = qk_ref.shape[0]
    lines = count // 4
    for j, ref in enumerate(refs):
        numbers = ref[lines * 3 // 2 :, :].astype(F32)[:8, :]
        table_ref[8 * j : 8 * (j + 1), :] = numbers.astype(jnp.int32)
    run_copies([(table_ref, table)], sem)
    sort_rows(table, refs, raw, 0, False)
    sort_rows(table, refs, v_ref, lines, True)
    for i in range(count // TILE):
        rows = slice(TILE * i, TILE * (i + 1))
        turned = turn(raw[rows, :].astype(F32), cosine[rows, :], sine[rows, :])
        qk_ref[rows, :] = turned.astype(BF16)
        kq_ref[rows, :] = pltpu.roll(turned, 64, 1).astype(BF16)
    mask = allowed_tile()
    for i in range(count // TILE):
        rows = slice(TILE * i, TILE * (i + 1))
        keys = TILE * (i + 1)
        scores = dot_nt(scores_of(qk_ref, i), kq_ref[:keys, :])
        last = jnp.where(mask, scores[:, keys - TILE :], -1e30)
        scores = last if i == 0 else jnp.concatenate([scores[:, : keys - TILE], last], 1)
        top = jnp.max(scores, -1, keepdims=True)
        weights = jnp.exp(scores - top)
        total = jnp.sum(weights, -1, keepdims=True)
        weighted = dot(weights.astype(BF16), v_ref[:keys, :])
        att_ref[rows, :] = weighted / total
        lse_ref[rows, :] = top + jnp.log(total)


def attend_back_kernel(r0, r1, r2, r3, table_ref, qk_ref, kq_ref, v_ref, att_ref, *rest):
    lse_ref, cosine, sine, o0, o1, o2, o3, sums, ga_ref, kt_ref, vt_ref, gqk, gv = rest[:13]
    table, sem = rest[13:]
    refs = (r0, r1, r2, r3)
    count = qk_ref.shape[0]
    lines = count // 4
    run_copies([(table_ref, table)], sem)
    sort_rows(table, refs, ga_ref, 0, True)
    mask = allowed_tile()
    kt_ref[...] = jnp.zeros_like(kt_ref)
    vt_ref[...] = jnp.zeros_like(vt_ref)
    for i in range(count // TILE):
        rows = slice(TILE * i, TILE * (i + 1))
        keys = TILE * (i + 1)
        queries = scores_of(qk_ref, i)
        scores = dot_nt(queries, kq_ref[:keys, :])
        last = jnp.where(mask, scores[:, keys - TILE :], -1e30)
        scores = last if i == 0 else jnp.concatenate([scores[:, : keys - TILE], last], 1)
        probs = jnp.exp(scores - lse_ref[rows, :])
        grad_rows = ga_ref[rows, :]
        delta = jnp.sum(grad_rows.astype(F32) * att_ref[rows, :], -1, keepdims=True)
        grad_probs = dot_nt(grad_rows, v_ref[:keys, :])
        grad_scores = (probs * (grad_probs - delta)).astype(BF16)
        gqk[rows, :] = dot(grad_scores, kq_ref[:keys, :]) * HEAD_DIM ** (-0.5)
        vt_ref[:, :keys] += dot(grad_rows.astype(F32).T.astype(BF16), probs.astype(BF16))
        kt_ref[:, :keys] += dot(queries.astype(F32).T.astype(BF16), grad_scores)
    sum_q = jnp.zeros((1, 128), F32)
    sum_v = jnp.zeros((1, 64), F32)
    for i in range(count // TILE):
        rows = slice(TILE * i, TILE * (i + 1))
        grad_keys = pltpu.roll(kt_ref[:, rows].T, 64, 1)
        both = jnp.where(left_lanes(TILE), gqk[rows, :], grad_keys)
        both = turn(both, cosine[rows, :], -sine[rows, :])
        both = both.astype(BF16).astype(F32)
        values = vt_ref[:, rows].T.astype(BF16).astype(F32)
        gqk[rows, :] = both
        gv[rows, :] = values
        sum_q = sum_q + jnp.sum(both, 0, keepdims=True)
        sum_v = sum_v + jnp.sum(values, 0, keepdims=True)
    sums[...] = jnp.zeros_like(sums)
    sums[0:1, :64] = sum_q[:, :64]
    sums[1:2, :64] = sum_v
    outs = (o0, o1, o2, o3)
    for j, i, source in block_rows(table):
        lanes = slice(0, 64) if i < 4 else slice(64, 128)
        outs[j][64 * i : 64 * (i + 1), :] = gqk[source, :].astype(BF16)
        start = lines + 64 * (i % 4)
        outs[j][start : start + 64, lanes] = gv[source, :].astype(BF16)
        start += lines // 2
        outs[j][start : start + 64, lanes] = att_ref[source, :].astype(BF16)


def split_lines(low, keep, send):
    line, _, _ = spot()
    rows = low.shape[0] // LINES
    for k, (ref, base) in enumerate(((keep, 0), (send, 0), (keep, rows), (send, rows))):
        part = pl.ds(pl.multiple_of(rows * (line ^ k), rows), rows)
        ref[base : base + rows, :] = low[part, :].astype(ref.dtype)


def feed_kernel(ln, w_in, vectors, w_down, hidden_ref, actt_ref, keep, send, act_ref, low_ref):
    line, _, _ = spot()
    row = VEC * (line // (LINES // 2)) + 6 + 2 * (line % (LINES // 2))
    bias = jnp.concatenate([vectors[pl.ds(row, 1), :], vectors[pl.ds(row + 1, 1), :]], 1)
    for f in range(4):
        cols = slice(256 * f, 256 * (f + 1))
        hidden = dot(ln[...], w_in[:, cols]) + bias[:, cols]
        hidden_ref[:, cols] = hidden
        active = 0.5 * hidden * (1.0 + lax.erf(hidden * 0.7071067811865476))
        act_ref[:, cols] = active.astype(BF16)
        actt_ref[cols, :] = active.astype(BF16).T
    for f in range(4):
        cols = slice(256 * f, 256 * (f + 1))
        low_ref[:, cols] = dot(act_ref[...], w_down[:, cols])
    split_lines(low_ref, keep, send)


def feed_grad_kernel(cot, hidden, w_in, w_down, gh_ref, sums, low_ref, keep, send):
    for f in range(4):
        cols = slice(256 * f, 256 * (f + 1))
        grad_active = dot_nt(cot[...], w_down[cols, :])
        h = hidden[:, cols]
        slope = 0.5 * (1.0 + lax.erf(h * 0.7071067811865476)) + h * jnp.exp(
            -0.5 * h * h
        ) * 0.3989422804014327
        grad_hidden = (slope * grad_active).astype(BF16)
        gh_ref[:, cols] = grad_hidden
        total = jnp.sum(grad_hidden.astype(F32), 0, keepdims=True)
        sums[:, cols] = jnp.broadcast_to(total, (8, 256))
    for i in range(4):
        low_ref[:, 256 * i : 256 * (i + 1)] = dot_nt(gh_ref[...], w_in[256 * i : 256 * (i + 1), :])
    split_lines(low_ref, keep, send)


def feed_terms_kernel(cot_ref, actt, lnt, gh, sums, send, keep, chunk_ref):
    line, _, core = spot()
    cot = cot_ref[...]
    block = send.shape[0] // 4
    for f in range(4):
        chunk_ref[...] = dot(actt[256 * f : 256 * (f + 1), :], cot)
        base = block * f
        send[base : base + 128, :] = chunk_ref[
            pl.ds(pl.multiple_of((1 - core) * 128, 128), 128), :
        ].astype(BF16)
        keep[base : base + 128, :] = chunk_ref[pl.ds(pl.multiple_of(core * 128, 128), 128), :]
    for z in range(4):
        chunk_ref[...] = dot(lnt[256 * z : 256 * (z + 1), :], gh[...])
        for f in range(4):
            base = block * f + 128 + 32 * z
            send[base : base + 32, :] = chunk_ref[
                pl.ds(pl.multiple_of(64 * f + 32 * (1 - core), 32), 32), :
            ].astype(BF16)
            keep[base : base + 32, :] = chunk_ref[
                pl.ds(pl.multiple_of(64 * f + 32 * core, 32), 32), :
            ]
    cot_sum = jnp.sum(cot.astype(F32), 0, keepdims=True)
    picked = jnp.where(
        line < 2,
        jnp.where(line == 0, cot_sum[:, 0:256], cot_sum[:, 256:512]),
        jnp.where(line == 2, cot_sum[:, 512:768], cot_sum[:, 768:1024]),
    )
    zero = jnp.zeros((1, 640), F32)
    for f in range(4):
        even, odd = sums[:1, 256 * f : 256 * f + 128], sums[:1, 256 * f + 128 : 256 * f + 256]
        first = core == 0
        base = block * f + 256
        given = jnp.concatenate([jnp.where(first, odd, even), picked, zero], 1)
        kept = jnp.concatenate([jnp.where(first, even, odd), picked, zero], 1)
        send[base : base + VEC, :] = jnp.broadcast_to(given, (VEC, 1024)).astype(BF16)
        keep[base : base + VEC, :] = jnp.broadcast_to(kept, (VEC, 1024))


def share_twin_kernel(keep, received, o0, o1, o2, o3):
    _, place, _ = spot()
    block = o0.shape[0]
    for slot, ref in enumerate((o0, o1, o2, o3)):
        rows = pl.ds(pl.multiple_of((place ^ slot) * block, 16), block)
        ref[...] = (keep[rows, :] + received[rows, :].astype(F32)).astype(ref.dtype)


def adder(own, r1, r2, r3):
    def total(rows, cols=slice(None)):
        return (own[rows, cols].astype(F32) + r1[rows, cols].astype(F32)) + (
            r2[rows, cols].astype(F32) + r3[rows, cols].astype(F32)
        )

    return total


def owned_lanes(rows):
    _, place, core = spot()
    return pltpu.roll(rows, lax.rem(256 - (64 * place + 32 * core), 256), 1)[:, :32]


def feed_sum_kernel(own, r1, r2, r3, down_ref, bias_in, bias_out, i0, i1, i2, i3):
    line, _, _ = spot()
    total = adder(own, r1, r2, r3)
    down_ref[...] = total(slice(0, 128))
    bias_in[...] = total(slice(256, 264), slice(0, 128))[:1]
    bias_out[...] = owned_lanes(total(slice(256, 264), slice(128, 384)))[:1]
    for slot, ref in enumerate((i0, i1, i2, i3)):
        rows = pl.ds(pl.multiple_of(128 + 32 * (line ^ slot), 32), 32)
        ref[...] = total(rows).astype(ref.dtype)


def halve_kernel(keep, received, own, send):
    rows = own.shape[0]
    own[...] = keep[:rows, :] + received[:rows, :].astype(F32)
    send[...] = (keep[rows:, :] + received[rows:, :].astype(F32)).astype(BF16)


def unpack_kernel(r0, r1, r2, r3, mixed, att_t, s1, s2, s3):
    line, place, _ = spot()
    rows = s1.shape[0]
    total = LINES * rows
    fold = total // 2
    parts = [ref[...].astype(F32) for ref in (r0, r1, r2, r3)]
    keep_left = left_lanes(total)
    chunks = [[], [], [], []]
    for pair in range(2):
        one, two = parts[2 * pair], parts[2 * pair + 1]
        even, odd = one[:total], two[:total]
        values, attended = slice(total, total + fold), slice(total + fold, total + 2 * fold)
        chunks[0].append(unfold_pair(one[attended], two[attended]))
        chunks[1].append(jnp.where(keep_left, even, pltpu.roll(odd, 64, 1)))
        chunks[2].append(jnp.where(keep_left, pltpu.roll(even, 64, 1), odd))
        chunks[3].append(unfold_pair(one[values], two[values]))
    for index, both in enumerate(chunks):
        for pair, chunk in enumerate(reorder(both, place)):
            base = 256 * index + 128 * pair
            mixed[:, base : base + 128] = chunk.astype(BF16)
    for k, ref in ((1, s1), (2, s2), (3, s3)):
        ref[...] = mixed[pl.ds(pl.multiple_of(rows * (line ^ k), rows), rows), :]
    att_t[...] = mixed[:, :256].T


def grads_kernel(mixed, low, normed, lnt, qkv, att_t, cot, head_sums, *rest):
    send, keep, low_ref, chunk_ref, out_ref = rest
    _, place, core = spot()
    low_ref[...] = low[...]
    for i in range(3):
        cols = slice(256 * (i + 1), 256 * (i + 2))
        low_ref[...] += dot_nt(mixed[:, cols], line_columns(qkv, i))
    grad = low_ref[...]
    sum_gain = jnp.sum(grad * normed[...], 0, keepdims=True)
    sum_bias = jnp.sum(grad, 0, keepdims=True)
    block = send.shape[0] // 4
    for z in range(4):
        chunk_ref[...] = dot(lnt[256 * z : 256 * (z + 1), :], mixed[:, 256:])
        for f in range(4):
            base = block * f + 32 * z
            send[base : base + 32, :] = chunk_ref[
                pl.ds(pl.multiple_of(64 * f + 32 * (1 - core), 32), 32), :
            ].astype(BF16)
            keep[base : base + 32, :] = chunk_ref[
                pl.ds(pl.multiple_of(64 * f + 32 * core, 32), 32), :
            ]
    out_ref[...] = dot(att_t[...], cot[...])
    sums = [sum_gain[:, 256 * i : 256 * (i + 1)] for i in range(4)]
    sums += [sum_bias[:, 256 * i : 256 * (i + 1)] for i in range(4)]
    spare = jnp.concatenate([head_sums[...], jnp.zeros((8, 128), F32)], 1)
    for f in range(4):
        base = block * f + 128
        vec = jnp.concatenate(sums + [jnp.where(place == f, spare, 0.0)], 0)
        for ref, side in ((send, 1 - core), (keep, core)):
            rows = out_ref[pl.ds(pl.multiple_of(64 * f + 32 * side, 32), 32), :]
            tail = jnp.concatenate([rows[:16, 768:], rows[16:, 768:], vec], 1)
            ref[base : base + 32, :] = rows[:, :768].astype(ref.dtype)
            ref[base + 32 : base + 48, :] = tail.astype(ref.dtype)


def grad_sum_kernel(own, r1, r2, r3, grad_out, qv, i0, i1, i2, i3):
    line, _, core = spot()
    total = adder(own, r1, r2, r3)
    tail = total(slice(160, 176))
    grad_out[:, :768] = total(slice(128, 160))
    grad_out[:16, 768:] = tail[:, :256]
    grad_out[16:, 768:] = tail[:, 256:512]
    qv[...] = jnp.where(core == 0, tail[8:10, 512:544], tail[8:10, 544:576])
    for slot, ref in enumerate((i0, i1, i2, i3)):
        rows = pl.ds(pl.multiple_of(32 * (line ^ slot), 32), 32)
        ref[:32, :] = total(rows).astype(ref.dtype)
        ref[32:, :] = tail.astype(ref.dtype)


def join_in_kernel(i0, i1, i2, i3, out):
    line, _, _ = spot()
    for slot, ref in enumerate((i0, i1, i2, i3)):
        cols = pl.ds(pl.multiple_of((line ^ slot) * 1024, 1024), 1024)
        out[:, cols] = ref[...].astype(F32)


def join_qkv_kernel(i0, i1, i2, i3, out, gain, bias, vec_ref):
    line, _, _ = spot()
    vec = jnp.zeros((VEC, 256), F32)
    for slot, ref in enumerate((i0, i1, i2, i3)):
        for part in range(3):
            cols = pl.ds(pl.multiple_of(1024 * part + (line ^ slot) * 256, 256), 256)
            out[:, cols] = ref[:32, 256 * part : 256 * (part + 1)].astype(F32)
        vec = vec + ref[32:, 512:768].astype(F32)
    vec_ref[...] = owned_lanes(vec)
    gain[...] = vec_ref[pl.ds(line, 1), :]
    bias[...] = vec_ref[pl.ds(4 + line, 1), :]


def hold_kernel(x, out):
    out[...] = x[...]


def tokens_kernel(mixed, r1, r2, r3, qkv, w_out, *rest):
    low, low_rest, grad, grad_rest, tokens, cot, vectors, layer_out, grad_tokens = rest
    line, _, _ = spot()
    rows = low.shape[0]
    mine = pl.ds(pl.multiple_of(rows * line, rows), rows)
    branch = low[...] + low_rest[...].astype(F32)
    grad_ln = grad[...] + grad_rest[...].astype(F32)
    for k, ref in enumerate((mixed.at[mine, :], r1, r2, r3)):
        base = 256 * (line ^ k)
        part = pl.ds(pl.multiple_of(base, 256), 256)
        branch = branch + dot(ref[:, :256], w_out[part, :])
        for i in range(3):
            part = pl.ds(pl.multiple_of(base + 1024 * i, 256), 256)
            grad_ln = grad_ln + dot_nt(ref[:, 256 * (i + 1) : 256 * (i + 2)], qkv[:, part])
    own = tokens[:rows, :]
    branch = branch + own.astype(F32)
    layer_out[...] = (branch + full_row(vectors, 2) + full_row(vectors, 3)).astype(BF16)
    normed, inverse = normalise(own)
    g = grad_ln * full_row(vectors, 0)
    back = inverse * (
        g - jnp.mean(g, -1, keepdims=True) - normed * jnp.mean(g * normed, -1, keepdims=True)
    )
    grad_tokens[...] = (cot[mine, :].astype(F32) + back).astype(BF16)


def turn_tables(count):
    half_rot = ROT // 2
    inverse = 10000.0 ** (-2.0 * np.arange(half_rot) / ROT)
    angles = np.arange(count)[:, None] * inverse[None, :]
    cosine = np.ones((count, HEAD_DIM), np.float32)
    sine = np.zeros((count, HEAD_DIM), np.float32)
    cosine[:, :half_rot] = cosine[:, half_rot:ROT] = np.cos(angles)
    sine[:, :half_rot] = -np.sin(angles)
    sine[:, half_rot:ROT] = np.sin(angles)
    return tuple(np.concatenate([t, t], -1) for t in (cosine, sine))


def head_body(
    tokens,
    block_order,
    ln_gain,
    ln_bias,
    w_qkv,
    qv_bias,
    w_out,
    b_out,
    w_in,
    b_in,
    w_down,
    b_down,
    cotangent,
):
    positions = range(LINES * ACROSS)

    def over_lines(x, k):
        return lax.ppermute(x, "ctx", [(i, i ^ (k * ACROSS)) for i in positions])

    def over_places(x, j):
        return lax.ppermute(x, "ctx", [(i, i ^ j) for i in positions])

    def twin(x):
        return near(lax.ppermute(raw(x), "fsdp", [(0, 1), (1, 0)]))

    def with_lines(blocks):
        return [blocks[0]] + [near(over_lines(raw(blocks[k]), k)) for k in range(1, LINES)]

    def with_places(blocks):
        return [blocks[0]] + [near(over_places(raw(blocks[j]), j)) for j in range(1, ACROSS)]

    rows, width = tokens.shape[1], tokens.shape[2]
    half = w_qkv.shape[0]
    feed = w_in.shape[1]
    head_cols = width // LINES
    feed_cols = feed // LINES
    qkv_cols = 3 * head_cols
    length = rows * LINES * ACROSS
    line_rows = rows * LINES
    slot_rows = line_rows * 3 // 2
    rotation = turn_tables(length)
    packed_rows = 5 * half + feed_cols + VEC
    table = pltpu.SMEM((32, 128), jnp.int32)
    one_copy = pltpu.SemaphoreType.DMA((1,))
    block = 128 + 128 + VEC
    qkv_block = 128 + 32 + VEC

    last = []

    def run(kernel, out_shapes, scratch, *operands, after=(), loose_in=0):
        results = call(
            kernel, out_shapes, scratch, *operands, after=(*after, *last), loose_in=loose_in
        )
        last[:] = results[:1]
        return results
    (token_block,) = run(
        pack_kernel,
        [near((rows + VEC, width), BF16)],
        [],
        block_order.reshape(2), far(tokens[0]),
    )
    from_two = over_lines(raw(token_block), 2)
    token_lines = [
        token_block,
        near(over_lines(raw(token_block), 1)),
        near(from_two),
        near(over_lines(from_two, 1)),
    ]
    (packed,) = run(
        prepare_kernel,
        [near((packed_rows, width), BF16)],
        [pltpu.SemaphoreType.DMA((6,))],
        far(w_qkv), far(w_in), far(w_out), far(w_down),
        *map(far, (ln_gain, ln_bias, b_out, b_down, qv_bias, b_in)),
        loose_in=4,
    )
    (cot_own,) = run(
        hold_kernel,
        [near((rows, width), BF16)],
        [],
        far(cotangent[0]),
        after=token_lines[1:3],
    )
    cot_lines = with_lines([cot_own] * LINES)
    qkv, in_rows, w_out_full, down_rows, vectors = run(
        assemble_kernel,
        [
            near((width, 3 * width), BF16),
            near((width, feed_cols), BF16),
            near((width, width), BF16),
            near((feed_cols, width), BF16),
            near((2 * VEC, half), F32),
        ],
        [pltpu.VMEM((2 * VEC, half), BF16), pltpu.SemaphoreType.DMA((13,))],
        packed, twin(packed),
        loose_in=2,
    )
    *slots, ln_low, ln_turned, normed = run(
        project_kernel,
        [near((slot_rows + VEC, 128), BF16)] * 4
        + [
            near((line_rows, width), BF16),
            near((width, line_rows), BF16),
            near((line_rows, width), F32),
        ],
        [],
        *token_lines, vectors, qkv,
    )
    slots_in = with_places(slots)
    hidden, active_turned, low_keep, low_send = run(
        feed_kernel,
        [
            near((line_rows, feed_cols), F32),
            near((feed_cols, line_rows), BF16),
            near((2 * rows, width), F32),
            near((2 * rows, width), BF16),
        ],
        [pltpu.VMEM((line_rows, feed_cols), BF16), pltpu.VMEM((line_rows, width), F32)],
        ln_low, in_rows, vectors, down_rows,
    )
    low_received = near(over_lines(raw(low_send), 1))
    *back_slots, cot_rows = run(
        back_rows_kernel,
        [near((line_rows // 2, 128), BF16)] * 4 + [near((line_rows, width), BF16)],
        [],
        *cot_lines, w_out_full,
    )
    back_in = with_places(back_slots)
    grad_hidden, hidden_sums, feed_grad_low, grad_keep, grad_send = run(
        feed_grad_kernel,
        [
            near((line_rows, feed_cols), BF16),
            near((8, feed_cols), F32),
            near((line_rows, width), F32),
            near((2 * rows, width), F32),
            near((2 * rows, width), BF16),
        ],
        [],
        cot_rows, hidden, in_rows, down_rows,
    )
    grad_received = near(over_lines(raw(grad_send), 1))
    qk_rows, kq_rows, value_rows, attended, lse, numbers = run(
        attend_kernel,
        [
            near((length, 128), BF16),
            near((length, 128), BF16),
            near((length, 64), BF16),
            near((length, 64), F32),
            near((length, 1), F32),
            near((32, 128), jnp.int32),
        ],
        [pltpu.VMEM((length, 128), BF16), table, one_copy],
        *slots_in, *rotation,
    )
    feed_send, feed_keep = run(
        feed_terms_kernel,
        [near((4 * block, width), BF16), near((4 * block, width), F32)],
        [pltpu.VMEM((256, 1024), F32)],
        cot_rows, active_turned, ln_turned, grad_hidden, hidden_sums,
    )
    feed_twin = twin(feed_send)
    *grad_slots, bias_sums = run(
        attend_back_kernel,
        [near((line_rows * 2, 128), BF16)] * 4 + [near((8, 128), F32)],
        [
            pltpu.VMEM((length, 64), BF16),
            pltpu.VMEM((128, length), F32),
            pltpu.VMEM((64, length), F32),
            pltpu.VMEM((length, 128), F32),
            pltpu.VMEM((length, 64), F32),
            table,
            one_copy,
        ],
        *back_in, numbers, qk_rows, kq_rows, value_rows, attended, lse, *rotation,
    )
    grad_slots_in = with_places(grad_slots)
    low_own, low_half = run(
        halve_kernel,
        [near((rows, width), F32), near((rows, width), BF16)],
        [],
        low_keep, low_received,
    )
    low_rest = near(over_lines(raw(low_half), 2))
    grad_own, grad_half = run(
        halve_kernel,
        [near((rows, width), F32), near((rows, width), BF16)],
        [],
        grad_keep, grad_received,
    )
    grad_rest = near(over_lines(raw(grad_half), 2))
    mixed, att_turned, *mixed_slots = run(
        unpack_kernel,
        [near((line_rows, width), BF16), near((head_cols, line_rows), BF16)]
        + [near((rows, width), BF16)] * 3,
        [],
        *grad_slots_in,
    )
    _, *mixed_in = with_lines([mixed, *mixed_slots])
    qkv_send, qkv_keep = run(
        grads_kernel,
        [near((4 * qkv_block, qkv_cols), BF16), near((4 * qkv_block, qkv_cols), F32)],
        [
            pltpu.VMEM((line_rows, width), F32),
            pltpu.VMEM((256, qkv_cols), F32),
            pltpu.VMEM((head_cols, width), F32),
        ],
        mixed, feed_grad_low, normed, ln_turned, qkv, att_turned, cot_rows, bias_sums,
    )
    qkv_terms = twin(qkv_send)
    feed_blocks = run(
        share_twin_kernel,
        [near((block, width), F32)] + [near((block, width), BF16)] * 3,
        [],
        feed_keep, feed_twin,
    )
    feed_in = with_places(feed_blocks)
    qkv_blocks = run(
        share_twin_kernel,
        [near((qkv_block, qkv_cols), F32)] + [near((qkv_block, qkv_cols), BF16)] * 3,
        [],
        qkv_keep, qkv_terms,
    )
    qkv_sums = with_places(qkv_blocks)
    grad_down, grad_b_in, grad_b, *in_slots = run(
        feed_sum_kernel,
        [((128, width), F32), ((1, 128), F32), ((1, 32), F32), near((32, width), F32)]
        + [near((32, width), BF16)] * 3,
        [],
        *feed_in,
    )
    in_parts = with_lines(in_slots)
    layer_out, grad_tokens = run(
        tokens_kernel,
        [((rows, width), BF16), ((rows, width), BF16)],
        [],
        mixed, *mixed_in, qkv, w_out_full, low_own, low_rest, grad_own, grad_rest,
        token_block, cot_rows, vectors,
    )
    grad_out, grad_qv, *qkv_parts = run(
        grad_sum_kernel,
        [((32, width), F32), ((2, 32), F32), near((32 + VEC, qkv_cols), F32)]
        + [near((32 + VEC, qkv_cols), BF16)] * 3,
        [],
        *qkv_sums,
    )
    qkv_parts = with_lines(qkv_parts)
    (grad_in,) = run(join_in_kernel, [((32, feed), F32)], [], *in_parts)
    grad_qkv, grad_gain, grad_shift = run(
        join_qkv_kernel,
        [((32, 3 * width), F32), ((1, 32), F32), ((1, 32), F32)],
        [pltpu.VMEM((VEC, 32), F32)],
        *qkv_parts,
    )
    return (
        layer_out[None],
        grad_tokens[None],
        grad_gain[0],
        grad_shift[0],
        grad_qkv,
        grad_qv,
        grad_out,
        grad_b[0],
        grad_in,
        grad_b_in[0],
        grad_down,
        grad_b[0],
    )


def solution(mesh):
    one_head_each = mesh.shape["ctx"] == HEADS and mesh.shape["fsdp"] == 2
    return jax.shard_map(
        head_body if one_head_each else body,
        mesh=mesh,
        in_specs=(
            P("fsdp", "ctx", None),
            P("ctx", None),
            P("fsdp"),
            P("fsdp"),
            P("fsdp", None),
            P(None, "fsdp"),
            P("fsdp", None),
            P("fsdp"),
            P("fsdp", None),
            P("fsdp"),
            P("fsdp", None),
            P("fsdp"),
            P("fsdp", "ctx", None),
        ),
        out_specs=(
            P("fsdp", "ctx", None),
            P("fsdp", "ctx", None),
            P(("ctx", "fsdp")),
            P(("ctx", "fsdp")),
            P(("ctx", "fsdp"), None),
            P(None, ("ctx", "fsdp")),
            P(("ctx", "fsdp"), None),
            P(("ctx", "fsdp")),
            P(("ctx", "fsdp"), None),
            P(("ctx", "fsdp")),
            P(("ctx", "fsdp"), None),
            P(("ctx", "fsdp")),
        ),
        check_vma=False,
    )
```

```python
from functools import partial
import math

import jax
import jax.numpy as jnp
import numpy as np
from jax import lax
from jax.experimental import pallas as pl
from jax.experimental.pallas import tpu as pltpu
from jax.sharding import PartitionSpec as P

HEADS = 16
HEAD_DIM = 64
ROT = 16


epsilon = 1e-05


def from_behind(block, axis, distance):
    devices = range(lax.axis_size(axis))
    route = [((i - distance) % len(devices), i) for i in devices]
    return lax.ppermute(block, axis, route)


def rotate(vectors, cosine, sine_part):
    half_rot = ROT // 2
    rotary_part = vectors[..., :ROT]
    turned = jnp.concatenate([-rotary_part[..., half_rot:], rotary_part[..., :half_rot]], -1)
    return jnp.concatenate([rotary_part * cosine + turned * sine_part, vectors[..., ROT:]], -1)


def tables(positions):
    freq_index = jnp.arange(ROT // 2, dtype=jnp.float32)
    inverse = 10000.0 ** (-2.0 * freq_index / ROT)
    angles = positions.astype(jnp.float32)[:, None] * inverse[None, :]
    angles = jnp.concatenate([angles, angles], -1)
    return (jnp.cos(angles), jnp.sin(angles))


def spread_positions(orders, half_rows):
    offsets = jnp.arange(half_rows, dtype=jnp.int32)
    return (orders[:, :, None] * half_rows + offsets[None, None, :]).reshape(-1)


def outer_sum(left_side, right_side):
    return lax.dot_general(
        left_side, right_side, (((0,), (0,)), ((), ())), preferred_element_type=jnp.float32
    )


def times_transposed(left_side, right_side):
    return lax.dot_general(
        left_side, right_side, (((1,), (1,)), ((), ())), preferred_element_type=jnp.float32
    )


def attend_block(carried, queries, query_pos, key_rows, value_rows, key_pos, score_scale):
    row_max, row_sum, weighted = carried
    scores = (
        jnp.einsum("qhd,khd->hqk", queries, key_rows, preferred_element_type=jnp.float32)
        * score_scale
    )
    allowed = (query_pos[:, None] >= key_pos[None, :])[None]
    new_max = jnp.maximum(row_max, jnp.max(jnp.where(allowed, scores, -1e30), -1))
    weights = jnp.where(allowed, jnp.exp(scores - new_max[:, :, None]), 0.0)
    rescale = jnp.exp(row_max - new_max)
    row_sum = row_sum * rescale + jnp.sum(weights, -1)
    weighted = weighted * rescale.T[:, :, None] + jnp.einsum(
        "hqk,khd->qhd", weights.astype(jnp.bfloat16), value_rows, preferred_element_type=jnp.float32
    )
    return (new_max, row_sum, weighted)


def block_grads(
    queries, grad_rows, log_sum, delta_rows, query_pos, key_rows, value_rows, key_pos, score_scale
):
    scores = (
        jnp.einsum("qhd,khd->hqk", queries, key_rows, preferred_element_type=jnp.float32)
        * score_scale
    )
    allowed = (query_pos[:, None] >= key_pos[None, :])[None]
    probs = jnp.where(allowed, jnp.exp(scores - log_sum[:, :, None]), 0.0)
    grad_values = jnp.einsum(
        "hqk,qhd->khd", probs.astype(jnp.bfloat16), grad_rows, preferred_element_type=jnp.float32
    )
    grad_probs = jnp.einsum(
        "qhd,khd->hqk", grad_rows, value_rows, preferred_element_type=jnp.float32
    )
    grad_scores = (probs * (grad_probs - delta_rows[:, :, None])).astype(jnp.bfloat16)
    grad_queries = (
        jnp.einsum("hqk,khd->qhd", grad_scores, key_rows, preferred_element_type=jnp.float32)
        * score_scale
    )
    grad_keys = (
        jnp.einsum("hqk,qhd->khd", grad_scores, queries, preferred_element_type=jnp.float32)
        * score_scale
    )
    return (grad_queries, grad_keys, grad_values)


def body(
    tokens,
    block_order,
    ln_gain,
    ln_bias,
    w_qkv,
    qv_bias,
    w_out,
    b_out,
    w_in,
    b_in,
    w_down,
    b_down,
    cotangent,
):
    gathered = (
        lax.all_gather(ln_gain, "fsdp", axis=0, tiled=True),
        lax.all_gather(ln_bias, "fsdp", axis=0, tiled=True),
        lax.all_gather(w_qkv, "fsdp", axis=0, tiled=True),
        lax.all_gather(qv_bias, "fsdp", axis=1, tiled=True),
        lax.all_gather(w_out, "fsdp", axis=0, tiled=True),
        lax.all_gather(b_out, "fsdp", axis=0, tiled=True),
        lax.all_gather(w_in, "fsdp", axis=0, tiled=True),
        lax.all_gather(b_in, "fsdp", axis=0, tiled=True),
        lax.all_gather(w_down, "fsdp", axis=0, tiled=True),
        lax.all_gather(b_down, "fsdp", axis=0, tiled=True),
    )
    (
        gain_full,
        shift_full,
        qkv_full,
        bias_full,
        out_full,
        out_bias,
        in_full,
        in_bias,
        down_full,
        down_bias,
    ) = gathered
    tok_rows = tokens.shape[1]
    model_width = tokens.shape[2]
    half_rows = tok_rows // 2
    score_scale = HEAD_DIM ** (-0.5)
    head_shape = (tok_rows, HEADS, HEAD_DIM)
    flat_shape = (tok_rows, model_width)
    inputs = tokens[0].astype(jnp.float32)
    row_mean = jnp.mean(inputs, -1, keepdims=True)
    centered = inputs - row_mean
    inverse = lax.rsqrt(jnp.mean(centered * centered, -1, keepdims=True) + epsilon)
    normed = centered * inverse
    ln_out = (normed * gain_full.astype(jnp.float32) + shift_full.astype(jnp.float32)).astype(
        jnp.bfloat16
    )
    qkv_pre = jnp.dot(ln_out, qkv_full, preferred_element_type=jnp.float32)
    positions = spread_positions(block_order, half_rows)
    cosine, sine_part = tables(positions)
    cosine = cosine[:, None, :]
    sine_part = sine_part[:, None, :]
    query_pre = qkv_pre[:, :model_width] + bias_full[0].astype(jnp.float32)
    query_rows = rotate(query_pre.reshape(head_shape), cosine, sine_part).astype(jnp.bfloat16)
    key_rows = rotate(
        qkv_pre[:, model_width : 2 * model_width].reshape(head_shape), cosine, sine_part
    ).astype(jnp.bfloat16)
    value_rows = (qkv_pre[:, 2 * model_width :] + bias_full[1].astype(jnp.float32)).astype(
        jnp.bfloat16
    )
    key_flat = key_rows.reshape(flat_shape)
    start_state = (
        jnp.full((HEADS, tok_rows), -1e30, jnp.float32),
        jnp.zeros((HEADS, tok_rows), jnp.float32),
        jnp.zeros(head_shape, jnp.float32),
    )
    carried = start_state
    piece_keys = lax.all_gather(key_flat, "ctx", axis=0, tiled=True)
    piece_values = lax.all_gather(value_rows, "ctx", axis=0, tiled=True)
    piece_orders = lax.all_gather(block_order, "ctx", axis=0, tiled=True)
    shard_count = piece_orders.shape[0]
    group_size = math.gcd(shard_count, max(1, 1024 // tok_rows))
    rounds = shard_count // group_size
    stacked = (
        piece_keys.reshape(rounds, group_size * tok_rows, HEADS, HEAD_DIM),
        piece_values.reshape(rounds, group_size * tok_rows, HEADS, HEAD_DIM),
        piece_orders.reshape(rounds, group_size, 2),
    )

    def one_round(inner_state, block_item):
        key_pos = spread_positions(block_item[2], half_rows)
        return (
            attend_block(
                inner_state,
                query_rows,
                positions,
                block_item[0],
                block_item[1],
                key_pos,
                score_scale,
            ),
            None,
        )

    carried, _ = lax.scan(one_round, carried, stacked)
    row_max, row_sum, weighted = carried
    attended_f32 = weighted / row_sum.T[:, :, None]
    log_sum = row_max + jnp.log(row_sum)
    attended = attended_f32.reshape(flat_shape).astype(jnp.bfloat16)
    branch = jnp.dot(attended, out_full, preferred_element_type=jnp.float32) + out_bias.astype(
        jnp.float32
    )
    hidden = jnp.dot(ln_out, in_full, preferred_element_type=jnp.float32) + in_bias.astype(
        jnp.float32
    )
    active = jax.nn.gelu(hidden, approximate=False).astype(jnp.bfloat16)
    feed_out = jnp.dot(active, down_full, preferred_element_type=jnp.float32) + down_bias.astype(
        jnp.float32
    )
    layer_out = (inputs + branch + feed_out).astype(jnp.bfloat16)[None]
    gain_back, qkv_back, out_back, in_back, down_back = (
        gain_full,
        qkv_full,
        out_full,
        in_full,
        down_full,
    )
    grad_out = cotangent[0]
    grad_f32 = grad_out.astype(jnp.float32)
    grad_attended = times_transposed(grad_out, out_back).astype(jnp.bfloat16).reshape(head_shape)
    grad_active = times_transposed(grad_out, down_back)
    _, gelu_pull = jax.vjp(partial(jax.nn.gelu, approximate=False), hidden)
    grad_hidden = gelu_pull(grad_active)[0].astype(jnp.bfloat16)
    delta_rows = jnp.sum(grad_attended.astype(jnp.float32) * attended_f32, -1).T
    cotangent_sum = jnp.sum(grad_f32, 0)
    term_out_w = outer_sum(attended, grad_out)
    term_in_w = outer_sum(ln_out, grad_hidden)
    term_in_b = jnp.sum(grad_hidden.astype(jnp.float32), 0)
    term_down_w = outer_sum(active, grad_out)
    cycle_size = lax.axis_size("ctx")
    zeros_flat = jnp.zeros(flat_shape, jnp.float32)
    zeros_heads = jnp.zeros(head_shape, jnp.float32)

    def send_home(grad_keys, grad_values):
        return (
            from_behind(grad_keys.astype(jnp.bfloat16), "ctx", 1).astype(grad_keys.dtype),
            from_behind(grad_values.astype(jnp.bfloat16), "ctx", 1).astype(grad_values.dtype),
        )

    def visit_keys(carried):
        visit_key, visit_value, visit_order, grad_keys, grad_values, grad_query = carried
        part_query, part_key, part_value = block_grads(
            query_rows,
            grad_attended,
            log_sum,
            delta_rows,
            positions,
            visit_key.reshape(head_shape),
            visit_value.reshape(head_shape),
            spread_positions(visit_order, half_rows),
            score_scale,
        )
        return (
            grad_keys + part_key.reshape(flat_shape),
            grad_values + part_value.reshape(flat_shape),
            grad_query + part_query,
        )

    def cycle_step(step_index, carried):
        grad_keys, grad_values, grad_query = visit_keys(carried)
        visit_key, visit_value, visit_order = from_behind(
            (carried[0], carried[1], carried[2]), "ctx", 1
        )
        grad_keys, grad_values = send_home(grad_keys, grad_values)
        return (visit_key, visit_value, visit_order, grad_keys, grad_values, grad_query)

    carried = lax.fori_loop(
        0,
        cycle_size - 1,
        cycle_step,
        (key_flat, value_rows, block_order, zeros_flat, zeros_flat, zeros_heads),
    )
    grad_keys, grad_values, grad_query = visit_keys(carried)
    grad_keys, grad_values = send_home(grad_keys, grad_values)
    grad_keys = grad_keys.reshape(head_shape)
    grad_values = grad_values.reshape(head_shape)
    grad_q_pre = rotate(grad_query, cosine, -sine_part).reshape(flat_shape).astype(jnp.bfloat16)
    grad_k_pre = rotate(grad_keys, cosine, -sine_part).reshape(flat_shape).astype(jnp.bfloat16)
    grad_v_pre = grad_values.reshape(flat_shape).astype(jnp.bfloat16)
    grad_qkv = jnp.concatenate([grad_q_pre, grad_k_pre, grad_v_pre], -1)
    grad_ln = times_transposed(grad_qkv, qkv_back) + times_transposed(grad_hidden, in_back)
    grad_normed = grad_ln * gain_back.astype(jnp.float32)
    grad_inputs = inverse * (
        grad_normed
        - jnp.mean(grad_normed, -1, keepdims=True)
        - normed * jnp.mean(grad_normed * normed, -1, keepdims=True)
    )
    grad_tokens = (grad_f32 + grad_inputs).astype(jnp.bfloat16)[None]
    term_gain = jnp.sum(grad_ln * normed, 0)
    term_bias = jnp.sum(grad_ln, 0)
    term_qkv = outer_sum(ln_out, grad_qkv)
    term_qv = jnp.stack(
        [jnp.sum(grad_q_pre.astype(jnp.float32), 0), jnp.sum(grad_v_pre.astype(jnp.float32), 0)], 0
    )
    (
        sum_gain,
        sum_bias,
        sum_qkv,
        sum_qv,
        sum_out_w,
        sum_out_b,
        sum_in_w,
        sum_in_b,
        sum_down_w,
        sum_down_b,
    ) = (
        lax.psum_scatter(term_gain, ("ctx", "fsdp"), scatter_dimension=0, tiled=True),
        lax.psum_scatter(term_bias, ("ctx", "fsdp"), scatter_dimension=0, tiled=True),
        lax.psum_scatter(term_qkv, ("ctx", "fsdp"), scatter_dimension=0, tiled=True),
        lax.psum_scatter(term_qv, ("ctx", "fsdp"), scatter_dimension=1, tiled=True),
        lax.psum_scatter(term_out_w, ("ctx", "fsdp"), scatter_dimension=0, tiled=True),
        lax.psum_scatter(cotangent_sum, ("ctx", "fsdp"), scatter_dimension=0, tiled=True),
        lax.psum_scatter(term_in_w, ("ctx", "fsdp"), scatter_dimension=0, tiled=True),
        lax.psum_scatter(term_in_b, ("ctx", "fsdp"), scatter_dimension=0, tiled=True),
        lax.psum_scatter(term_down_w, ("ctx", "fsdp"), scatter_dimension=0, tiled=True),
        lax.psum_scatter(cotangent_sum, ("ctx", "fsdp"), scatter_dimension=0, tiled=True),
    )
    return (
        layer_out,
        grad_tokens,
        sum_gain,
        sum_bias,
        sum_qkv,
        sum_qv,
        sum_out_w,
        sum_out_b,
        sum_in_w,
        sum_in_b,
        sum_down_w,
        sum_down_b,
    )


LINES = 4
ACROSS = HEADS // LINES
F32 = jnp.float32
BF16 = jnp.bfloat16
VMEM_LIMIT = 16 * 1024 * 1024
TIMES = {'hold': 5000, 'feed_grad': 40, 'halve': 400, 'unpack': 150, 'feed_sum': 150, 'feed_terms': 5, 'share_twin': 400, 'join_in': 5, 'attend': 20, 'grads': 40}

VEC = 16


def dot(left, right):
    return jnp.dot(left, right, preferred_element_type=F32)


def dot_nt(left, right):
    return lax.dot_general(left, right, (((1,), (1,)), ((), ())), preferred_element_type=F32)


class Far(tuple):
    pass


class Near(tuple):
    pass


def far(*x):
    return Far(x)


def near(*x):
    return Near(x)


def raw(x):
    return x[0] if isinstance(x, (Far, Near)) else x


def placed(x):
    if isinstance(x, Far):
        return pltpu.with_memory_space_constraint(x[0], pltpu.HBM)
    if isinstance(x, Near):
        return pltpu.with_memory_space_constraint(x[0], pltpu.VMEM)
    return x


def spot():
    context = lax.axis_index("ctx")
    return context // ACROSS, context % ACROSS, lax.axis_index("fsdp")


def call(kernel, out_shapes, scratch, *operands, after=(), loose_in=0):
    whole = pl.BlockSpec(memory_space=pltpu.VMEM)
    loose = pl.BlockSpec(memory_space=pl.ANY)
    arrays, specs = [], []
    for x in operands:
        arrays.append(placed(x))
        if arrays[-1].dtype == jnp.int32 and arrays[-1].ndim == 1:
            specs.append(pl.BlockSpec(memory_space=pltpu.SMEM))
        else:
            specs.append(loose if len(specs) < loose_in else whole)
    outs = []
    for shape in out_shapes:
        if isinstance(shape, Far):
            outs.append(pltpu.HBM(*shape))
        elif isinstance(shape, Near):
            outs.append(pltpu.VMEM(*shape))
        else:
            outs.append(jax.ShapeDtypeStruct(*shape))
    count = len(arrays)

    def body(*refs):
        kernel(*refs[:count], *refs[count + len(after) :])

    name = kernel.__name__.removesuffix("_kernel")
    results = pl.pallas_call(
        body,
        name=name,
        out_shape=outs,
        in_specs=specs + [loose] * len(after),
        out_specs=[whole for _ in outs],
        scratch_shapes=scratch,
        compiler_params=pltpu.CompilerParams(vmem_limit_bytes=VMEM_LIMIT),
        cost_estimate=pl.CostEstimate(
            flops=TIMES.get(name, 0) * 115_000_000, bytes_accessed=0, transcendentals=0
        ),
    )(*arrays, *map(placed, after))
    return [
        near(x) if isinstance(shape, Near) else x for x, shape in zip(results, out_shapes)
    ]


def run_copies(pairs, sems):
    copies = [pltpu.make_async_copy(x, y, sems.at[i]) for i, (x, y) in enumerate(pairs)]
    for copy in copies:
        copy.start()
    for copy in copies:
        copy.wait()


def prepare_kernel(qkv, w_in, w_out, w_down, gain, shift, b_out, b_down, qv, b_in, packed, sems):
    line, _, _ = spot()
    feed = w_in.shape[1] // LINES
    half, width = w_out.shape
    part = line % (LINES // 2)
    row = 0
    pairs = []
    sources = [
        w_in.at[:, pl.ds(pl.multiple_of(feed * line, 128), feed)],
        w_out,
        w_down.at[pl.ds(pl.multiple_of(feed * part, 16), feed), :],
    ]
    for source in sources + [qkv.at[:, width * i : width * (i + 1)] for i in range(3)]:
        pairs.append((source, packed.at[row : row + source.shape[0], :]))
        row += source.shape[0]
    rows = [x[...].astype(F32).reshape(1, half) for x in (gain, shift, b_out, b_down)]
    rows += [qv[...].astype(F32), b_in[...].astype(F32).reshape(4, half)]
    rows.append(jnp.zeros((VEC - 10, half), F32))
    packed[row : row + VEC, :half] = jnp.concatenate(rows, 0).astype(BF16)
    run_copies(pairs, sems)


def assemble_kernel(own, twin, qkv, w_in, w_out, w_down, vectors, low, sems):
    line, _, core = spot()
    width = w_out.shape[1]
    half = width // 2
    feed = w_down.shape[0]
    down_row = 2 * half
    qkv_row = down_row + feed
    vec_row = qkv_row + 3 * half
    pairs = []
    for source, side in ((own, core), (twin, 1 - core)):
        rows = pl.ds(pl.multiple_of(half * side, half), half)
        pairs.append((source.at[:half, :], w_in.at[rows, :]))
        pairs.append((source.at[half:down_row, :], w_out.at[rows, :]))
        for i in range(3):
            base = qkv_row + half * i
            pairs.append(
                (source.at[base : base + half, :], qkv.at[rows, width * i : width * (i + 1)])
            )
        spare = pl.ds(pl.multiple_of(VEC * side, VEC), VEC)
        pairs.append((source.at[vec_row:, :half], low.at[spare, :]))
    holds = core == line // (LINES // 2)

    @pl.when(holds)
    def _():
        run_copies(pairs + [(own.at[down_row:qkv_row, :], w_down)], sems)

    @pl.when(jnp.logical_not(holds))
    def _():
        run_copies(pairs + [(twin.at[down_row:qkv_row, :], w_down)], sems)

    vectors[...] = low[...].astype(F32)


def line_columns(qkv, part):
    line, _, _ = spot()
    width = qkv.shape[1] // 3
    base = width * part + width // LINES * line
    return qkv[:, pl.ds(pl.multiple_of(base, 128), width // LINES)]


def line_rows_of(w_out):
    line, _, _ = spot()
    count = w_out.shape[0] // LINES
    return w_out[pl.ds(pl.multiple_of(count * line, 16), count), :]


def full_row(vectors, index):
    return jnp.concatenate(
        [vectors[index : index + 1, :], vectors[VEC + index : VEC + index + 1, :]], 1
    )


def pack_kernel(order, tokens, packed):
    rows = tokens.shape[0]
    packed[:rows, :] = tokens[...]
    lane = lax.broadcasted_iota(jnp.int32, (VEC, 128), 1)
    numbers = jnp.where(lane == 0, order[0], jnp.where(lane == 1, order[1], 0))
    packed[rows:, :128] = numbers.astype(F32).astype(BF16)
    packed[rows:, 128:] = jnp.zeros((VEC, tokens.shape[1] - 128), BF16)


def reorder(chunks, place):
    upper, lower = chunks
    turned = (place & 2) != 0
    near_by = (place & 1) != 0
    first = jnp.where(turned, lower, upper)
    second = jnp.where(turned, upper, lower)
    first = jnp.where(near_by, pltpu.roll(first, 64, 1), first)
    second = jnp.where(near_by, pltpu.roll(second, 64, 1), second)
    return first, second


def left_lanes(rows):
    return lax.broadcasted_iota(jnp.int32, (rows, 128), 1) < 64


def pair_heads(one, two, slot):
    keep = left_lanes(one.shape[0])
    if slot % 2 == 0:
        return jnp.where(keep, one, pltpu.roll(two, 64, 1))
    return jnp.where(keep, pltpu.roll(one, 64, 1), two)


def fold_rows(chunk, slot):
    rows = chunk.shape[0] // 2
    return pair_heads(chunk[:rows], chunk[rows:], slot)


def unfold_pair(even, odd):
    keep = left_lanes(even.shape[0])
    top = jnp.where(keep, even, pltpu.roll(odd, 64, 1))
    bottom = jnp.where(keep, pltpu.roll(even, 64, 1), odd)
    return jnp.concatenate([top, bottom], 0)


def normalise(rows):
    x = rows.astype(F32)
    centred = x - jnp.mean(x, -1, keepdims=True)
    inverse = lax.rsqrt(jnp.mean(centred * centred, -1, keepdims=True) + epsilon)
    return centred * inverse, inverse


def two_chunks(x):
    return x[:, :128], x[:, 128:256]


def two_chunks(x):
    return x[:, :128], x[:, 128:256]


def project_kernel(t0, t1, t2, t3, vectors, qkv, s0, s1, s2, s3, ln_ref, lnt_ref, normed_ref):
    line, place, _ = spot()
    rows = t0.shape[0] - VEC
    gain, shift = full_row(vectors, 0), full_row(vectors, 1)
    numbers = jnp.zeros((VEC, 128), F32)
    for k, ref in enumerate((t0, t1, t2, t3)):
        source = line ^ k
        part = pl.ds(pl.multiple_of(rows * source, rows), rows)
        normed, _ = normalise(ref[:rows, :])
        normed_ref[part, :] = normed
        ln_ref[part, :] = (normed * gain + shift).astype(BF16)
        numbers = numbers + pltpu.roll(ref[rows:, :128].astype(F32), 2 * source, 1)
    side = VEC * (line // (LINES // 2))
    lanes = pl.ds(pl.multiple_of(256 * (line % (LINES // 2)), 256), 256)
    bias_q = vectors[pl.ds(side + 4, 1), lanes]
    bias_v = vectors[pl.ds(side + 5, 1), lanes]
    q_chunks = reorder(two_chunks(dot(ln_ref[...], line_columns(qkv, 0)) + bias_q), place)
    k_chunks = reorder(two_chunks(dot(ln_ref[...], line_columns(qkv, 1))), place)
    v_chunks = reorder(two_chunks(dot(ln_ref[...], line_columns(qkv, 2)) + bias_v), place)
    total = ln_ref.shape[0]
    end = total * 3 // 2
    for slot, ref in enumerate((s0, s1, s2, s3)):
        pair = slot // 2
        ref[:total, :] = pair_heads(q_chunks[pair], k_chunks[pair], slot).astype(BF16)
        ref[total:end, :] = fold_rows(v_chunks[pair], slot).astype(BF16)
        ref[end:, :] = numbers.astype(BF16)
    lnt_ref[...] = ln_ref[...].T


def back_rows_kernel(c0, c1, c2, c3, w_out, s0, s1, s2, s3, cot):
    line, place, _ = spot()
    rows = c0.shape[0]
    for k, ref in enumerate((c0, c1, c2, c3)):
        cot[pl.ds(pl.multiple_of(rows * (line ^ k), rows), rows), :] = ref[...]
    chunks = reorder(two_chunks(dot_nt(cot[...], line_rows_of(w_out))), place)
    for slot, ref in enumerate((s0, s1, s2, s3)):
        ref[...] = fold_rows(chunks[slot // 2], slot).astype(BF16)


def block_rows(table):
    for j in range(4):
        for i in range(8):
            yield j, i, pl.ds(pl.multiple_of(table[8 * j, i] * 64, 64), 64)


def sort_rows(table, slots, target, base, folded):
    for j, i, dest in block_rows(table):
        if folded:
            start = base + 64 * (i % 4)
            lanes = slice(0, 64) if i < 4 else slice(64, 128)
            target[dest, :] = slots[j][start : start + 64, lanes]
        else:
            target[dest, :] = slots[j][base + 64 * i : base + 64 * (i + 1), :]


def turn(x, cosine, sine):
    lane = lax.broadcasted_iota(jnp.int32, x.shape, 1) & (HEAD_DIM - 1)
    other = jnp.where(lane < ROT // 2, pltpu.roll(x, 120, 1), pltpu.roll(x, 8, 1))
    return x * cosine + other * sine


TILE = 256


def scores_of(qk_ref, i):
    rows = slice(TILE * i, TILE * (i + 1))
    queries = jnp.where(left_lanes(TILE), qk_ref[rows, :], jnp.zeros((), BF16))
    queries = queries * jnp.asarray(HEAD_DIM ** (-0.5), BF16)
    return queries


def allowed_tile():
    row = lax.broadcasted_iota(jnp.int32, (TILE, TILE), 0)
    col = lax.broadcasted_iota(jnp.int32, (TILE, TILE), 1)
    return row >= col


def attend_kernel(r0, r1, r2, r3, cosine, sine, *rest):
    qk_ref, kq_ref, v_ref, att_ref, lse_ref, table_ref, raw, table, sem = rest
    refs = (r0, r1, r2, r3)
    count = qk_ref.shape[0]
    lines = count // 4
    for j, ref in enumerate(refs):
        numbers = ref[lines * 3 // 2 :, :].astype(F32)[:8, :]
        table_ref[8 * j : 8 * (j + 1), :] = numbers.astype(jnp.int32)
    run_copies([(table_ref, table)], sem)
    sort_rows(table, refs, raw, 0, False)
    sort_rows(table, refs, v_ref, lines, True)
    for i in range(count // TILE):
        rows = slice(TILE * i, TILE * (i + 1))
        turned = turn(raw[rows, :].astype(F32), cosine[rows, :], sine[rows, :])
        qk_ref[rows, :] = turned.astype(BF16)
        kq_ref[rows, :] = pltpu.roll(turned, 64, 1).astype(BF16)
    mask = allowed_tile()
    for i in range(count // TILE):
        rows = slice(TILE * i, TILE * (i + 1))
        keys = TILE * (i + 1)
        scores = dot_nt(scores_of(qk_ref, i), kq_ref[:keys, :])
        last = jnp.where(mask, scores[:, keys - TILE :], -1e30)
        scores = last if i == 0 else jnp.concatenate([scores[:, : keys - TILE], last], 1)
        top = jnp.max(scores, -1, keepdims=True)
        weights = jnp.exp(scores - top)
        total = jnp.sum(weights, -1, keepdims=True)
        weighted = dot(weights.astype(BF16), v_ref[:keys, :])
        att_ref[rows, :] = weighted / total
        lse_ref[rows, :] = top + jnp.log(total)


def attend_back_kernel(r0, r1, r2, r3, table_ref, qk_ref, kq_ref, v_ref, att_ref, *rest):
    lse_ref, cosine, sine, o0, o1, o2, o3, sums, ga_ref, kt_ref, vt_ref, gqk, gv = rest[:13]
    table, sem = rest[13:]
    refs = (r0, r1, r2, r3)
    count = qk_ref.shape[0]
    lines = count // 4
    run_copies([(table_ref, table)], sem)
    sort_rows(table, refs, ga_ref, 0, True)
    mask = allowed_tile()
    kt_ref[...] = jnp.zeros_like(kt_ref)
    vt_ref[...] = jnp.zeros_like(vt_ref)
    for i in range(count // TILE):
        rows = slice(TILE * i, TILE * (i + 1))
        keys = TILE * (i + 1)
        queries = scores_of(qk_ref, i)
        scores = dot_nt(queries, kq_ref[:keys, :])
        last = jnp.where(mask, scores[:, keys - TILE :], -1e30)
        scores = last if i == 0 else jnp.concatenate([scores[:, : keys - TILE], last], 1)
        probs = jnp.exp(scores - lse_ref[rows, :])
        grad_rows = ga_ref[rows, :]
        delta = jnp.sum(grad_rows.astype(F32) * att_ref[rows, :], -1, keepdims=True)
        grad_probs = dot_nt(grad_rows, v_ref[:keys, :])
        grad_scores = (probs * (grad_probs - delta)).astype(BF16)
        gqk[rows, :] = dot(grad_scores, kq_ref[:keys, :]) * HEAD_DIM ** (-0.5)
        vt_ref[:, :keys] += dot(grad_rows.astype(F32).T.astype(BF16), probs.astype(BF16))
        kt_ref[:, :keys] += dot(queries.astype(F32).T.astype(BF16), grad_scores)
    sum_q = jnp.zeros((1, 128), F32)
    sum_v = jnp.zeros((1, 64), F32)
    for i in range(count // TILE):
        rows = slice(TILE * i, TILE * (i + 1))
        grad_keys = pltpu.roll(kt_ref[:, rows].T, 64, 1)
        both = jnp.where(left_lanes(TILE), gqk[rows, :], grad_keys)
        both = turn(both, cosine[rows, :], -sine[rows, :])
        both = both.astype(BF16).astype(F32)
        values = vt_ref[:, rows].T.astype(BF16).astype(F32)
        gqk[rows, :] = both
        gv[rows, :] = values
        sum_q = sum_q + jnp.sum(both, 0, keepdims=True)
        sum_v = sum_v + jnp.sum(values, 0, keepdims=True)
    sums[...] = jnp.zeros_like(sums)
    sums[0:1, :64] = sum_q[:, :64]
    sums[1:2, :64] = sum_v
    outs = (o0, o1, o2, o3)
    for j, i, source in block_rows(table):
        lanes = slice(0, 64) if i < 4 else slice(64, 128)
        outs[j][64 * i : 64 * (i + 1), :] = gqk[source, :].astype(BF16)
        start = lines + 64 * (i % 4)
        outs[j][start : start + 64, lanes] = gv[source, :].astype(BF16)
        start += lines // 2
        outs[j][start : start + 64, lanes] = att_ref[source, :].astype(BF16)


def split_lines(low, keep, send):
    line, _, _ = spot()
    rows = low.shape[0] // LINES
    for k, (ref, base) in enumerate(((keep, 0), (send, 0), (keep, rows), (send, rows))):
        part = pl.ds(pl.multiple_of(rows * (line ^ k), rows), rows)
        ref[base : base + rows, :] = low[part, :].astype(ref.dtype)


def feed_kernel(ln, w_in, vectors, w_down, hidden_ref, actt_ref, keep, send, act_ref, low_ref):
    line, _, _ = spot()
    row = VEC * (line // (LINES // 2)) + 6 + 2 * (line % (LINES // 2))
    bias = jnp.concatenate([vectors[pl.ds(row, 1), :], vectors[pl.ds(row + 1, 1), :]], 1)
    for f in range(4):
        cols = slice(256 * f, 256 * (f + 1))
        hidden = dot(ln[...], w_in[:, cols]) + bias[:, cols]
        hidden_ref[:, cols] = hidden
        active = 0.5 * hidden * (1.0 + lax.erf(hidden * 0.7071067811865476))
        act_ref[:, cols] = active.astype(BF16)
        actt_ref[cols, :] = active.astype(BF16).T
    for f in range(4):
        cols = slice(256 * f, 256 * (f + 1))
        low_ref[:, cols] = dot(act_ref[...], w_down[:, cols])
    split_lines(low_ref, keep, send)


def feed_grad_kernel(cot, hidden, w_in, w_down, gh_ref, sums, low_ref, keep, send):
    for f in range(4):
        cols = slice(256 * f, 256 * (f + 1))
        grad_active = dot_nt(cot[...], w_down[cols, :])
        h = hidden[:, cols]
        slope = 0.5 * (1.0 + lax.erf(h * 0.7071067811865476)) + h * jnp.exp(
            -0.5 * h * h
        ) * 0.3989422804014327
        grad_hidden = (slope * grad_active).astype(BF16)
        gh_ref[:, cols] = grad_hidden
        total = jnp.sum(grad_hidden.astype(F32), 0, keepdims=True)
        sums[:, cols] = jnp.broadcast_to(total, (8, 256))
    for i in range(4):
        low_ref[:, 256 * i : 256 * (i + 1)] = dot_nt(gh_ref[...], w_in[256 * i : 256 * (i + 1), :])
    split_lines(low_ref, keep, send)


def feed_terms_kernel(cot_ref, actt, lnt, gh, sums, send, keep, chunk_ref):
    line, _, core = spot()
    cot = cot_ref[...]
    block = send.shape[0] // 4
    for f in range(4):
        chunk_ref[...] = dot(actt[256 * f : 256 * (f + 1), :], cot)
        base = block * f
        send[base : base + 128, :] = chunk_ref[
            pl.ds(pl.multiple_of((1 - core) * 128, 128), 128), :
        ].astype(BF16)
        keep[base : base + 128, :] = chunk_ref[pl.ds(pl.multiple_of(core * 128, 128), 128), :]
    for z in range(4):
        chunk_ref[...] = dot(lnt[256 * z : 256 * (z + 1), :], gh[...])
        for f in range(4):
            base = block * f + 128 + 32 * z
            send[base : base + 32, :] = chunk_ref[
                pl.ds(pl.multiple_of(64 * f + 32 * (1 - core), 32), 32), :
            ].astype(BF16)
            keep[base : base + 32, :] = chunk_ref[
                pl.ds(pl.multiple_of(64 * f + 32 * core, 32), 32), :
            ]
    cot_sum = jnp.sum(cot.astype(F32), 0, keepdims=True)
    picked = jnp.where(
        line < 2,
        jnp.where(line == 0, cot_sum[:, 0:256], cot_sum[:, 256:512]),
        jnp.where(line == 2, cot_sum[:, 512:768], cot_sum[:, 768:1024]),
    )
    zero = jnp.zeros((1, 640), F32)
    for f in range(4):
        even, odd = sums[:1, 256 * f : 256 * f + 128], sums[:1, 256 * f + 128 : 256 * f + 256]
        first = core == 0
        base = block * f + 256
        given = jnp.concatenate([jnp.where(first, odd, even), picked, zero], 1)
        kept = jnp.concatenate([jnp.where(first, even, odd), picked, zero], 1)
        send[base : base + VEC, :] = jnp.broadcast_to(given, (VEC, 1024)).astype(BF16)
        keep[base : base + VEC, :] = jnp.broadcast_to(kept, (VEC, 1024))


def share_twin_kernel(keep, received, o0, o1, o2, o3):
    _, place, _ = spot()
    block = o0.shape[0]
    for slot, ref in enumerate((o0, o1, o2, o3)):
        rows = pl.ds(pl.multiple_of((place ^ slot) * block, 16), block)
        ref[...] = (keep[rows, :] + received[rows, :].astype(F32)).astype(ref.dtype)


def adder(own, r1, r2, r3):
    def total(rows, cols=slice(None)):
        return (own[rows, cols].astype(F32) + r1[rows, cols].astype(F32)) + (
            r2[rows, cols].astype(F32) + r3[rows, cols].astype(F32)
        )

    return total


def owned_lanes(rows):
    _, place, core = spot()
    return pltpu.roll(rows, lax.rem(256 - (64 * place + 32 * core), 256), 1)[:, :32]


def feed_sum_kernel(own, r1, r2, r3, down_ref, bias_in, bias_out, i0, i1, i2, i3):
    line, _, _ = spot()
    total = adder(own, r1, r2, r3)
    down_ref[...] = total(slice(0, 128))
    bias_in[...] = total(slice(256, 264), slice(0, 128))[:1]
    bias_out[...] = owned_lanes(total(slice(256, 264), slice(128, 384)))[:1]
    for slot, ref in enumerate((i0, i1, i2, i3)):
        rows = pl.ds(pl.multiple_of(128 + 32 * (line ^ slot), 32), 32)
        ref[...] = total(rows).astype(ref.dtype)


def halve_kernel(keep, received, own, send):
    rows = own.shape[0]
    own[...] = keep[:rows, :] + received[:rows, :].astype(F32)
    send[...] = (keep[rows:, :] + received[rows:, :].astype(F32)).astype(BF16)


def unpack_kernel(r0, r1, r2, r3, mixed, att_t, s1, s2, s3):
    line, place, _ = spot()
    rows = s1.shape[0]
    total = LINES * rows
    fold = total // 2
    parts = [ref[...].astype(F32) for ref in (r0, r1, r2, r3)]
    keep_left = left_lanes(total)
    chunks = [[], [], [], []]
    for pair in range(2):
        one, two = parts[2 * pair], parts[2 * pair + 1]
        even, odd = one[:total], two[:total]
        values, attended = slice(total, total + fold), slice(total + fold, total + 2 * fold)
        chunks[0].append(unfold_pair(one[attended], two[attended]))
        chunks[1].append(jnp.where(keep_left, even, pltpu.roll(odd, 64, 1)))
        chunks[2].append(jnp.where(keep_left, pltpu.roll(even, 64, 1), odd))
        chunks[3].append(unfold_pair(one[values], two[values]))
    for index, both in enumerate(chunks):
        for pair, chunk in enumerate(reorder(both, place)):
            base = 256 * index + 128 * pair
            mixed[:, base : base + 128] = chunk.astype(BF16)
    for k, ref in ((1, s1), (2, s2), (3, s3)):
        ref[...] = mixed[pl.ds(pl.multiple_of(rows * (line ^ k), rows), rows), :]
    att_t[...] = mixed[:, :256].T


def grads_kernel(mixed, low, normed, lnt, qkv, att_t, cot, head_sums, *rest):
    send, keep, low_ref, chunk_ref, out_ref = rest
    _, place, core = spot()
    low_ref[...] = low[...]
    for i in range(3):
        cols = slice(256 * (i + 1), 256 * (i + 2))
        low_ref[...] += dot_nt(mixed[:, cols], line_columns(qkv, i))
    grad = low_ref[...]
    sum_gain = jnp.sum(grad * normed[...], 0, keepdims=True)
    sum_bias = jnp.sum(grad, 0, keepdims=True)
    block = send.shape[0] // 4
    for z in range(4):
        chunk_ref[...] = dot(lnt[256 * z : 256 * (z + 1), :], mixed[:, 256:])
        for f in range(4):
            base = block * f + 32 * z
            send[base : base + 32, :] = chunk_ref[
                pl.ds(pl.multiple_of(64 * f + 32 * (1 - core), 32), 32), :
            ].astype(BF16)
            keep[base : base + 32, :] = chunk_ref[
                pl.ds(pl.multiple_of(64 * f + 32 * core, 32), 32), :
            ]
    out_ref[...] = dot(att_t[...], cot[...])
    sums = [sum_gain[:, 256 * i : 256 * (i + 1)] for i in range(4)]
    sums += [sum_bias[:, 256 * i : 256 * (i + 1)] for i in range(4)]
    spare = jnp.concatenate([head_sums[...], jnp.zeros((8, 128), F32)], 1)
    for f in range(4):
        base = block * f + 128
        vec = jnp.concatenate(sums + [jnp.where(place == f, spare, 0.0)], 0)
        for ref, side in ((send, 1 - core), (keep, core)):
            rows = out_ref[pl.ds(pl.multiple_of(64 * f + 32 * side, 32), 32), :]
            tail = jnp.concatenate([rows[:16, 768:], rows[16:, 768:], vec], 1)
            ref[base : base + 32, :] = rows[:, :768].astype(ref.dtype)
            ref[base + 32 : base + 48, :] = tail.astype(ref.dtype)


def grad_sum_kernel(own, r1, r2, r3, grad_out, qv, i0, i1, i2, i3):
    line, _, core = spot()
    total = adder(own, r1, r2, r3)
    tail = total(slice(160, 176))
    grad_out[:, :768] = total(slice(128, 160))
    grad_out[:16, 768:] = tail[:, :256]
    grad_out[16:, 768:] = tail[:, 256:512]
    qv[...] = jnp.where(core == 0, tail[8:10, 512:544], tail[8:10, 544:576])
    for slot, ref in enumerate((i0, i1, i2, i3)):
        rows = pl.ds(pl.multiple_of(32 * (line ^ slot), 32), 32)
        ref[:32, :] = total(rows).astype(ref.dtype)
        ref[32:, :] = tail.astype(ref.dtype)


def join_in_kernel(i0, i1, i2, i3, out):
    line, _, _ = spot()
    for slot, ref in enumerate((i0, i1, i2, i3)):
        cols = pl.ds(pl.multiple_of((line ^ slot) * 1024, 1024), 1024)
        out[:, cols] = ref[...].astype(F32)


def join_qkv_kernel(i0, i1, i2, i3, out, gain, bias, vec_ref):
    line, _, _ = spot()
    vec = jnp.zeros((VEC, 256), F32)
    for slot, ref in enumerate((i0, i1, i2, i3)):
        for part in range(3):
            cols = pl.ds(pl.multiple_of(1024 * part + (line ^ slot) * 256, 256), 256)
            out[:, cols] = ref[:32, 256 * part : 256 * (part + 1)].astype(F32)
        vec = vec + ref[32:, 512:768].astype(F32)
    vec_ref[...] = owned_lanes(vec)
    gain[...] = vec_ref[pl.ds(line, 1), :]
    bias[...] = vec_ref[pl.ds(4 + line, 1), :]


def hold_kernel(x, out):
    out[...] = x[...]


def tokens_kernel(mixed, r1, r2, r3, qkv, w_out, *rest):
    low, low_rest, grad, grad_rest, tokens, cot, vectors, layer_out, grad_tokens = rest
    line, _, _ = spot()
    rows = low.shape[0]
    mine = pl.ds(pl.multiple_of(rows * line, rows), rows)
    branch = low[...] + low_rest[...].astype(F32)
    grad_ln = grad[...] + grad_rest[...].astype(F32)
    for k, ref in enumerate((mixed.at[mine, :], r1, r2, r3)):
        base = 256 * (line ^ k)
        part = pl.ds(pl.multiple_of(base, 256), 256)
        branch = branch + dot(ref[:, :256], w_out[part, :])
        for i in range(3):
            part = pl.ds(pl.multiple_of(base + 1024 * i, 256), 256)
            grad_ln = grad_ln + dot_nt(ref[:, 256 * (i + 1) : 256 * (i + 2)], qkv[:, part])
    own = tokens[:rows, :]
    branch = branch + own.astype(F32)
    layer_out[...] = (branch + full_row(vectors, 2) + full_row(vectors, 3)).astype(BF16)
    normed, inverse = normalise(own)
    g = grad_ln * full_row(vectors, 0)
    back = inverse * (
        g - jnp.mean(g, -1, keepdims=True) - normed * jnp.mean(g * normed, -1, keepdims=True)
    )
    grad_tokens[...] = (cot[mine, :].astype(F32) + back).astype(BF16)


def turn_tables(count):
    half_rot = ROT // 2
    inverse = 10000.0 ** (-2.0 * np.arange(half_rot) / ROT)
    angles = np.arange(count)[:, None] * inverse[None, :]
    cosine = np.ones((count, HEAD_DIM), np.float32)
    sine = np.zeros((count, HEAD_DIM), np.float32)
    cosine[:, :half_rot] = cosine[:, half_rot:ROT] = np.cos(angles)
    sine[:, :half_rot] = -np.sin(angles)
    sine[:, half_rot:ROT] = np.sin(angles)
    return tuple(np.concatenate([t, t], -1) for t in (cosine, sine))


def head_body(
    tokens,
    block_order,
    ln_gain,
    ln_bias,
    w_qkv,
    qv_bias,
    w_out,
    b_out,
    w_in,
    b_in,
    w_down,
    b_down,
    cotangent,
):
    positions = range(LINES * ACROSS)

    def over_lines(x, k):
        return lax.ppermute(x, "ctx", [(i, i ^ (k * ACROSS)) for i in positions])

    def over_places(x, j):
        return lax.ppermute(x, "ctx", [(i, i ^ j) for i in positions])

    def twin(x):
        return near(lax.ppermute(raw(x), "fsdp", [(0, 1), (1, 0)]))

    def with_lines(blocks):
        return [blocks[0]] + [near(over_lines(raw(blocks[k]), k)) for k in range(1, LINES)]

    def with_places(blocks):
        return [blocks[0]] + [near(over_places(raw(blocks[j]), j)) for j in range(1, ACROSS)]

    rows, width = tokens.shape[1], tokens.shape[2]
    half = w_qkv.shape[0]
    feed = w_in.shape[1]
    head_cols = width // LINES
    feed_cols = feed // LINES
    qkv_cols = 3 * head_cols
    length = rows * LINES * ACROSS
    line_rows = rows * LINES
    slot_rows = line_rows * 3 // 2
    rotation = turn_tables(length)
    packed_rows = 5 * half + feed_cols + VEC
    table = pltpu.SMEM((32, 128), jnp.int32)
    one_copy = pltpu.SemaphoreType.DMA((1,))
    block = 128 + 128 + VEC
    qkv_block = 128 + 32 + VEC

    last = []

    def run(kernel, out_shapes, scratch, *operands, after=(), loose_in=0):
        results = call(
            kernel, out_shapes, scratch, *operands, after=(*after, *last), loose_in=loose_in
        )
        last[:] = [far(results[0])] if isinstance(out_shapes[0], Far) else results[:1]
        return results
    (token_block,) = run(
        pack_kernel,
        [near((rows + VEC, width), BF16)],
        [],
        block_order.reshape(2), far(tokens[0]),
    )
    from_two = over_lines(raw(token_block), 2)
    token_lines = [
        token_block,
        near(over_lines(raw(token_block), 1)),
        near(from_two),
        near(over_lines(from_two, 1)),
    ]
    (packed,) = run(
        prepare_kernel,
        [near((packed_rows, width), BF16)],
        [pltpu.SemaphoreType.DMA((6,))],
        far(w_qkv), far(w_in), far(w_out), far(w_down),
        *map(far, (ln_gain, ln_bias, b_out, b_down, qv_bias, b_in)),
        loose_in=4,
    )
    (cot_own,) = run(
        hold_kernel,
        [near((rows, width), BF16)],
        [],
        far(cotangent[0]),
        after=token_lines[1:3],
    )
    cot_two = over_lines(raw(cot_own), 2)
    cot_lines = [
        cot_own,
        near(over_lines(raw(cot_own), 1)),
        near(cot_two),
        near(over_lines(cot_two, 1)),
    ]
    qkv, in_rows, w_out_full, down_rows, vectors = run(
        assemble_kernel,
        [
            near((width, 3 * width), BF16),
            near((width, feed_cols), BF16),
            near((width, width), BF16),
            near((feed_cols, width), BF16),
            near((2 * VEC, half), F32),
        ],
        [pltpu.VMEM((2 * VEC, half), BF16), pltpu.SemaphoreType.DMA((13,))],
        packed, twin(packed),
        loose_in=2,
    )
    *slots, ln_low, ln_turned, normed = run(
        project_kernel,
        [near((slot_rows + VEC, 128), BF16)] * 4
        + [
            near((line_rows, width), BF16),
            near((width, line_rows), BF16),
            near((line_rows, width), F32),
        ],
        [],
        *token_lines, vectors, qkv,
    )
    slots_in = with_places(slots)
    hidden, active_turned, low_keep, low_send = run(
        feed_kernel,
        [
            near((line_rows, feed_cols), F32),
            near((feed_cols, line_rows), BF16),
            near((2 * rows, width), F32),
            near((2 * rows, width), BF16),
        ],
        [pltpu.VMEM((line_rows, feed_cols), BF16), pltpu.VMEM((line_rows, width), F32)],
        ln_low, in_rows, vectors, down_rows,
    )
    low_received = near(over_lines(raw(low_send), 1))
    qk_rows, kq_rows, value_rows, attended, lse, numbers = run(
        attend_kernel,
        [
            near((length, 128), BF16),
            near((length, 128), BF16),
            near((length, 64), BF16),
            near((length, 64), F32),
            near((length, 1), F32),
            near((32, 128), jnp.int32),
        ],
        [pltpu.VMEM((length, 128), BF16), table, one_copy],
        *slots_in, *rotation,
    )
    *back_slots, cot_rows = run(
        back_rows_kernel,
        [near((line_rows // 2, 128), BF16)] * 4 + [near((line_rows, width), BF16)],
        [],
        *cot_lines, w_out_full,
    )
    back_in = with_places(back_slots)
    grad_hidden, hidden_sums, feed_grad_low, grad_keep, grad_send = run(
        feed_grad_kernel,
        [
            near((line_rows, feed_cols), BF16),
            near((8, feed_cols), F32),
            near((line_rows, width), F32),
            near((2 * rows, width), F32),
            near((2 * rows, width), BF16),
        ],
        [],
        cot_rows, hidden, in_rows, down_rows,
    )
    grad_received = near(over_lines(raw(grad_send), 1))
    feed_send, feed_keep = run(
        feed_terms_kernel,
        [near((4 * block, width), BF16), near((4 * block, width), F32)],
        [pltpu.VMEM((256, 1024), F32)],
        cot_rows, active_turned, ln_turned, grad_hidden, hidden_sums,
    )
    feed_twin = twin(feed_send)
    *grad_slots, bias_sums = run(
        attend_back_kernel,
        [near((line_rows * 2, 128), BF16)] * 4 + [near((8, 128), F32)],
        [
            pltpu.VMEM((length, 64), BF16),
            pltpu.VMEM((128, length), F32),
            pltpu.VMEM((64, length), F32),
            pltpu.VMEM((length, 128), F32),
            pltpu.VMEM((length, 64), F32),
            table,
            one_copy,
        ],
        *back_in, numbers, qk_rows, kq_rows, value_rows, attended, lse, *rotation,
    )
    grad_slots_in = with_places(grad_slots)
    low_own, low_half = run(
        halve_kernel,
        [near((rows, width), F32), near((rows, width), BF16)],
        [],
        low_keep, low_received,
    )
    low_rest = near(over_lines(raw(low_half), 2))
    grad_own, grad_half = run(
        halve_kernel,
        [near((rows, width), F32), near((rows, width), BF16)],
        [],
        grad_keep, grad_received,
    )
    grad_rest = near(over_lines(raw(grad_half), 2))
    mixed, att_turned, *mixed_slots = run(
        unpack_kernel,
        [near((line_rows, width), BF16), near((head_cols, line_rows), BF16)]
        + [near((rows, width), BF16)] * 3,
        [],
        *grad_slots_in,
    )
    _, *mixed_in = with_lines([mixed, *mixed_slots])
    qkv_send, qkv_keep = run(
        grads_kernel,
        [near((4 * qkv_block, qkv_cols), BF16), near((4 * qkv_block, qkv_cols), F32)],
        [
            pltpu.VMEM((line_rows, width), F32),
            pltpu.VMEM((256, qkv_cols), F32),
            pltpu.VMEM((head_cols, width), F32),
        ],
        mixed, feed_grad_low, normed, ln_turned, qkv, att_turned, cot_rows, bias_sums,
    )
    qkv_terms = twin(qkv_send)
    feed_blocks = run(
        share_twin_kernel,
        [near((block, width), F32)] + [near((block, width), BF16)] * 3,
        [],
        feed_keep, feed_twin,
    )
    feed_in = with_places(feed_blocks)
    qkv_blocks = run(
        share_twin_kernel,
        [near((qkv_block, qkv_cols), F32)] + [near((qkv_block, qkv_cols), BF16)] * 3,
        [],
        qkv_keep, qkv_terms,
    )
    qkv_sums = with_places(qkv_blocks)
    grad_down, grad_b_in, grad_b, *in_slots = run(
        feed_sum_kernel,
        [far((128, width), F32), ((1, 128), F32), ((1, 32), F32), near((32, width), F32)]
        + [near((32, width), BF16)] * 3,
        [],
        *feed_in,
    )
    in_parts = with_lines(in_slots)
    layer_out, grad_tokens = run(
        tokens_kernel,
        [far((rows, width), BF16), far((rows, width), BF16)],
        [],
        mixed, *mixed_in, qkv, w_out_full, low_own, low_rest, grad_own, grad_rest,
        far(tokens[0]), cot_rows, vectors,
    )
    grad_out, grad_qv, *qkv_parts = run(
        grad_sum_kernel,
        [far((32, width), F32), far((2, 32), F32), near((32 + VEC, qkv_cols), F32)]
        + [near((32 + VEC, qkv_cols), BF16)] * 3,
        [],
        *qkv_sums,
    )
    qkv_parts = with_lines(qkv_parts)
    (grad_in,) = run(join_in_kernel, [far((32, feed), F32)], [], *in_parts)
    grad_qkv, grad_gain, grad_shift = run(
        join_qkv_kernel,
        [far((32, 3 * width), F32), ((1, 32), F32), ((1, 32), F32)],
        [pltpu.VMEM((VEC, 32), F32)],
        *qkv_parts,
    )
    return (
        layer_out[None],
        grad_tokens[None],
        grad_gain[0],
        grad_shift[0],
        grad_qkv,
        grad_qv,
        grad_out,
        grad_b[0],
        grad_in,
        grad_b_in[0],
        grad_down,
        grad_b[0],
    )


def solution(mesh):
    one_head_each = mesh.shape["ctx"] == HEADS and mesh.shape["fsdp"] == 2
    return jax.shard_map(
        head_body if one_head_each else body,
        mesh=mesh,
        in_specs=(
            P("fsdp", "ctx", None),
            P("ctx", None),
            P("fsdp"),
            P("fsdp"),
            P("fsdp", None),
            P(None, "fsdp"),
            P("fsdp", None),
            P("fsdp"),
            P("fsdp", None),
            P("fsdp"),
            P("fsdp", None),
            P("fsdp"),
            P("fsdp", "ctx", None),
        ),
        out_specs=(
            P("fsdp", "ctx", None),
            P("fsdp", "ctx", None),
            P(("ctx", "fsdp")),
            P(("ctx", "fsdp")),
            P(("ctx", "fsdp"), None),
            P(None, ("ctx", "fsdp")),
            P(("ctx", "fsdp"), None),
            P(("ctx", "fsdp")),
            P(("ctx", "fsdp"), None),
            P(("ctx", "fsdp")),
            P(("ctx", "fsdp"), None),
            P(("ctx", "fsdp")),
        ),
        check_vma=False,
    )
```

```python
from functools import partial
import math

import jax
import jax.numpy as jnp
import numpy as np
from jax import lax
from jax.experimental import pallas as pl
from jax.experimental.pallas import tpu as pltpu
from jax.sharding import PartitionSpec as P

HEADS = 16
HEAD_DIM = 64
ROT = 16


epsilon = 1e-05


def from_behind(block, axis, distance):
    devices = range(lax.axis_size(axis))
    route = [((i - distance) % len(devices), i) for i in devices]
    return lax.ppermute(block, axis, route)


def rotate(vectors, cosine, sine_part):
    half_rot = ROT // 2
    rotary_part = vectors[..., :ROT]
    turned = jnp.concatenate([-rotary_part[..., half_rot:], rotary_part[..., :half_rot]], -1)
    return jnp.concatenate([rotary_part * cosine + turned * sine_part, vectors[..., ROT:]], -1)


def tables(positions):
    freq_index = jnp.arange(ROT // 2, dtype=jnp.float32)
    inverse = 10000.0 ** (-2.0 * freq_index / ROT)
    angles = positions.astype(jnp.float32)[:, None] * inverse[None, :]
    angles = jnp.concatenate([angles, angles], -1)
    return (jnp.cos(angles), jnp.sin(angles))


def spread_positions(orders, half_rows):
    offsets = jnp.arange(half_rows, dtype=jnp.int32)
    return (orders[:, :, None] * half_rows + offsets[None, None, :]).reshape(-1)


def outer_sum(left_side, right_side):
    return lax.dot_general(
        left_side, right_side, (((0,), (0,)), ((), ())), preferred_element_type=jnp.float32
    )


def times_transposed(left_side, right_side):
    return lax.dot_general(
        left_side, right_side, (((1,), (1,)), ((), ())), preferred_element_type=jnp.float32
    )


def attend_block(carried, queries, query_pos, key_rows, value_rows, key_pos, score_scale):
    row_max, row_sum, weighted = carried
    scores = (
        jnp.einsum("qhd,khd->hqk", queries, key_rows, preferred_element_type=jnp.float32)
        * score_scale
    )
    allowed = (query_pos[:, None] >= key_pos[None, :])[None]
    new_max = jnp.maximum(row_max, jnp.max(jnp.where(allowed, scores, -1e30), -1))
    weights = jnp.where(allowed, jnp.exp(scores - new_max[:, :, None]), 0.0)
    rescale = jnp.exp(row_max - new_max)
    row_sum = row_sum * rescale + jnp.sum(weights, -1)
    weighted = weighted * rescale.T[:, :, None] + jnp.einsum(
        "hqk,khd->qhd", weights.astype(jnp.bfloat16), value_rows, preferred_element_type=jnp.float32
    )
    return (new_max, row_sum, weighted)


def block_grads(
    queries, grad_rows, log_sum, delta_rows, query_pos, key_rows, value_rows, key_pos, score_scale
):
    scores = (
        jnp.einsum("qhd,khd->hqk", queries, key_rows, preferred_element_type=jnp.float32)
        * score_scale
    )
    allowed = (query_pos[:, None] >= key_pos[None, :])[None]
    probs = jnp.where(allowed, jnp.exp(scores - log_sum[:, :, None]), 0.0)
    grad_values = jnp.einsum(
        "hqk,qhd->khd", probs.astype(jnp.bfloat16), grad_rows, preferred_element_type=jnp.float32
    )
    grad_probs = jnp.einsum(
        "qhd,khd->hqk", grad_rows, value_rows, preferred_element_type=jnp.float32
    )
    grad_scores = (probs * (grad_probs - delta_rows[:, :, None])).astype(jnp.bfloat16)
    grad_queries = (
        jnp.einsum("hqk,khd->qhd", grad_scores, key_rows, preferred_element_type=jnp.float32)
        * score_scale
    )
    grad_keys = (
        jnp.einsum("hqk,qhd->khd", grad_scores, queries, preferred_element_type=jnp.float32)
        * score_scale
    )
    return (grad_queries, grad_keys, grad_values)


def body(
    tokens,
    block_order,
    ln_gain,
    ln_bias,
    w_qkv,
    qv_bias,
    w_out,
    b_out,
    w_in,
    b_in,
    w_down,
    b_down,
    cotangent,
):
    gathered = (
        lax.all_gather(ln_gain, "fsdp", axis=0, tiled=True),
        lax.all_gather(ln_bias, "fsdp", axis=0, tiled=True),
        lax.all_gather(w_qkv, "fsdp", axis=0, tiled=True),
        lax.all_gather(qv_bias, "fsdp", axis=1, tiled=True),
        lax.all_gather(w_out, "fsdp", axis=0, tiled=True),
        lax.all_gather(b_out, "fsdp", axis=0, tiled=True),
        lax.all_gather(w_in, "fsdp", axis=0, tiled=True),
        lax.all_gather(b_in, "fsdp", axis=0, tiled=True),
        lax.all_gather(w_down, "fsdp", axis=0, tiled=True),
        lax.all_gather(b_down, "fsdp", axis=0, tiled=True),
    )
    (
        gain_full,
        shift_full,
        qkv_full,
        bias_full,
        out_full,
        out_bias,
        in_full,
        in_bias,
        down_full,
        down_bias,
    ) = gathered
    tok_rows = tokens.shape[1]
    model_width = tokens.shape[2]
    half_rows = tok_rows // 2
    score_scale = HEAD_DIM ** (-0.5)
    head_shape = (tok_rows, HEADS, HEAD_DIM)
    flat_shape = (tok_rows, model_width)
    inputs = tokens[0].astype(jnp.float32)
    row_mean = jnp.mean(inputs, -1, keepdims=True)
    centered = inputs - row_mean
    inverse = lax.rsqrt(jnp.mean(centered * centered, -1, keepdims=True) + epsilon)
    normed = centered * inverse
    ln_out = (normed * gain_full.astype(jnp.float32) + shift_full.astype(jnp.float32)).astype(
        jnp.bfloat16
    )
    qkv_pre = jnp.dot(ln_out, qkv_full, preferred_element_type=jnp.float32)
    positions = spread_positions(block_order, half_rows)
    cosine, sine_part = tables(positions)
    cosine = cosine[:, None, :]
    sine_part = sine_part[:, None, :]
    query_pre = qkv_pre[:, :model_width] + bias_full[0].astype(jnp.float32)
    query_rows = rotate(query_pre.reshape(head_shape), cosine, sine_part).astype(jnp.bfloat16)
    key_rows = rotate(
        qkv_pre[:, model_width : 2 * model_width].reshape(head_shape), cosine, sine_part
    ).astype(jnp.bfloat16)
    value_rows = (qkv_pre[:, 2 * model_width :] + bias_full[1].astype(jnp.float32)).astype(
        jnp.bfloat16
    )
    key_flat = key_rows.reshape(flat_shape)
    start_state = (
        jnp.full((HEADS, tok_rows), -1e30, jnp.float32),
        jnp.zeros((HEADS, tok_rows), jnp.float32),
        jnp.zeros(head_shape, jnp.float32),
    )
    carried = start_state
    piece_keys = lax.all_gather(key_flat, "ctx", axis=0, tiled=True)
    piece_values = lax.all_gather(value_rows, "ctx", axis=0, tiled=True)
    piece_orders = lax.all_gather(block_order, "ctx", axis=0, tiled=True)
    shard_count = piece_orders.shape[0]
    group_size = math.gcd(shard_count, max(1, 1024 // tok_rows))
    rounds = shard_count // group_size
    stacked = (
        piece_keys.reshape(rounds, group_size * tok_rows, HEADS, HEAD_DIM),
        piece_values.reshape(rounds, group_size * tok_rows, HEADS, HEAD_DIM),
        piece_orders.reshape(rounds, group_size, 2),
    )

    def one_round(inner_state, block_item):
        key_pos = spread_positions(block_item[2], half_rows)
        return (
            attend_block(
                inner_state,
                query_rows,
                positions,
                block_item[0],
                block_item[1],
                key_pos,
                score_scale,
            ),
            None,
        )

    carried, _ = lax.scan(one_round, carried, stacked)
    row_max, row_sum, weighted = carried
    attended_f32 = weighted / row_sum.T[:, :, None]
    log_sum = row_max + jnp.log(row_sum)
    attended = attended_f32.reshape(flat_shape).astype(jnp.bfloat16)
    branch = jnp.dot(attended, out_full, preferred_element_type=jnp.float32) + out_bias.astype(
        jnp.float32
    )
    hidden = jnp.dot(ln_out, in_full, preferred_element_type=jnp.float32) + in_bias.astype(
        jnp.float32
    )
    active = jax.nn.gelu(hidden, approximate=False).astype(jnp.bfloat16)
    feed_out = jnp.dot(active, down_full, preferred_element_type=jnp.float32) + down_bias.astype(
        jnp.float32
    )
    layer_out = (inputs + branch + feed_out).astype(jnp.bfloat16)[None]
    gain_back, qkv_back, out_back, in_back, down_back = (
        gain_full,
        qkv_full,
        out_full,
        in_full,
        down_full,
    )
    grad_out = cotangent[0]
    grad_f32 = grad_out.astype(jnp.float32)
    grad_attended = times_transposed(grad_out, out_back).astype(jnp.bfloat16).reshape(head_shape)
    grad_active = times_transposed(grad_out, down_back)
    _, gelu_pull = jax.vjp(partial(jax.nn.gelu, approximate=False), hidden)
    grad_hidden = gelu_pull(grad_active)[0].astype(jnp.bfloat16)
    delta_rows = jnp.sum(grad_attended.astype(jnp.float32) * attended_f32, -1).T
    cotangent_sum = jnp.sum(grad_f32, 0)
    term_out_w = outer_sum(attended, grad_out)
    term_in_w = outer_sum(ln_out, grad_hidden)
    term_in_b = jnp.sum(grad_hidden.astype(jnp.float32), 0)
    term_down_w = outer_sum(active, grad_out)
    cycle_size = lax.axis_size("ctx")
    zeros_flat = jnp.zeros(flat_shape, jnp.float32)
    zeros_heads = jnp.zeros(head_shape, jnp.float32)

    def send_home(grad_keys, grad_values):
        return (
            from_behind(grad_keys.astype(jnp.bfloat16), "ctx", 1).astype(grad_keys.dtype),
            from_behind(grad_values.astype(jnp.bfloat16), "ctx", 1).astype(grad_values.dtype),
        )

    def visit_keys(carried):
        visit_key, visit_value, visit_order, grad_keys, grad_values, grad_query = carried
        part_query, part_key, part_value = block_grads(
            query_rows,
            grad_attended,
            log_sum,
            delta_rows,
            positions,
            visit_key.reshape(head_shape),
            visit_value.reshape(head_shape),
            spread_positions(visit_order, half_rows),
            score_scale,
        )
        return (
            grad_keys + part_key.reshape(flat_shape),
            grad_values + part_value.reshape(flat_shape),
            grad_query + part_query,
        )

    def cycle_step(step_index, carried):
        grad_keys, grad_values, grad_query = visit_keys(carried)
        visit_key, visit_value, visit_order = from_behind(
            (carried[0], carried[1], carried[2]), "ctx", 1
        )
        grad_keys, grad_values = send_home(grad_keys, grad_values)
        return (visit_key, visit_value, visit_order, grad_keys, grad_values, grad_query)

    carried = lax.fori_loop(
        0,
        cycle_size - 1,
        cycle_step,
        (key_flat, value_rows, block_order, zeros_flat, zeros_flat, zeros_heads),
    )
    grad_keys, grad_values, grad_query = visit_keys(carried)
    grad_keys, grad_values = send_home(grad_keys, grad_values)
    grad_keys = grad_keys.reshape(head_shape)
    grad_values = grad_values.reshape(head_shape)
    grad_q_pre = rotate(grad_query, cosine, -sine_part).reshape(flat_shape).astype(jnp.bfloat16)
    grad_k_pre = rotate(grad_keys, cosine, -sine_part).reshape(flat_shape).astype(jnp.bfloat16)
    grad_v_pre = grad_values.reshape(flat_shape).astype(jnp.bfloat16)
    grad_qkv = jnp.concatenate([grad_q_pre, grad_k_pre, grad_v_pre], -1)
    grad_ln = times_transposed(grad_qkv, qkv_back) + times_transposed(grad_hidden, in_back)
    grad_normed = grad_ln * gain_back.astype(jnp.float32)
    grad_inputs = inverse * (
        grad_normed
        - jnp.mean(grad_normed, -1, keepdims=True)
        - normed * jnp.mean(grad_normed * normed, -1, keepdims=True)
    )
    grad_tokens = (grad_f32 + grad_inputs).astype(jnp.bfloat16)[None]
    term_gain = jnp.sum(grad_ln * normed, 0)
    term_bias = jnp.sum(grad_ln, 0)
    term_qkv = outer_sum(ln_out, grad_qkv)
    term_qv = jnp.stack(
        [jnp.sum(grad_q_pre.astype(jnp.float32), 0), jnp.sum(grad_v_pre.astype(jnp.float32), 0)], 0
    )
    (
        sum_gain,
        sum_bias,
        sum_qkv,
        sum_qv,
        sum_out_w,
        sum_out_b,
        sum_in_w,
        sum_in_b,
        sum_down_w,
        sum_down_b,
    ) = (
        lax.psum_scatter(term_gain, ("ctx", "fsdp"), scatter_dimension=0, tiled=True),
        lax.psum_scatter(term_bias, ("ctx", "fsdp"), scatter_dimension=0, tiled=True),
        lax.psum_scatter(term_qkv, ("ctx", "fsdp"), scatter_dimension=0, tiled=True),
        lax.psum_scatter(term_qv, ("ctx", "fsdp"), scatter_dimension=1, tiled=True),
        lax.psum_scatter(term_out_w, ("ctx", "fsdp"), scatter_dimension=0, tiled=True),
        lax.psum_scatter(cotangent_sum, ("ctx", "fsdp"), scatter_dimension=0, tiled=True),
        lax.psum_scatter(term_in_w, ("ctx", "fsdp"), scatter_dimension=0, tiled=True),
        lax.psum_scatter(term_in_b, ("ctx", "fsdp"), scatter_dimension=0, tiled=True),
        lax.psum_scatter(term_down_w, ("ctx", "fsdp"), scatter_dimension=0, tiled=True),
        lax.psum_scatter(cotangent_sum, ("ctx", "fsdp"), scatter_dimension=0, tiled=True),
    )
    return (
        layer_out,
        grad_tokens,
        sum_gain,
        sum_bias,
        sum_qkv,
        sum_qv,
        sum_out_w,
        sum_out_b,
        sum_in_w,
        sum_in_b,
        sum_down_w,
        sum_down_b,
    )


LINES = 4
ACROSS = HEADS // LINES
F32 = jnp.float32
BF16 = jnp.bfloat16
VMEM_LIMIT = 16 * 1024 * 1024
TIMES = {'hold': 5000, 'feed_grad': 40, 'halve': 400, 'unpack': 150, 'feed_sum': 150, 'feed_terms': 5, 'share_twin': 400, 'join_in': 5, 'attend': 20, 'grads': 40}

VEC = 16


def dot(left, right):
    return jnp.dot(left, right, preferred_element_type=F32)


def dot_nt(left, right):
    return lax.dot_general(left, right, (((1,), (1,)), ((), ())), preferred_element_type=F32)


class Far(tuple):
    pass


class Near(tuple):
    pass


def far(*x):
    return Far(x)


def near(*x):
    return Near(x)


def raw(x):
    return x[0] if isinstance(x, (Far, Near)) else x


def placed(x):
    if isinstance(x, Far):
        return pltpu.with_memory_space_constraint(x[0], pltpu.HBM)
    if isinstance(x, Near):
        return pltpu.with_memory_space_constraint(x[0], pltpu.VMEM)
    return x


def spot():
    context = lax.axis_index("ctx")
    return context // ACROSS, context % ACROSS, lax.axis_index("fsdp")


def call(kernel, out_shapes, scratch, *operands, after=(), loose_in=0):
    whole = pl.BlockSpec(memory_space=pltpu.VMEM)
    loose = pl.BlockSpec(memory_space=pl.ANY)
    arrays, specs = [], []
    for x in operands:
        arrays.append(placed(x))
        if arrays[-1].dtype == jnp.int32 and arrays[-1].ndim == 1:
            specs.append(pl.BlockSpec(memory_space=pltpu.SMEM))
        else:
            specs.append(loose if len(specs) < loose_in else whole)
    outs = []
    for shape in out_shapes:
        if isinstance(shape, Far):
            outs.append(pltpu.HBM(*shape))
        elif isinstance(shape, Near):
            outs.append(pltpu.VMEM(*shape))
        else:
            outs.append(jax.ShapeDtypeStruct(*shape))
    count = len(arrays)

    def body(*refs):
        kernel(*refs[:count], *refs[count + len(after) :])

    name = kernel.__name__.removesuffix("_kernel")
    results = pl.pallas_call(
        body,
        name=name,
        out_shape=outs,
        in_specs=specs + [loose] * len(after),
        out_specs=[whole for _ in outs],
        scratch_shapes=scratch,
        compiler_params=pltpu.CompilerParams(vmem_limit_bytes=VMEM_LIMIT),
        cost_estimate=pl.CostEstimate(
            flops=TIMES.get(name, 0) * 115_000_000, bytes_accessed=0, transcendentals=0
        ),
    )(*arrays, *map(placed, after))
    return [
        near(x) if isinstance(shape, Near) else x for x, shape in zip(results, out_shapes)
    ]


def run_copies(pairs, sems):
    copies = [pltpu.make_async_copy(x, y, sems.at[i]) for i, (x, y) in enumerate(pairs)]
    for copy in copies:
        copy.start()
    for copy in copies:
        copy.wait()


def prepare_kernel(qkv, w_in, w_out, w_down, gain, shift, b_out, b_down, qv, b_in, packed, sems):
    line, _, _ = spot()
    feed = w_in.shape[1] // LINES
    half, width = w_out.shape
    part = line % (LINES // 2)
    row = 0
    pairs = []
    sources = [
        w_in.at[:, pl.ds(pl.multiple_of(feed * line, 128), feed)],
        w_out,
        w_down.at[pl.ds(pl.multiple_of(feed * part, 16), feed), :],
    ]
    for source in sources + [qkv.at[:, width * i : width * (i + 1)] for i in range(3)]:
        pairs.append((source, packed.at[row : row + source.shape[0], :]))
        row += source.shape[0]
    rows = [x[...].astype(F32).reshape(1, half) for x in (gain, shift, b_out, b_down)]
    rows += [qv[...].astype(F32), b_in[...].astype(F32).reshape(4, half)]
    rows.append(jnp.zeros((VEC - 10, half), F32))
    packed[row : row + VEC, :half] = jnp.concatenate(rows, 0).astype(BF16)
    run_copies(pairs, sems)


def assemble_kernel(own, twin, qkv, w_in, w_out, w_down, vectors, low, sems):
    line, _, core = spot()
    width = w_out.shape[1]
    half = width // 2
    feed = w_down.shape[0]
    down_row = 2 * half
    qkv_row = down_row + feed
    vec_row = qkv_row + 3 * half
    pairs = []
    for source, side in ((own, core), (twin, 1 - core)):
        rows = pl.ds(pl.multiple_of(half * side, half), half)
        pairs.append((source.at[:half, :], w_in.at[rows, :]))
        pairs.append((source.at[half:down_row, :], w_out.at[rows, :]))
        for i in range(3):
            base = qkv_row + half * i
            pairs.append(
                (source.at[base : base + half, :], qkv.at[rows, width * i : width * (i + 1)])
            )
        spare = pl.ds(pl.multiple_of(VEC * side, VEC), VEC)
        pairs.append((source.at[vec_row:, :half], low.at[spare, :]))
    holds = core == line // (LINES // 2)

    @pl.when(holds)
    def _():
        run_copies(pairs + [(own.at[down_row:qkv_row, :], w_down)], sems)

    @pl.when(jnp.logical_not(holds))
    def _():
        run_copies(pairs + [(twin.at[down_row:qkv_row, :], w_down)], sems)

    vectors[...] = low[...].astype(F32)


def line_columns(qkv, part):
    line, _, _ = spot()
    width = qkv.shape[1] // 3
    base = width * part + width // LINES * line
    return qkv[:, pl.ds(pl.multiple_of(base, 128), width // LINES)]


def line_rows_of(w_out):
    line, _, _ = spot()
    count = w_out.shape[0] // LINES
    return w_out[pl.ds(pl.multiple_of(count * line, 16), count), :]


def full_row(vectors, index):
    return jnp.concatenate(
        [vectors[index : index + 1, :], vectors[VEC + index : VEC + index + 1, :]], 1
    )


def pack_kernel(order, tokens, packed):
    rows = tokens.shape[0]
    packed[:rows, :] = tokens[...]
    lane = lax.broadcasted_iota(jnp.int32, (VEC, 128), 1)
    numbers = jnp.where(lane == 0, order[0], jnp.where(lane == 1, order[1], 0))
    packed[rows:, :128] = numbers.astype(F32).astype(BF16)
    packed[rows:, 128:] = jnp.zeros((VEC, tokens.shape[1] - 128), BF16)


def reorder(chunks, place):
    upper, lower = chunks
    turned = (place & 2) != 0
    near_by = (place & 1) != 0
    first = jnp.where(turned, lower, upper)
    second = jnp.where(turned, upper, lower)
    first = jnp.where(near_by, pltpu.roll(first, 64, 1), first)
    second = jnp.where(near_by, pltpu.roll(second, 64, 1), second)
    return first, second


def left_lanes(rows):
    return lax.broadcasted_iota(jnp.int32, (rows, 128), 1) < 64


def pair_heads(one, two, slot):
    keep = left_lanes(one.shape[0])
    if slot % 2 == 0:
        return jnp.where(keep, one, pltpu.roll(two, 64, 1))
    return jnp.where(keep, pltpu.roll(one, 64, 1), two)


def fold_rows(chunk, slot):
    rows = chunk.shape[0] // 2
    return pair_heads(chunk[:rows], chunk[rows:], slot)


def unfold_pair(even, odd):
    keep = left_lanes(even.shape[0])
    top = jnp.where(keep, even, pltpu.roll(odd, 64, 1))
    bottom = jnp.where(keep, pltpu.roll(even, 64, 1), odd)
    return jnp.concatenate([top, bottom], 0)


def normalise(rows):
    x = rows.astype(F32)
    centred = x - jnp.mean(x, -1, keepdims=True)
    inverse = lax.rsqrt(jnp.mean(centred * centred, -1, keepdims=True) + epsilon)
    return centred * inverse, inverse


def two_chunks(x):
    return x[:, :128], x[:, 128:256]


def two_chunks(x):
    return x[:, :128], x[:, 128:256]


def project_kernel(t0, t1, t2, t3, vectors, qkv, s0, s1, s2, s3, ln_ref, lnt_ref, normed_ref):
    line, place, _ = spot()
    rows = t0.shape[0] - VEC
    gain, shift = full_row(vectors, 0), full_row(vectors, 1)
    numbers = jnp.zeros((VEC, 128), F32)
    for k, ref in enumerate((t0, t1, t2, t3)):
        source = line ^ k
        part = pl.ds(pl.multiple_of(rows * source, rows), rows)
        normed, _ = normalise(ref[:rows, :])
        normed_ref[part, :] = normed
        ln_ref[part, :] = (normed * gain + shift).astype(BF16)
        numbers = numbers + pltpu.roll(ref[rows:, :128].astype(F32), 2 * source, 1)
    side = VEC * (line // (LINES // 2))
    lanes = pl.ds(pl.multiple_of(256 * (line % (LINES // 2)), 256), 256)
    bias_q = vectors[pl.ds(side + 4, 1), lanes]
    bias_v = vectors[pl.ds(side + 5, 1), lanes]
    q_chunks = reorder(two_chunks(dot(ln_ref[...], line_columns(qkv, 0)) + bias_q), place)
    k_chunks = reorder(two_chunks(dot(ln_ref[...], line_columns(qkv, 1))), place)
    v_chunks = reorder(two_chunks(dot(ln_ref[...], line_columns(qkv, 2)) + bias_v), place)
    total = ln_ref.shape[0]
    end = total * 3 // 2
    for slot, ref in enumerate((s0, s1, s2, s3)):
        pair = slot // 2
        ref[:total, :] = pair_heads(q_chunks[pair], k_chunks[pair], slot).astype(BF16)
        ref[total:end, :] = fold_rows(v_chunks[pair], slot).astype(BF16)
        ref[end:, :] = numbers.astype(BF16)
    lnt_ref[...] = ln_ref[...].T


def back_rows_kernel(c0, c1, c2, c3, w_out, s0, s1, s2, s3, cot):
    line, place, _ = spot()
    rows = c0.shape[0]
    for k, ref in enumerate((c0, c1, c2, c3)):
        cot[pl.ds(pl.multiple_of(rows * (line ^ k), rows), rows), :] = ref[...]
    chunks = reorder(two_chunks(dot_nt(cot[...], line_rows_of(w_out))), place)
    for slot, ref in enumerate((s0, s1, s2, s3)):
        ref[...] = fold_rows(chunks[slot // 2], slot).astype(BF16)


def block_rows(table):
    for j in range(4):
        for i in range(8):
            yield j, i, pl.ds(pl.multiple_of(table[8 * j, i] * 64, 64), 64)


def sort_rows(table, slots, target, base, folded):
    for j, i, dest in block_rows(table):
        if folded:
            start = base + 64 * (i % 4)
            lanes = slice(0, 64) if i < 4 else slice(64, 128)
            target[dest, :] = slots[j][start : start + 64, lanes]
        else:
            target[dest, :] = slots[j][base + 64 * i : base + 64 * (i + 1), :]


def turn(x, cosine, sine):
    lane = lax.broadcasted_iota(jnp.int32, x.shape, 1) & (HEAD_DIM - 1)
    other = jnp.where(lane < ROT // 2, pltpu.roll(x, 120, 1), pltpu.roll(x, 8, 1))
    return x * cosine + other * sine


TILE = 256


def scores_of(qk_ref, i):
    rows = slice(TILE * i, TILE * (i + 1))
    queries = jnp.where(left_lanes(TILE), qk_ref[rows, :], jnp.zeros((), BF16))
    queries = queries * jnp.asarray(HEAD_DIM ** (-0.5), BF16)
    return queries


def allowed_tile():
    row = lax.broadcasted_iota(jnp.int32, (TILE, TILE), 0)
    col = lax.broadcasted_iota(jnp.int32, (TILE, TILE), 1)
    return row >= col


def attend_kernel(r0, r1, r2, r3, cosine, sine, *rest):
    qk_ref, kq_ref, v_ref, att_ref, lse_ref, table_ref, raw, table, sem = rest
    refs = (r0, r1, r2, r3)
    count = qk_ref.shape[0]
    lines = count // 4
    for j, ref in enumerate(refs):
        numbers = ref[lines * 3 // 2 :, :].astype(F32)[:8, :]
        table_ref[8 * j : 8 * (j + 1), :] = numbers.astype(jnp.int32)
    run_copies([(table_ref, table)], sem)
    sort_rows(table, refs, raw, 0, False)
    sort_rows(table, refs, v_ref, lines, True)
    for i in range(count // TILE):
        rows = slice(TILE * i, TILE * (i + 1))
        turned = turn(raw[rows, :].astype(F32), cosine[rows, :], sine[rows, :])
        qk_ref[rows, :] = turned.astype(BF16)
        kq_ref[rows, :] = pltpu.roll(turned, 64, 1).astype(BF16)
    mask = allowed_tile()
    for i in range(count // TILE):
        rows = slice(TILE * i, TILE * (i + 1))
        keys = TILE * (i + 1)
        scores = dot_nt(scores_of(qk_ref, i), kq_ref[:keys, :])
        last = jnp.where(mask, scores[:, keys - TILE :], -1e30)
        scores = last if i == 0 else jnp.concatenate([scores[:, : keys - TILE], last], 1)
        top = jnp.max(scores, -1, keepdims=True)
        weights = jnp.exp(scores - top)
        total = jnp.sum(weights, -1, keepdims=True)
        weighted = dot(weights.astype(BF16), v_ref[:keys, :])
        att_ref[rows, :] = weighted / total
        lse_ref[rows, :] = top + jnp.log(total)


def attend_back_kernel(r0, r1, r2, r3, table_ref, qk_ref, kq_ref, v_ref, att_ref, *rest):
    lse_ref, cosine, sine, o0, o1, o2, o3, sums, ga_ref, kt_ref, vt_ref, gqk, gv = rest[:13]
    table, sem = rest[13:]
    refs = (r0, r1, r2, r3)
    count = qk_ref.shape[0]
    lines = count // 4
    run_copies([(table_ref, table)], sem)
    sort_rows(table, refs, ga_ref, 0, True)
    mask = allowed_tile()
    kt_ref[...] = jnp.zeros_like(kt_ref)
    vt_ref[...] = jnp.zeros_like(vt_ref)
    for i in range(count // TILE):
        rows = slice(TILE * i, TILE * (i + 1))
        keys = TILE * (i + 1)
        queries = scores_of(qk_ref, i)
        scores = dot_nt(queries, kq_ref[:keys, :])
        last = jnp.where(mask, scores[:, keys - TILE :], -1e30)
        scores = last if i == 0 else jnp.concatenate([scores[:, : keys - TILE], last], 1)
        probs = jnp.exp(scores - lse_ref[rows, :])
        grad_rows = ga_ref[rows, :]
        delta = jnp.sum(grad_rows.astype(F32) * att_ref[rows, :], -1, keepdims=True)
        grad_probs = dot_nt(grad_rows, v_ref[:keys, :])
        grad_scores = (probs * (grad_probs - delta)).astype(BF16)
        gqk[rows, :] = dot(grad_scores, kq_ref[:keys, :]) * HEAD_DIM ** (-0.5)
        vt_ref[:, :keys] += dot(grad_rows.astype(F32).T.astype(BF16), probs.astype(BF16))
        kt_ref[:, :keys] += dot(queries.astype(F32).T.astype(BF16), grad_scores)
    sum_q = jnp.zeros((1, 128), F32)
    sum_v = jnp.zeros((1, 64), F32)
    for i in range(count // TILE):
        rows = slice(TILE * i, TILE * (i + 1))
        grad_keys = pltpu.roll(kt_ref[:, rows].T, 64, 1)
        both = jnp.where(left_lanes(TILE), gqk[rows, :], grad_keys)
        both = turn(both, cosine[rows, :], -sine[rows, :])
        both = both.astype(BF16).astype(F32)
        values = vt_ref[:, rows].T.astype(BF16).astype(F32)
        gqk[rows, :] = both
        gv[rows, :] = values
        sum_q = sum_q + jnp.sum(both, 0, keepdims=True)
        sum_v = sum_v + jnp.sum(values, 0, keepdims=True)
    sums[...] = jnp.zeros_like(sums)
    sums[0:1, :64] = sum_q[:, :64]
    sums[1:2, :64] = sum_v
    outs = (o0, o1, o2, o3)
    for j, i, source in block_rows(table):
        lanes = slice(0, 64) if i < 4 else slice(64, 128)
        outs[j][64 * i : 64 * (i + 1), :] = gqk[source, :].astype(BF16)
        start = lines + 64 * (i % 4)
        outs[j][start : start + 64, lanes] = gv[source, :].astype(BF16)
        start += lines // 2
        outs[j][start : start + 64, lanes] = att_ref[source, :].astype(BF16)


def split_lines(low, keep, send):
    line, _, _ = spot()
    rows = low.shape[0] // LINES
    for k, (ref, base) in enumerate(((keep, 0), (send, 0), (keep, rows), (send, rows))):
        part = pl.ds(pl.multiple_of(rows * (line ^ k), rows), rows)
        ref[base : base + rows, :] = low[part, :].astype(ref.dtype)


def feed_kernel(ln, w_in, vectors, w_down, hidden_ref, actt_ref, keep, send, act_ref, low_ref):
    line, _, _ = spot()
    row = VEC * (line // (LINES // 2)) + 6 + 2 * (line % (LINES // 2))
    bias = jnp.concatenate([vectors[pl.ds(row, 1), :], vectors[pl.ds(row + 1, 1), :]], 1)
    for f in range(4):
        cols = slice(256 * f, 256 * (f + 1))
        hidden = dot(ln[...], w_in[:, cols]) + bias[:, cols]
        hidden_ref[:, cols] = hidden
        active = 0.5 * hidden * (1.0 + lax.erf(hidden * 0.7071067811865476))
        act_ref[:, cols] = active.astype(BF16)
        actt_ref[cols, :] = active.astype(BF16).T
    for f in range(4):
        cols = slice(256 * f, 256 * (f + 1))
        low_ref[:, cols] = dot(act_ref[...], w_down[:, cols])
    split_lines(low_ref, keep, send)


def feed_grad_kernel(cot, hidden, w_in, w_down, gh_ref, sums, low_ref, keep, send):
    for f in range(4):
        cols = slice(256 * f, 256 * (f + 1))
        grad_active = dot_nt(cot[...], w_down[cols, :])
        h = hidden[:, cols]
        slope = 0.5 * (1.0 + lax.erf(h * 0.7071067811865476)) + h * jnp.exp(
            -0.5 * h * h
        ) * 0.3989422804014327
        grad_hidden = (slope * grad_active).astype(BF16)
        gh_ref[:, cols] = grad_hidden
        total = jnp.sum(grad_hidden.astype(F32), 0, keepdims=True)
        sums[:, cols] = jnp.broadcast_to(total, (8, 256))
    for i in range(4):
        low_ref[:, 256 * i : 256 * (i + 1)] = dot_nt(gh_ref[...], w_in[256 * i : 256 * (i + 1), :])
    split_lines(low_ref, keep, send)


def feed_terms_kernel(cot_ref, actt, lnt, gh, sums, send, keep, chunk_ref):
    line, _, core = spot()
    cot = cot_ref[...]
    block = send.shape[0] // 4
    for f in range(4):
        chunk_ref[...] = dot(actt[256 * f : 256 * (f + 1), :], cot)
        base = block * f
        send[base : base + 128, :] = chunk_ref[
            pl.ds(pl.multiple_of((1 - core) * 128, 128), 128), :
        ].astype(BF16)
        keep[base : base + 128, :] = chunk_ref[pl.ds(pl.multiple_of(core * 128, 128), 128), :]
    for z in range(4):
        chunk_ref[...] = dot(lnt[256 * z : 256 * (z + 1), :], gh[...])
        for f in range(4):
            base = block * f + 128 + 32 * z
            send[base : base + 32, :] = chunk_ref[
                pl.ds(pl.multiple_of(64 * f + 32 * (1 - core), 32), 32), :
            ].astype(BF16)
            keep[base : base + 32, :] = chunk_ref[
                pl.ds(pl.multiple_of(64 * f + 32 * core, 32), 32), :
            ]
    cot_sum = jnp.sum(cot.astype(F32), 0, keepdims=True)
    picked = jnp.where(
        line < 2,
        jnp.where(line == 0, cot_sum[:, 0:256], cot_sum[:, 256:512]),
        jnp.where(line == 2, cot_sum[:, 512:768], cot_sum[:, 768:1024]),
    )
    zero = jnp.zeros((1, 640), F32)
    for f in range(4):
        even, odd = sums[:1, 256 * f : 256 * f + 128], sums[:1, 256 * f + 128 : 256 * f + 256]
        first = core == 0
        base = block * f + 256
        given = jnp.concatenate([jnp.where(first, odd, even), picked, zero], 1)
        kept = jnp.concatenate([jnp.where(first, even, odd), picked, zero], 1)
        send[base : base + VEC, :] = jnp.broadcast_to(given, (VEC, 1024)).astype(BF16)
        keep[base : base + VEC, :] = jnp.broadcast_to(kept, (VEC, 1024))


def share_twin_kernel(keep, received, o0, o1, o2, o3):
    _, place, _ = spot()
    block = o0.shape[0]
    for slot, ref in enumerate((o0, o1, o2, o3)):
        rows = pl.ds(pl.multiple_of((place ^ slot) * block, 16), block)
        ref[...] = (keep[rows, :] + received[rows, :].astype(F32)).astype(ref.dtype)


def adder(own, r1, r2, r3):
    def total(rows, cols=slice(None)):
        return (own[rows, cols].astype(F32) + r1[rows, cols].astype(F32)) + (
            r2[rows, cols].astype(F32) + r3[rows, cols].astype(F32)
        )

    return total


def owned_lanes(rows):
    _, place, core = spot()
    return pltpu.roll(rows, lax.rem(256 - (64 * place + 32 * core), 256), 1)[:, :32]


def feed_sum_kernel(own, r1, r2, r3, down_ref, bias_in, bias_out, i0, i1, i2, i3):
    line, _, _ = spot()
    total = adder(own, r1, r2, r3)
    down_ref[...] = total(slice(0, 128))
    bias_in[...] = total(slice(256, 264), slice(0, 128))[:1]
    bias_out[...] = owned_lanes(total(slice(256, 264), slice(128, 384)))[:1]
    for slot, ref in enumerate((i0, i1, i2, i3)):
        rows = pl.ds(pl.multiple_of(128 + 32 * (line ^ slot), 32), 32)
        ref[...] = total(rows).astype(ref.dtype)


def halve_kernel(keep, received, own, send):
    rows = own.shape[0]
    own[...] = keep[:rows, :] + received[:rows, :].astype(F32)
    send[...] = (keep[rows:, :] + received[rows:, :].astype(F32)).astype(BF16)


def unpack_kernel(r0, r1, r2, r3, mixed, att_t, s1, s2, s3):
    line, place, _ = spot()
    rows = s1.shape[0]
    total = LINES * rows
    fold = total // 2
    parts = [ref[...].astype(F32) for ref in (r0, r1, r2, r3)]
    keep_left = left_lanes(total)
    chunks = [[], [], [], []]
    for pair in range(2):
        one, two = parts[2 * pair], parts[2 * pair + 1]
        even, odd = one[:total], two[:total]
        values, attended = slice(total, total + fold), slice(total + fold, total + 2 * fold)
        chunks[0].append(unfold_pair(one[attended], two[attended]))
        chunks[1].append(jnp.where(keep_left, even, pltpu.roll(odd, 64, 1)))
        chunks[2].append(jnp.where(keep_left, pltpu.roll(even, 64, 1), odd))
        chunks[3].append(unfold_pair(one[values], two[values]))
    for index, both in enumerate(chunks):
        for pair, chunk in enumerate(reorder(both, place)):
            base = 256 * index + 128 * pair
            mixed[:, base : base + 128] = chunk.astype(BF16)
    for k, ref in ((1, s1), (2, s2), (3, s3)):
        ref[...] = mixed[pl.ds(pl.multiple_of(rows * (line ^ k), rows), rows), :]
    att_t[...] = mixed[:, :256].T


def grads_kernel(mixed, low, normed, lnt, qkv, att_t, cot, head_sums, *rest):
    send, keep, low_ref, chunk_ref, out_ref = rest
    _, place, core = spot()
    low_ref[...] = low[...]
    for i in range(3):
        cols = slice(256 * (i + 1), 256 * (i + 2))
        low_ref[...] += dot_nt(mixed[:, cols], line_columns(qkv, i))
    grad = low_ref[...]
    sum_gain = jnp.sum(grad * normed[...], 0, keepdims=True)
    sum_bias = jnp.sum(grad, 0, keepdims=True)
    block = send.shape[0] // 4
    for z in range(4):
        chunk_ref[...] = dot(lnt[256 * z : 256 * (z + 1), :], mixed[:, 256:])
        for f in range(4):
            base = block * f + 32 * z
            send[base : base + 32, :] = chunk_ref[
                pl.ds(pl.multiple_of(64 * f + 32 * (1 - core), 32), 32), :
            ].astype(BF16)
            keep[base : base + 32, :] = chunk_ref[
                pl.ds(pl.multiple_of(64 * f + 32 * core, 32), 32), :
            ]
    out_ref[...] = dot(att_t[...], cot[...])
    sums = [sum_gain[:, 256 * i : 256 * (i + 1)] for i in range(4)]
    sums += [sum_bias[:, 256 * i : 256 * (i + 1)] for i in range(4)]
    spare = jnp.concatenate([head_sums[...], jnp.zeros((8, 128), F32)], 1)
    for f in range(4):
        base = block * f + 128
        vec = jnp.concatenate(sums + [jnp.where(place == f, spare, 0.0)], 0)
        for ref, side in ((send, 1 - core), (keep, core)):
            rows = out_ref[pl.ds(pl.multiple_of(64 * f + 32 * side, 32), 32), :]
            tail = jnp.concatenate([rows[:16, 768:], rows[16:, 768:], vec], 1)
            ref[base : base + 32, :] = rows[:, :768].astype(ref.dtype)
            ref[base + 32 : base + 48, :] = tail.astype(ref.dtype)


def grad_sum_kernel(own, r1, r2, r3, grad_out, qv, i0, i1, i2, i3):
    line, _, core = spot()
    total = adder(own, r1, r2, r3)
    tail = total(slice(160, 176))
    grad_out[:, :768] = total(slice(128, 160))
    grad_out[:16, 768:] = tail[:, :256]
    grad_out[16:, 768:] = tail[:, 256:512]
    qv[...] = jnp.where(core == 0, tail[8:10, 512:544], tail[8:10, 544:576])
    for slot, ref in enumerate((i0, i1, i2, i3)):
        rows = pl.ds(pl.multiple_of(32 * (line ^ slot), 32), 32)
        ref[:32, :] = total(rows).astype(ref.dtype)
        ref[32:, :] = tail.astype(ref.dtype)


def join_in_kernel(i0, i1, i2, i3, out):
    line, _, _ = spot()
    for slot, ref in enumerate((i0, i1, i2, i3)):
        cols = pl.ds(pl.multiple_of((line ^ slot) * 1024, 1024), 1024)
        out[:, cols] = ref[...].astype(F32)


def join_qkv_kernel(i0, i1, i2, i3, out, gain, bias, vec_ref):
    line, _, _ = spot()
    vec = jnp.zeros((VEC, 256), F32)
    for slot, ref in enumerate((i0, i1, i2, i3)):
        for part in range(3):
            cols = pl.ds(pl.multiple_of(1024 * part + (line ^ slot) * 256, 256), 256)
            out[:, cols] = ref[:32, 256 * part : 256 * (part + 1)].astype(F32)
        vec = vec + ref[32:, 512:768].astype(F32)
    vec_ref[...] = owned_lanes(vec)
    gain[...] = vec_ref[pl.ds(line, 1), :].reshape(32)
    bias[...] = vec_ref[pl.ds(4 + line, 1), :].reshape(32)


def hold_kernel(x, out):
    out[...] = x[...]


def tokens_kernel(mixed, r1, r2, r3, qkv, w_out, *rest):
    low, low_rest, grad, grad_rest, tokens, cot, vectors, layer_out, grad_tokens = rest
    line, _, _ = spot()
    rows = low.shape[0]
    mine = pl.ds(pl.multiple_of(rows * line, rows), rows)
    branch = low[...] + low_rest[...].astype(F32)
    grad_ln = grad[...] + grad_rest[...].astype(F32)
    for k, ref in enumerate((mixed.at[mine, :], r1, r2, r3)):
        base = 256 * (line ^ k)
        part = pl.ds(pl.multiple_of(base, 256), 256)
        branch = branch + dot(ref[:, :256], w_out[part, :])
        for i in range(3):
            part = pl.ds(pl.multiple_of(base + 1024 * i, 256), 256)
            grad_ln = grad_ln + dot_nt(ref[:, 256 * (i + 1) : 256 * (i + 2)], qkv[:, part])
    own = tokens[:rows, :]
    branch = branch + own.astype(F32)
    layer_out[...] = (branch + full_row(vectors, 2) + full_row(vectors, 3)).astype(BF16)
    normed, inverse = normalise(own)
    g = grad_ln * full_row(vectors, 0)
    back = inverse * (
        g - jnp.mean(g, -1, keepdims=True) - normed * jnp.mean(g * normed, -1, keepdims=True)
    )
    grad_tokens[...] = (cot[mine, :].astype(F32) + back).astype(BF16)


def turn_tables(count):
    half_rot = ROT // 2
    inverse = 10000.0 ** (-2.0 * np.arange(half_rot) / ROT)
    angles = np.arange(count)[:, None] * inverse[None, :]
    cosine = np.ones((count, HEAD_DIM), np.float32)
    sine = np.zeros((count, HEAD_DIM), np.float32)
    cosine[:, :half_rot] = cosine[:, half_rot:ROT] = np.cos(angles)
    sine[:, :half_rot] = -np.sin(angles)
    sine[:, half_rot:ROT] = np.sin(angles)
    return tuple(np.concatenate([t, t], -1) for t in (cosine, sine))


def head_body(
    tokens,
    block_order,
    ln_gain,
    ln_bias,
    w_qkv,
    qv_bias,
    w_out,
    b_out,
    w_in,
    b_in,
    w_down,
    b_down,
    cotangent,
):
    positions = range(LINES * ACROSS)

    def over_lines(x, k):
        return lax.ppermute(x, "ctx", [(i, i ^ (k * ACROSS)) for i in positions])

    def over_places(x, j):
        return lax.ppermute(x, "ctx", [(i, i ^ j) for i in positions])

    def twin(x):
        return near(lax.ppermute(raw(x), "fsdp", [(0, 1), (1, 0)]))

    def with_lines(blocks):
        return [blocks[0]] + [near(over_lines(raw(blocks[k]), k)) for k in range(1, LINES)]

    def with_places(blocks):
        return [blocks[0]] + [near(over_places(raw(blocks[j]), j)) for j in range(1, ACROSS)]

    rows, width = tokens.shape[1], tokens.shape[2]
    half = w_qkv.shape[0]
    feed = w_in.shape[1]
    head_cols = width // LINES
    feed_cols = feed // LINES
    qkv_cols = 3 * head_cols
    length = rows * LINES * ACROSS
    line_rows = rows * LINES
    slot_rows = line_rows * 3 // 2
    rotation = turn_tables(length)
    packed_rows = 5 * half + feed_cols + VEC
    table = pltpu.SMEM((32, 128), jnp.int32)
    one_copy = pltpu.SemaphoreType.DMA((1,))
    block = 128 + 128 + VEC
    qkv_block = 128 + 32 + VEC

    last = []

    def run(kernel, out_shapes, scratch, *operands, after=(), loose_in=0):
        results = call(
            kernel, out_shapes, scratch, *operands, after=(*after, *last), loose_in=loose_in
        )
        last[:] = [far(results[0])] if isinstance(out_shapes[0], Far) else results[:1]
        return results
    (token_block,) = run(
        pack_kernel,
        [near((rows + VEC, width), BF16)],
        [],
        far(block_order.reshape(2)), far(tokens[0]),
    )
    from_two = over_lines(raw(token_block), 2)
    token_lines = [
        token_block,
        near(over_lines(raw(token_block), 1)),
        near(from_two),
        near(over_lines(from_two, 1)),
    ]
    (packed,) = run(
        prepare_kernel,
        [near((packed_rows, width), BF16)],
        [pltpu.SemaphoreType.DMA((6,))],
        far(w_qkv), far(w_in), far(w_out), far(w_down),
        *map(far, (ln_gain, ln_bias, b_out, b_down, qv_bias, b_in)),
        loose_in=4,
    )
    (cot_own,) = run(
        hold_kernel,
        [near((rows, width), BF16)],
        [],
        far(cotangent[0]),
        after=token_lines[1:3],
    )
    cot_two = over_lines(raw(cot_own), 2)
    cot_lines = [
        cot_own,
        near(over_lines(raw(cot_own), 1)),
        near(cot_two),
        near(over_lines(cot_two, 1)),
    ]
    qkv, in_rows, w_out_full, down_rows, vectors = run(
        assemble_kernel,
        [
            near((width, 3 * width), BF16),
            near((width, feed_cols), BF16),
            near((width, width), BF16),
            near((feed_cols, width), BF16),
            near((2 * VEC, half), F32),
        ],
        [pltpu.VMEM((2 * VEC, half), BF16), pltpu.SemaphoreType.DMA((13,))],
        packed, twin(packed),
        loose_in=2,
    )
    *slots, ln_low, ln_turned, normed = run(
        project_kernel,
        [near((slot_rows + VEC, 128), BF16)] * 4
        + [
            near((line_rows, width), BF16),
            near((width, line_rows), BF16),
            near((line_rows, width), F32),
        ],
        [],
        *token_lines, vectors, qkv,
    )
    slots_in = with_places(slots)
    hidden, active_turned, low_keep, low_send = run(
        feed_kernel,
        [
            near((line_rows, feed_cols), F32),
            near((feed_cols, line_rows), BF16),
            near((2 * rows, width), F32),
            near((2 * rows, width), BF16),
        ],
        [pltpu.VMEM((line_rows, feed_cols), BF16), pltpu.VMEM((line_rows, width), F32)],
        ln_low, in_rows, vectors, down_rows,
    )
    low_received = near(over_lines(raw(low_send), 1))
    qk_rows, kq_rows, value_rows, attended, lse, numbers = run(
        attend_kernel,
        [
            near((length, 128), BF16),
            near((length, 128), BF16),
            near((length, 64), BF16),
            near((length, 64), F32),
            near((length, 1), F32),
            near((32, 128), jnp.int32),
        ],
        [pltpu.VMEM((length, 128), BF16), table, one_copy],
        *slots_in, *rotation,
    )
    *back_slots, cot_rows = run(
        back_rows_kernel,
        [near((line_rows // 2, 128), BF16)] * 4 + [near((line_rows, width), BF16)],
        [],
        *cot_lines, w_out_full,
    )
    back_in = with_places(back_slots)
    grad_hidden, hidden_sums, feed_grad_low, grad_keep, grad_send = run(
        feed_grad_kernel,
        [
            near((line_rows, feed_cols), BF16),
            near((8, feed_cols), F32),
            near((line_rows, width), F32),
            near((2 * rows, width), F32),
            near((2 * rows, width), BF16),
        ],
        [],
        cot_rows, hidden, in_rows, down_rows,
    )
    grad_received = near(over_lines(raw(grad_send), 1))
    feed_send, feed_keep = run(
        feed_terms_kernel,
        [near((4 * block, width), BF16), near((4 * block, width), F32)],
        [pltpu.VMEM((256, 1024), F32)],
        cot_rows, active_turned, ln_turned, grad_hidden, hidden_sums,
    )
    feed_twin = twin(feed_send)
    *grad_slots, bias_sums = run(
        attend_back_kernel,
        [near((line_rows * 2, 128), BF16)] * 4 + [near((8, 128), F32)],
        [
            pltpu.VMEM((length, 64), BF16),
            pltpu.VMEM((128, length), F32),
            pltpu.VMEM((64, length), F32),
            pltpu.VMEM((length, 128), F32),
            pltpu.VMEM((length, 64), F32),
            table,
            one_copy,
        ],
        *back_in, numbers, qk_rows, kq_rows, value_rows, attended, lse, *rotation,
    )
    grad_slots_in = with_places(grad_slots)
    low_own, low_half = run(
        halve_kernel,
        [near((rows, width), F32), near((rows, width), BF16)],
        [],
        low_keep, low_received,
    )
    low_rest = near(over_lines(raw(low_half), 2))
    grad_own, grad_half = run(
        halve_kernel,
        [near((rows, width), F32), near((rows, width), BF16)],
        [],
        grad_keep, grad_received,
    )
    grad_rest = near(over_lines(raw(grad_half), 2))
    mixed, att_turned, *mixed_slots = run(
        unpack_kernel,
        [near((line_rows, width), BF16), near((head_cols, line_rows), BF16)]
        + [near((rows, width), BF16)] * 3,
        [],
        *grad_slots_in,
    )
    _, *mixed_in = with_lines([mixed, *mixed_slots])
    qkv_send, qkv_keep = run(
        grads_kernel,
        [near((4 * qkv_block, qkv_cols), BF16), near((4 * qkv_block, qkv_cols), F32)],
        [
            pltpu.VMEM((line_rows, width), F32),
            pltpu.VMEM((256, qkv_cols), F32),
            pltpu.VMEM((head_cols, width), F32),
        ],
        mixed, feed_grad_low, normed, ln_turned, qkv, att_turned, cot_rows, bias_sums,
    )
    qkv_terms = twin(qkv_send)
    feed_blocks = run(
        share_twin_kernel,
        [near((block, width), F32)] + [near((block, width), BF16)] * 3,
        [],
        feed_keep, feed_twin,
    )
    feed_in = with_places(feed_blocks)
    qkv_blocks = run(
        share_twin_kernel,
        [near((qkv_block, qkv_cols), F32)] + [near((qkv_block, qkv_cols), BF16)] * 3,
        [],
        qkv_keep, qkv_terms,
    )
    qkv_sums = with_places(qkv_blocks)
    grad_down, grad_b_in, grad_b, *in_slots = run(
        feed_sum_kernel,
        [far((128, width), F32), ((1, 128), F32), ((1, 32), F32), near((32, width), F32)]
        + [near((32, width), BF16)] * 3,
        [],
        *feed_in,
    )
    in_parts = with_lines(in_slots)
    layer_out, grad_tokens = run(
        tokens_kernel,
        [far((rows, width), BF16), far((rows, width), BF16)],
        [],
        mixed, *mixed_in, qkv, w_out_full, low_own, low_rest, grad_own, grad_rest,
        far(tokens[0]), cot_rows, vectors,
    )
    grad_out, grad_qv, *qkv_parts = run(
        grad_sum_kernel,
        [far((32, width), F32), far((2, 32), F32), near((32 + VEC, qkv_cols), F32)]
        + [near((32 + VEC, qkv_cols), BF16)] * 3,
        [],
        *qkv_sums,
    )
    qkv_parts = with_lines(qkv_parts)
    (grad_in,) = run(join_in_kernel, [far((32, feed), F32)], [], *in_parts)
    grad_qkv, grad_gain, grad_shift = run(
        join_qkv_kernel,
        [far((32, 3 * width), F32), far((32,), F32), far((32,), F32)],
        [pltpu.VMEM((VEC, 32), F32)],
        *qkv_parts,
    )
    return (
        layer_out[None],
        grad_tokens[None],
        grad_gain,
        grad_shift,
        grad_qkv,
        grad_qv,
        grad_out,
        grad_b[0],
        grad_in,
        grad_b_in[0],
        grad_down,
        grad_b[0],
    )


def solution(mesh):
    one_head_each = mesh.shape["ctx"] == HEADS and mesh.shape["fsdp"] == 2
    return jax.shard_map(
        head_body if one_head_each else body,
        mesh=mesh,
        in_specs=(
            P("fsdp", "ctx", None),
            P("ctx", None),
            P("fsdp"),
            P("fsdp"),
            P("fsdp", None),
            P(None, "fsdp"),
            P("fsdp", None),
            P("fsdp"),
            P("fsdp", None),
            P("fsdp"),
            P("fsdp", None),
            P("fsdp"),
            P("fsdp", "ctx", None),
        ),
        out_specs=(
            P("fsdp", "ctx", None),
            P("fsdp", "ctx", None),
            P(("ctx", "fsdp")),
            P(("ctx", "fsdp")),
            P(("ctx", "fsdp"), None),
            P(None, ("ctx", "fsdp")),
            P(("ctx", "fsdp"), None),
            P(("ctx", "fsdp")),
            P(("ctx", "fsdp"), None),
            P(("ctx", "fsdp")),
            P(("ctx", "fsdp"), None),
            P(("ctx", "fsdp")),
        ),
        check_vma=False,
    )
```

```python
from functools import partial
import math

import jax
import jax.numpy as jnp
import numpy as np
from jax import lax
from jax.experimental import pallas as pl
from jax.experimental.pallas import tpu as pltpu
from jax.sharding import PartitionSpec as P

HEADS = 16
HEAD_DIM = 64
ROT = 16


epsilon = 1e-05


def from_behind(block, axis, distance):
    devices = range(lax.axis_size(axis))
    route = [((i - distance) % len(devices), i) for i in devices]
    return lax.ppermute(block, axis, route)


def rotate(vectors, cosine, sine_part):
    half_rot = ROT // 2
    rotary_part = vectors[..., :ROT]
    turned = jnp.concatenate([-rotary_part[..., half_rot:], rotary_part[..., :half_rot]], -1)
    return jnp.concatenate([rotary_part * cosine + turned * sine_part, vectors[..., ROT:]], -1)


def tables(positions):
    freq_index = jnp.arange(ROT // 2, dtype=jnp.float32)
    inverse = 10000.0 ** (-2.0 * freq_index / ROT)
    angles = positions.astype(jnp.float32)[:, None] * inverse[None, :]
    angles = jnp.concatenate([angles, angles], -1)
    return (jnp.cos(angles), jnp.sin(angles))


def spread_positions(orders, half_rows):
    offsets = jnp.arange(half_rows, dtype=jnp.int32)
    return (orders[:, :, None] * half_rows + offsets[None, None, :]).reshape(-1)


def outer_sum(left_side, right_side):
    return lax.dot_general(
        left_side, right_side, (((0,), (0,)), ((), ())), preferred_element_type=jnp.float32
    )


def times_transposed(left_side, right_side):
    return lax.dot_general(
        left_side, right_side, (((1,), (1,)), ((), ())), preferred_element_type=jnp.float32
    )


def attend_block(carried, queries, query_pos, key_rows, value_rows, key_pos, score_scale):
    row_max, row_sum, weighted = carried
    scores = (
        jnp.einsum("qhd,khd->hqk", queries, key_rows, preferred_element_type=jnp.float32)
        * score_scale
    )
    allowed = (query_pos[:, None] >= key_pos[None, :])[None]
    new_max = jnp.maximum(row_max, jnp.max(jnp.where(allowed, scores, -1e30), -1))
    weights = jnp.where(allowed, jnp.exp(scores - new_max[:, :, None]), 0.0)
    rescale = jnp.exp(row_max - new_max)
    row_sum = row_sum * rescale + jnp.sum(weights, -1)
    weighted = weighted * rescale.T[:, :, None] + jnp.einsum(
        "hqk,khd->qhd", weights.astype(jnp.bfloat16), value_rows, preferred_element_type=jnp.float32
    )
    return (new_max, row_sum, weighted)


def block_grads(
    queries, grad_rows, log_sum, delta_rows, query_pos, key_rows, value_rows, key_pos, score_scale
):
    scores = (
        jnp.einsum("qhd,khd->hqk", queries, key_rows, preferred_element_type=jnp.float32)
        * score_scale
    )
    allowed = (query_pos[:, None] >= key_pos[None, :])[None]
    probs = jnp.where(allowed, jnp.exp(scores - log_sum[:, :, None]), 0.0)
    grad_values = jnp.einsum(
        "hqk,qhd->khd", probs.astype(jnp.bfloat16), grad_rows, preferred_element_type=jnp.float32
    )
    grad_probs = jnp.einsum(
        "qhd,khd->hqk", grad_rows, value_rows, preferred_element_type=jnp.float32
    )
    grad_scores = (probs * (grad_probs - delta_rows[:, :, None])).astype(jnp.bfloat16)
    grad_queries = (
        jnp.einsum("hqk,khd->qhd", grad_scores, key_rows, preferred_element_type=jnp.float32)
        * score_scale
    )
    grad_keys = (
        jnp.einsum("hqk,qhd->khd", grad_scores, queries, preferred_element_type=jnp.float32)
        * score_scale
    )
    return (grad_queries, grad_keys, grad_values)


def body(
    tokens,
    block_order,
    ln_gain,
    ln_bias,
    w_qkv,
    qv_bias,
    w_out,
    b_out,
    w_in,
    b_in,
    w_down,
    b_down,
    cotangent,
):
    gathered = (
        lax.all_gather(ln_gain, "fsdp", axis=0, tiled=True),
        lax.all_gather(ln_bias, "fsdp", axis=0, tiled=True),
        lax.all_gather(w_qkv, "fsdp", axis=0, tiled=True),
        lax.all_gather(qv_bias, "fsdp", axis=1, tiled=True),
        lax.all_gather(w_out, "fsdp", axis=0, tiled=True),
        lax.all_gather(b_out, "fsdp", axis=0, tiled=True),
        lax.all_gather(w_in, "fsdp", axis=0, tiled=True),
        lax.all_gather(b_in, "fsdp", axis=0, tiled=True),
        lax.all_gather(w_down, "fsdp", axis=0, tiled=True),
        lax.all_gather(b_down, "fsdp", axis=0, tiled=True),
    )
    (
        gain_full,
        shift_full,
        qkv_full,
        bias_full,
        out_full,
        out_bias,
        in_full,
        in_bias,
        down_full,
        down_bias,
    ) = gathered
    tok_rows = tokens.shape[1]
    model_width = tokens.shape[2]
    half_rows = tok_rows // 2
    score_scale = HEAD_DIM ** (-0.5)
    head_shape = (tok_rows, HEADS, HEAD_DIM)
    flat_shape = (tok_rows, model_width)
    inputs = tokens[0].astype(jnp.float32)
    row_mean = jnp.mean(inputs, -1, keepdims=True)
    centered = inputs - row_mean
    inverse = lax.rsqrt(jnp.mean(centered * centered, -1, keepdims=True) + epsilon)
    normed = centered * inverse
    ln_out = (normed * gain_full.astype(jnp.float32) + shift_full.astype(jnp.float32)).astype(
        jnp.bfloat16
    )
    qkv_pre = jnp.dot(ln_out, qkv_full, preferred_element_type=jnp.float32)
    positions = spread_positions(block_order, half_rows)
    cosine, sine_part = tables(positions)
    cosine = cosine[:, None, :]
    sine_part = sine_part[:, None, :]
    query_pre = qkv_pre[:, :model_width] + bias_full[0].astype(jnp.float32)
    query_rows = rotate(query_pre.reshape(head_shape), cosine, sine_part).astype(jnp.bfloat16)
    key_rows = rotate(
        qkv_pre[:, model_width : 2 * model_width].reshape(head_shape), cosine, sine_part
    ).astype(jnp.bfloat16)
    value_rows = (qkv_pre[:, 2 * model_width :] + bias_full[1].astype(jnp.float32)).astype(
        jnp.bfloat16
    )
    key_flat = key_rows.reshape(flat_shape)
    start_state = (
        jnp.full((HEADS, tok_rows), -1e30, jnp.float32),
        jnp.zeros((HEADS, tok_rows), jnp.float32),
        jnp.zeros(head_shape, jnp.float32),
    )
    carried = start_state
    piece_keys = lax.all_gather(key_flat, "ctx", axis=0, tiled=True)
    piece_values = lax.all_gather(value_rows, "ctx", axis=0, tiled=True)
    piece_orders = lax.all_gather(block_order, "ctx", axis=0, tiled=True)
    shard_count = piece_orders.shape[0]
    group_size = math.gcd(shard_count, max(1, 1024 // tok_rows))
    rounds = shard_count // group_size
    stacked = (
        piece_keys.reshape(rounds, group_size * tok_rows, HEADS, HEAD_DIM),
        piece_values.reshape(rounds, group_size * tok_rows, HEADS, HEAD_DIM),
        piece_orders.reshape(rounds, group_size, 2),
    )

    def one_round(inner_state, block_item):
        key_pos = spread_positions(block_item[2], half_rows)
        return (
            attend_block(
                inner_state,
                query_rows,
                positions,
                block_item[0],
                block_item[1],
                key_pos,
                score_scale,
            ),
            None,
        )

    carried, _ = lax.scan(one_round, carried, stacked)
    row_max, row_sum, weighted = carried
    attended_f32 = weighted / row_sum.T[:, :, None]
    log_sum = row_max + jnp.log(row_sum)
    attended = attended_f32.reshape(flat_shape).astype(jnp.bfloat16)
    branch = jnp.dot(attended, out_full, preferred_element_type=jnp.float32) + out_bias.astype(
        jnp.float32
    )
    hidden = jnp.dot(ln_out, in_full, preferred_element_type=jnp.float32) + in_bias.astype(
        jnp.float32
    )
    active = jax.nn.gelu(hidden, approximate=False).astype(jnp.bfloat16)
    feed_out = jnp.dot(active, down_full, preferred_element_type=jnp.float32) + down_bias.astype(
        jnp.float32
    )
    layer_out = (inputs + branch + feed_out).astype(jnp.bfloat16)[None]
    gain_back, qkv_back, out_back, in_back, down_back = (
        gain_full,
        qkv_full,
        out_full,
        in_full,
        down_full,
    )
    grad_out = cotangent[0]
    grad_f32 = grad_out.astype(jnp.float32)
    grad_attended = times_transposed(grad_out, out_back).astype(jnp.bfloat16).reshape(head_shape)
    grad_active = times_transposed(grad_out, down_back)
    _, gelu_pull = jax.vjp(partial(jax.nn.gelu, approximate=False), hidden)
    grad_hidden = gelu_pull(grad_active)[0].astype(jnp.bfloat16)
    delta_rows = jnp.sum(grad_attended.astype(jnp.float32) * attended_f32, -1).T
    cotangent_sum = jnp.sum(grad_f32, 0)
    term_out_w = outer_sum(attended, grad_out)
    term_in_w = outer_sum(ln_out, grad_hidden)
    term_in_b = jnp.sum(grad_hidden.astype(jnp.float32), 0)
    term_down_w = outer_sum(active, grad_out)
    cycle_size = lax.axis_size("ctx")
    zeros_flat = jnp.zeros(flat_shape, jnp.float32)
    zeros_heads = jnp.zeros(head_shape, jnp.float32)

    def send_home(grad_keys, grad_values):
        return (
            from_behind(grad_keys.astype(jnp.bfloat16), "ctx", 1).astype(grad_keys.dtype),
            from_behind(grad_values.astype(jnp.bfloat16), "ctx", 1).astype(grad_values.dtype),
        )

    def visit_keys(carried):
        visit_key, visit_value, visit_order, grad_keys, grad_values, grad_query = carried
        part_query, part_key, part_value = block_grads(
            query_rows,
            grad_attended,
            log_sum,
            delta_rows,
            positions,
            visit_key.reshape(head_shape),
            visit_value.reshape(head_shape),
            spread_positions(visit_order, half_rows),
            score_scale,
        )
        return (
            grad_keys + part_key.reshape(flat_shape),
            grad_values + part_value.reshape(flat_shape),
            grad_query + part_query,
        )

    def cycle_step(step_index, carried):
        grad_keys, grad_values, grad_query = visit_keys(carried)
        visit_key, visit_value, visit_order = from_behind(
            (carried[0], carried[1], carried[2]), "ctx", 1
        )
        grad_keys, grad_values = send_home(grad_keys, grad_values)
        return (visit_key, visit_value, visit_order, grad_keys, grad_values, grad_query)

    carried = lax.fori_loop(
        0,
        cycle_size - 1,
        cycle_step,
        (key_flat, value_rows, block_order, zeros_flat, zeros_flat, zeros_heads),
    )
    grad_keys, grad_values, grad_query = visit_keys(carried)
    grad_keys, grad_values = send_home(grad_keys, grad_values)
    grad_keys = grad_keys.reshape(head_shape)
    grad_values = grad_values.reshape(head_shape)
    grad_q_pre = rotate(grad_query, cosine, -sine_part).reshape(flat_shape).astype(jnp.bfloat16)
    grad_k_pre = rotate(grad_keys, cosine, -sine_part).reshape(flat_shape).astype(jnp.bfloat16)
    grad_v_pre = grad_values.reshape(flat_shape).astype(jnp.bfloat16)
    grad_qkv = jnp.concatenate([grad_q_pre, grad_k_pre, grad_v_pre], -1)
    grad_ln = times_transposed(grad_qkv, qkv_back) + times_transposed(grad_hidden, in_back)
    grad_normed = grad_ln * gain_back.astype(jnp.float32)
    grad_inputs = inverse * (
        grad_normed
        - jnp.mean(grad_normed, -1, keepdims=True)
        - normed * jnp.mean(grad_normed * normed, -1, keepdims=True)
    )
    grad_tokens = (grad_f32 + grad_inputs).astype(jnp.bfloat16)[None]
    term_gain = jnp.sum(grad_ln * normed, 0)
    term_bias = jnp.sum(grad_ln, 0)
    term_qkv = outer_sum(ln_out, grad_qkv)
    term_qv = jnp.stack(
        [jnp.sum(grad_q_pre.astype(jnp.float32), 0), jnp.sum(grad_v_pre.astype(jnp.float32), 0)], 0
    )
    (
        sum_gain,
        sum_bias,
        sum_qkv,
        sum_qv,
        sum_out_w,
        sum_out_b,
        sum_in_w,
        sum_in_b,
        sum_down_w,
        sum_down_b,
    ) = (
        lax.psum_scatter(term_gain, ("ctx", "fsdp"), scatter_dimension=0, tiled=True),
        lax.psum_scatter(term_bias, ("ctx", "fsdp"), scatter_dimension=0, tiled=True),
        lax.psum_scatter(term_qkv, ("ctx", "fsdp"), scatter_dimension=0, tiled=True),
        lax.psum_scatter(term_qv, ("ctx", "fsdp"), scatter_dimension=1, tiled=True),
        lax.psum_scatter(term_out_w, ("ctx", "fsdp"), scatter_dimension=0, tiled=True),
        lax.psum_scatter(cotangent_sum, ("ctx", "fsdp"), scatter_dimension=0, tiled=True),
        lax.psum_scatter(term_in_w, ("ctx", "fsdp"), scatter_dimension=0, tiled=True),
        lax.psum_scatter(term_in_b, ("ctx", "fsdp"), scatter_dimension=0, tiled=True),
        lax.psum_scatter(term_down_w, ("ctx", "fsdp"), scatter_dimension=0, tiled=True),
        lax.psum_scatter(cotangent_sum, ("ctx", "fsdp"), scatter_dimension=0, tiled=True),
    )
    return (
        layer_out,
        grad_tokens,
        sum_gain,
        sum_bias,
        sum_qkv,
        sum_qv,
        sum_out_w,
        sum_out_b,
        sum_in_w,
        sum_in_b,
        sum_down_w,
        sum_down_b,
    )


LINES = 4
ACROSS = HEADS // LINES
F32 = jnp.float32
BF16 = jnp.bfloat16
VMEM_LIMIT = 16 * 1024 * 1024
TIMES = {'hold': 5000, 'feed_grad': 40, 'halve': 400, 'unpack': 150, 'feed_sum': 150, 'feed_terms': 5, 'share_twin': 400, 'join_in': 5, 'attend': 20, 'grads': 40}

VEC = 16


def dot(left, right):
    return jnp.dot(left, right, preferred_element_type=F32)


def dot_nt(left, right):
    return lax.dot_general(left, right, (((1,), (1,)), ((), ())), preferred_element_type=F32)


class Far(tuple):
    pass


class Near(tuple):
    pass


def far(*x):
    return Far(x)


def near(*x):
    return Near(x)


def raw(x):
    return x[0] if isinstance(x, (Far, Near)) else x


def placed(x):
    if isinstance(x, Far):
        return pltpu.with_memory_space_constraint(x[0], pltpu.HBM)
    if isinstance(x, Near):
        return pltpu.with_memory_space_constraint(x[0], pltpu.VMEM)
    return x


def spot():
    context = lax.axis_index("ctx")
    return context // ACROSS, context % ACROSS, lax.axis_index("fsdp")


def call(kernel, out_shapes, scratch, *operands, after=(), loose_in=0):
    whole = pl.BlockSpec(memory_space=pltpu.VMEM)
    loose = pl.BlockSpec(memory_space=pl.ANY)
    arrays, specs = [], []
    for x in operands:
        arrays.append(placed(x))
        if arrays[-1].dtype == jnp.int32 and arrays[-1].ndim == 1:
            specs.append(pl.BlockSpec(memory_space=pltpu.SMEM))
        else:
            specs.append(loose if len(specs) < loose_in else whole)
    outs = []
    for shape in out_shapes:
        if isinstance(shape, Far):
            outs.append(pltpu.HBM(*shape))
        elif isinstance(shape, Near):
            outs.append(pltpu.VMEM(*shape))
        else:
            outs.append(jax.ShapeDtypeStruct(*shape))
    count = len(arrays)

    def body(*refs):
        kernel(*refs[:count], *refs[count + len(after) :])

    name = kernel.__name__.removesuffix("_kernel")
    results = pl.pallas_call(
        body,
        name=name,
        out_shape=outs,
        in_specs=specs + [loose] * len(after),
        out_specs=[whole for _ in outs],
        scratch_shapes=scratch,
        compiler_params=pltpu.CompilerParams(vmem_limit_bytes=VMEM_LIMIT),
        cost_estimate=pl.CostEstimate(
            flops=TIMES.get(name, 0) * 115_000_000, bytes_accessed=0, transcendentals=0
        ),
    )(*arrays, *map(placed, after))
    return [
        near(x) if isinstance(shape, Near) else x for x, shape in zip(results, out_shapes)
    ]


def run_copies(pairs, sems):
    copies = [pltpu.make_async_copy(x, y, sems.at[i]) for i, (x, y) in enumerate(pairs)]
    for copy in copies:
        copy.start()
    for copy in copies:
        copy.wait()


def prepare_kernel(qkv, w_in, w_out, w_down, gain, shift, b_out, b_down, qv, b_in, packed, sems):
    line, _, _ = spot()
    feed = w_in.shape[1] // LINES
    half, width = w_out.shape
    part = line % (LINES // 2)
    row = 0
    pairs = []
    sources = [
        w_in.at[:, pl.ds(pl.multiple_of(feed * line, 128), feed)],
        w_out,
        w_down.at[pl.ds(pl.multiple_of(feed * part, 16), feed), :],
    ]
    for source in sources + [qkv.at[:, width * i : width * (i + 1)] for i in range(3)]:
        pairs.append((source, packed.at[row : row + source.shape[0], :]))
        row += source.shape[0]
    rows = [x[...].astype(F32).reshape(1, half) for x in (gain, shift, b_out, b_down)]
    rows += [qv[...].astype(F32), b_in[...].astype(F32).reshape(4, half)]
    rows.append(jnp.zeros((VEC - 10, half), F32))
    packed[row : row + VEC, :half] = jnp.concatenate(rows, 0).astype(BF16)
    run_copies(pairs, sems)


def assemble_kernel(own, twin, qkv, w_in, w_out, w_down, vectors, low, sems):
    line, _, core = spot()
    width = w_out.shape[1]
    half = width // 2
    feed = w_down.shape[0]
    down_row = 2 * half
    qkv_row = down_row + feed
    vec_row = qkv_row + 3 * half
    pairs = []
    for source, side in ((own, core), (twin, 1 - core)):
        rows = pl.ds(pl.multiple_of(half * side, half), half)
        pairs.append((source.at[:half, :], w_in.at[rows, :]))
        pairs.append((source.at[half:down_row, :], w_out.at[rows, :]))
        for i in range(3):
            base = qkv_row + half * i
            pairs.append(
                (source.at[base : base + half, :], qkv.at[rows, width * i : width * (i + 1)])
            )
        spare = pl.ds(pl.multiple_of(VEC * side, VEC), VEC)
        pairs.append((source.at[vec_row:, :half], low.at[spare, :]))
    holds = core == line // (LINES // 2)

    @pl.when(holds)
    def _():
        run_copies(pairs + [(own.at[down_row:qkv_row, :], w_down)], sems)

    @pl.when(jnp.logical_not(holds))
    def _():
        run_copies(pairs + [(twin.at[down_row:qkv_row, :], w_down)], sems)

    vectors[...] = low[...].astype(F32)


def line_columns(qkv, part):
    line, _, _ = spot()
    width = qkv.shape[1] // 3
    base = width * part + width // LINES * line
    return qkv[:, pl.ds(pl.multiple_of(base, 128), width // LINES)]


def line_rows_of(w_out):
    line, _, _ = spot()
    count = w_out.shape[0] // LINES
    return w_out[pl.ds(pl.multiple_of(count * line, 16), count), :]


def full_row(vectors, index):
    return jnp.concatenate(
        [vectors[index : index + 1, :], vectors[VEC + index : VEC + index + 1, :]], 1
    )


def pack_kernel(order, tokens, packed):
    rows = tokens.shape[0]
    packed[:rows, :] = tokens[...]
    lane = lax.broadcasted_iota(jnp.int32, (VEC, 128), 1)
    numbers = jnp.where(lane == 0, order[0], jnp.where(lane == 1, order[1], 0))
    packed[rows:, :128] = numbers.astype(F32).astype(BF16)
    packed[rows:, 128:] = jnp.zeros((VEC, tokens.shape[1] - 128), BF16)


def reorder(chunks, place):
    upper, lower = chunks
    turned = (place & 2) != 0
    near_by = (place & 1) != 0
    first = jnp.where(turned, lower, upper)
    second = jnp.where(turned, upper, lower)
    first = jnp.where(near_by, pltpu.roll(first, 64, 1), first)
    second = jnp.where(near_by, pltpu.roll(second, 64, 1), second)
    return first, second


def left_lanes(rows):
    return lax.broadcasted_iota(jnp.int32, (rows, 128), 1) < 64


def pair_heads(one, two, slot):
    keep = left_lanes(one.shape[0])
    if slot % 2 == 0:
        return jnp.where(keep, one, pltpu.roll(two, 64, 1))
    return jnp.where(keep, pltpu.roll(one, 64, 1), two)


def fold_rows(chunk, slot):
    rows = chunk.shape[0] // 2
    return pair_heads(chunk[:rows], chunk[rows:], slot)


def unfold_pair(even, odd):
    keep = left_lanes(even.shape[0])
    top = jnp.where(keep, even, pltpu.roll(odd, 64, 1))
    bottom = jnp.where(keep, pltpu.roll(even, 64, 1), odd)
    return jnp.concatenate([top, bottom], 0)


def normalise(rows):
    x = rows.astype(F32)
    centred = x - jnp.mean(x, -1, keepdims=True)
    inverse = lax.rsqrt(jnp.mean(centred * centred, -1, keepdims=True) + epsilon)
    return centred * inverse, inverse


def two_chunks(x):
    return x[:, :128], x[:, 128:256]


def two_chunks(x):
    return x[:, :128], x[:, 128:256]


def project_kernel(t0, t1, t2, t3, vectors, qkv, s0, s1, s2, s3, ln_ref, lnt_ref, normed_ref):
    line, place, _ = spot()
    rows = t0.shape[0] - VEC
    gain, shift = full_row(vectors, 0), full_row(vectors, 1)
    numbers = jnp.zeros((VEC, 128), F32)
    for k, ref in enumerate((t0, t1, t2, t3)):
        source = line ^ k
        part = pl.ds(pl.multiple_of(rows * source, rows), rows)
        normed, _ = normalise(ref[:rows, :])
        normed_ref[part, :] = normed
        ln_ref[part, :] = (normed * gain + shift).astype(BF16)
        numbers = numbers + pltpu.roll(ref[rows:, :128].astype(F32), 2 * source, 1)
    side = VEC * (line // (LINES // 2))
    lanes = pl.ds(pl.multiple_of(256 * (line % (LINES // 2)), 256), 256)
    bias_q = vectors[pl.ds(side + 4, 1), lanes]
    bias_v = vectors[pl.ds(side + 5, 1), lanes]
    q_chunks = reorder(two_chunks(dot(ln_ref[...], line_columns(qkv, 0)) + bias_q), place)
    k_chunks = reorder(two_chunks(dot(ln_ref[...], line_columns(qkv, 1))), place)
    v_chunks = reorder(two_chunks(dot(ln_ref[...], line_columns(qkv, 2)) + bias_v), place)
    total = ln_ref.shape[0]
    end = total * 3 // 2
    for slot, ref in enumerate((s0, s1, s2, s3)):
        pair = slot // 2
        ref[:total, :] = pair_heads(q_chunks[pair], k_chunks[pair], slot).astype(BF16)
        ref[total:end, :] = fold_rows(v_chunks[pair], slot).astype(BF16)
        ref[end:, :] = numbers.astype(BF16)
    lnt_ref[...] = ln_ref[...].T


def back_rows_kernel(c0, c1, c2, c3, w_out, s0, s1, s2, s3, cot):
    line, place, _ = spot()
    rows = c0.shape[0]
    for k, ref in enumerate((c0, c1, c2, c3)):
        cot[pl.ds(pl.multiple_of(rows * (line ^ k), rows), rows), :] = ref[...]
    chunks = reorder(two_chunks(dot_nt(cot[...], line_rows_of(w_out))), place)
    for slot, ref in enumerate((s0, s1, s2, s3)):
        ref[...] = fold_rows(chunks[slot // 2], slot).astype(BF16)


def block_rows(table):
    for j in range(4):
        for i in range(8):
            yield j, i, pl.ds(pl.multiple_of(table[8 * j, i] * 64, 64), 64)


def sort_rows(table, slots, target, base, folded):
    for j, i, dest in block_rows(table):
        if folded:
            start = base + 64 * (i % 4)
            lanes = slice(0, 64) if i < 4 else slice(64, 128)
            target[dest, :] = slots[j][start : start + 64, lanes]
        else:
            target[dest, :] = slots[j][base + 64 * i : base + 64 * (i + 1), :]


def turn(x, cosine, sine):
    lane = lax.broadcasted_iota(jnp.int32, x.shape, 1) & (HEAD_DIM - 1)
    other = jnp.where(lane < ROT // 2, pltpu.roll(x, 120, 1), pltpu.roll(x, 8, 1))
    return x * cosine + other * sine


TILE = 256


def scores_of(qk_ref, i):
    rows = slice(TILE * i, TILE * (i + 1))
    queries = jnp.where(left_lanes(TILE), qk_ref[rows, :], jnp.zeros((), BF16))
    queries = queries * jnp.asarray(HEAD_DIM ** (-0.5), BF16)
    return queries


def allowed_tile():
    row = lax.broadcasted_iota(jnp.int32, (TILE, TILE), 0)
    col = lax.broadcasted_iota(jnp.int32, (TILE, TILE), 1)
    return row >= col


def attend_kernel(r0, r1, r2, r3, cosine, sine, *rest):
    qk_ref, kq_ref, v_ref, att_ref, lse_ref, table_ref, raw, table, sem = rest
    refs = (r0, r1, r2, r3)
    count = qk_ref.shape[0]
    lines = count // 4
    for j, ref in enumerate(refs):
        numbers = ref[lines * 3 // 2 :, :].astype(F32)[:8, :]
        table_ref[8 * j : 8 * (j + 1), :] = numbers.astype(jnp.int32)
    run_copies([(table_ref, table)], sem)
    sort_rows(table, refs, raw, 0, False)
    sort_rows(table, refs, v_ref, lines, True)
    for i in range(count // TILE):
        rows = slice(TILE * i, TILE * (i + 1))
        turned = turn(raw[rows, :].astype(F32), cosine[rows, :], sine[rows, :])
        qk_ref[rows, :] = turned.astype(BF16)
        kq_ref[rows, :] = pltpu.roll(turned, 64, 1).astype(BF16)
    mask = allowed_tile()
    for i in range(count // TILE):
        rows = slice(TILE * i, TILE * (i + 1))
        keys = TILE * (i + 1)
        scores = dot_nt(scores_of(qk_ref, i), kq_ref[:keys, :])
        last = jnp.where(mask, scores[:, keys - TILE :], -1e30)
        scores = last if i == 0 else jnp.concatenate([scores[:, : keys - TILE], last], 1)
        top = jnp.max(scores, -1, keepdims=True)
        weights = jnp.exp(scores - top)
        total = jnp.sum(weights, -1, keepdims=True)
        weighted = dot(weights.astype(BF16), v_ref[:keys, :])
        att_ref[rows, :] = weighted / total
        lse_ref[rows, :] = top + jnp.log(total)


def attend_back_kernel(r0, r1, r2, r3, table_ref, qk_ref, kq_ref, v_ref, att_ref, *rest):
    lse_ref, cosine, sine, o0, o1, o2, o3, sums, ga_ref, kt_ref, vt_ref, gqk, gv = rest[:13]
    table, sem = rest[13:]
    refs = (r0, r1, r2, r3)
    count = qk_ref.shape[0]
    lines = count // 4
    run_copies([(table_ref, table)], sem)
    sort_rows(table, refs, ga_ref, 0, True)
    mask = allowed_tile()
    kt_ref[...] = jnp.zeros_like(kt_ref)
    vt_ref[...] = jnp.zeros_like(vt_ref)
    for i in range(count // TILE):
        rows = slice(TILE * i, TILE * (i + 1))
        keys = TILE * (i + 1)
        queries = scores_of(qk_ref, i)
        scores = dot_nt(queries, kq_ref[:keys, :])
        last = jnp.where(mask, scores[:, keys - TILE :], -1e30)
        scores = last if i == 0 else jnp.concatenate([scores[:, : keys - TILE], last], 1)
        probs = jnp.exp(scores - lse_ref[rows, :])
        grad_rows = ga_ref[rows, :]
        delta = jnp.sum(grad_rows.astype(F32) * att_ref[rows, :], -1, keepdims=True)
        grad_probs = dot_nt(grad_rows, v_ref[:keys, :])
        grad_scores = (probs * (grad_probs - delta)).astype(BF16)
        gqk[rows, :] = dot(grad_scores, kq_ref[:keys, :]) * HEAD_DIM ** (-0.5)
        vt_ref[:, :keys] += dot(grad_rows.astype(F32).T.astype(BF16), probs.astype(BF16))
        kt_ref[:, :keys] += dot(queries.astype(F32).T.astype(BF16), grad_scores)
    sum_q = jnp.zeros((1, 128), F32)
    sum_v = jnp.zeros((1, 64), F32)
    for i in range(count // TILE):
        rows = slice(TILE * i, TILE * (i + 1))
        grad_keys = pltpu.roll(kt_ref[:, rows].T, 64, 1)
        both = jnp.where(left_lanes(TILE), gqk[rows, :], grad_keys)
        both = turn(both, cosine[rows, :], -sine[rows, :])
        both = both.astype(BF16).astype(F32)
        values = vt_ref[:, rows].T.astype(BF16).astype(F32)
        gqk[rows, :] = both
        gv[rows, :] = values
        sum_q = sum_q + jnp.sum(both, 0, keepdims=True)
        sum_v = sum_v + jnp.sum(values, 0, keepdims=True)
    sums[...] = jnp.zeros_like(sums)
    sums[0:1, :64] = sum_q[:, :64]
    sums[1:2, :64] = sum_v
    outs = (o0, o1, o2, o3)
    for j, i, source in block_rows(table):
        lanes = slice(0, 64) if i < 4 else slice(64, 128)
        outs[j][64 * i : 64 * (i + 1), :] = gqk[source, :].astype(BF16)
        start = lines + 64 * (i % 4)
        outs[j][start : start + 64, lanes] = gv[source, :].astype(BF16)
        start += lines // 2
        outs[j][start : start + 64, lanes] = att_ref[source, :].astype(BF16)


def split_lines(low, keep, send):
    line, _, _ = spot()
    rows = low.shape[0] // LINES
    for k, (ref, base) in enumerate(((keep, 0), (send, 0), (keep, rows), (send, rows))):
        part = pl.ds(pl.multiple_of(rows * (line ^ k), rows), rows)
        ref[base : base + rows, :] = low[part, :].astype(ref.dtype)


def feed_kernel(ln, w_in, vectors, w_down, hidden_ref, actt_ref, keep, send, act_ref, low_ref):
    line, _, _ = spot()
    row = VEC * (line // (LINES // 2)) + 6 + 2 * (line % (LINES // 2))
    bias = jnp.concatenate([vectors[pl.ds(row, 1), :], vectors[pl.ds(row + 1, 1), :]], 1)
    for f in range(4):
        cols = slice(256 * f, 256 * (f + 1))
        hidden = dot(ln[...], w_in[:, cols]) + bias[:, cols]
        hidden_ref[:, cols] = hidden
        active = 0.5 * hidden * (1.0 + lax.erf(hidden * 0.7071067811865476))
        act_ref[:, cols] = active.astype(BF16)
        actt_ref[cols, :] = active.astype(BF16).T
    for f in range(4):
        cols = slice(256 * f, 256 * (f + 1))
        low_ref[:, cols] = dot(act_ref[...], w_down[:, cols])
    split_lines(low_ref, keep, send)


def feed_grad_kernel(cot, hidden, w_in, w_down, gh_ref, sums, low_ref, keep, send):
    for f in range(4):
        cols = slice(256 * f, 256 * (f + 1))
        grad_active = dot_nt(cot[...], w_down[cols, :])
        h = hidden[:, cols]
        slope = 0.5 * (1.0 + lax.erf(h * 0.7071067811865476)) + h * jnp.exp(
            -0.5 * h * h
        ) * 0.3989422804014327
        grad_hidden = (slope * grad_active).astype(BF16)
        gh_ref[:, cols] = grad_hidden
        total = jnp.sum(grad_hidden.astype(F32), 0, keepdims=True)
        sums[:, cols] = jnp.broadcast_to(total, (8, 256))
    for i in range(4):
        low_ref[:, 256 * i : 256 * (i + 1)] = dot_nt(gh_ref[...], w_in[256 * i : 256 * (i + 1), :])
    split_lines(low_ref, keep, send)


def feed_terms_kernel(cot_ref, actt, lnt, gh, sums, send, keep, chunk_ref):
    line, _, core = spot()
    cot = cot_ref[...]
    block = send.shape[0] // 4
    for f in range(4):
        chunk_ref[...] = dot(actt[256 * f : 256 * (f + 1), :], cot)
        base = block * f
        send[base : base + 128, :] = chunk_ref[
            pl.ds(pl.multiple_of((1 - core) * 128, 128), 128), :
        ].astype(BF16)
        keep[base : base + 128, :] = chunk_ref[pl.ds(pl.multiple_of(core * 128, 128), 128), :]
    for z in range(4):
        chunk_ref[...] = dot(lnt[256 * z : 256 * (z + 1), :], gh[...])
        for f in range(4):
            base = block * f + 128 + 32 * z
            send[base : base + 32, :] = chunk_ref[
                pl.ds(pl.multiple_of(64 * f + 32 * (1 - core), 32), 32), :
            ].astype(BF16)
            keep[base : base + 32, :] = chunk_ref[
                pl.ds(pl.multiple_of(64 * f + 32 * core, 32), 32), :
            ]
    cot_sum = jnp.sum(cot.astype(F32), 0, keepdims=True)
    picked = jnp.where(
        line < 2,
        jnp.where(line == 0, cot_sum[:, 0:256], cot_sum[:, 256:512]),
        jnp.where(line == 2, cot_sum[:, 512:768], cot_sum[:, 768:1024]),
    )
    zero = jnp.zeros((1, 640), F32)
    for f in range(4):
        even, odd = sums[:1, 256 * f : 256 * f + 128], sums[:1, 256 * f + 128 : 256 * f + 256]
        first = core == 0
        base = block * f + 256
        given = jnp.concatenate([jnp.where(first, odd, even), picked, zero], 1)
        kept = jnp.concatenate([jnp.where(first, even, odd), picked, zero], 1)
        send[base : base + VEC, :] = jnp.broadcast_to(given, (VEC, 1024)).astype(BF16)
        keep[base : base + VEC, :] = jnp.broadcast_to(kept, (VEC, 1024))


def share_twin_kernel(keep, received, o0, o1, o2, o3):
    _, place, _ = spot()
    block = o0.shape[0]
    for slot, ref in enumerate((o0, o1, o2, o3)):
        rows = pl.ds(pl.multiple_of((place ^ slot) * block, 16), block)
        ref[...] = (keep[rows, :] + received[rows, :].astype(F32)).astype(ref.dtype)


def adder(own, r1, r2, r3):
    def total(rows, cols=slice(None)):
        return (own[rows, cols].astype(F32) + r1[rows, cols].astype(F32)) + (
            r2[rows, cols].astype(F32) + r3[rows, cols].astype(F32)
        )

    return total


def owned_lanes(rows):
    _, place, core = spot()
    return pltpu.roll(rows, lax.rem(256 - (64 * place + 32 * core), 256), 1)[:, :32]


def feed_sum_kernel(own, r1, r2, r3, down_ref, bias_in, bias_out, i0, i1, i2, i3):
    line, _, _ = spot()
    total = adder(own, r1, r2, r3)
    down_ref[...] = total(slice(0, 128))
    bias_in[...] = total(slice(256, 264), slice(0, 128))[:1].reshape(128)
    bias_out[...] = owned_lanes(total(slice(256, 264), slice(128, 384)))[:1].reshape(32)
    for slot, ref in enumerate((i0, i1, i2, i3)):
        rows = pl.ds(pl.multiple_of(128 + 32 * (line ^ slot), 32), 32)
        ref[...] = total(rows).astype(ref.dtype)


def halve_kernel(keep, received, own, send):
    rows = own.shape[0]
    own[...] = keep[:rows, :] + received[:rows, :].astype(F32)
    send[...] = (keep[rows:, :] + received[rows:, :].astype(F32)).astype(BF16)


def unpack_kernel(r0, r1, r2, r3, mixed, att_t, s1, s2, s3):
    line, place, _ = spot()
    rows = s1.shape[0]
    total = LINES * rows
    fold = total // 2
    parts = [ref[...].astype(F32) for ref in (r0, r1, r2, r3)]
    keep_left = left_lanes(total)
    chunks = [[], [], [], []]
    for pair in range(2):
        one, two = parts[2 * pair], parts[2 * pair + 1]
        even, odd = one[:total], two[:total]
        values, attended = slice(total, total + fold), slice(total + fold, total + 2 * fold)
        chunks[0].append(unfold_pair(one[attended], two[attended]))
        chunks[1].append(jnp.where(keep_left, even, pltpu.roll(odd, 64, 1)))
        chunks[2].append(jnp.where(keep_left, pltpu.roll(even, 64, 1), odd))
        chunks[3].append(unfold_pair(one[values], two[values]))
    for index, both in enumerate(chunks):
        for pair, chunk in enumerate(reorder(both, place)):
            base = 256 * index + 128 * pair
            mixed[:, base : base + 128] = chunk.astype(BF16)
    for k, ref in ((1, s1), (2, s2), (3, s3)):
        ref[...] = mixed[pl.ds(pl.multiple_of(rows * (line ^ k), rows), rows), :]
    att_t[...] = mixed[:, :256].T


def grads_kernel(mixed, low, normed, lnt, qkv, att_t, cot, head_sums, *rest):
    send, keep, low_ref, chunk_ref, out_ref = rest
    _, place, core = spot()
    low_ref[...] = low[...]
    for i in range(3):
        cols = slice(256 * (i + 1), 256 * (i + 2))
        low_ref[...] += dot_nt(mixed[:, cols], line_columns(qkv, i))
    grad = low_ref[...]
    sum_gain = jnp.sum(grad * normed[...], 0, keepdims=True)
    sum_bias = jnp.sum(grad, 0, keepdims=True)
    block = send.shape[0] // 4
    for z in range(4):
        chunk_ref[...] = dot(lnt[256 * z : 256 * (z + 1), :], mixed[:, 256:])
        for f in range(4):
            base = block * f + 32 * z
            send[base : base + 32, :] = chunk_ref[
                pl.ds(pl.multiple_of(64 * f + 32 * (1 - core), 32), 32), :
            ].astype(BF16)
            keep[base : base + 32, :] = chunk_ref[
                pl.ds(pl.multiple_of(64 * f + 32 * core, 32), 32), :
            ]
    out_ref[...] = dot(att_t[...], cot[...])
    sums = [sum_gain[:, 256 * i : 256 * (i + 1)] for i in range(4)]
    sums += [sum_bias[:, 256 * i : 256 * (i + 1)] for i in range(4)]
    spare = jnp.concatenate([head_sums[...], jnp.zeros((8, 128), F32)], 1)
    for f in range(4):
        base = block * f + 128
        vec = jnp.concatenate(sums + [jnp.where(place == f, spare, 0.0)], 0)
        for ref, side in ((send, 1 - core), (keep, core)):
            rows = out_ref[pl.ds(pl.multiple_of(64 * f + 32 * side, 32), 32), :]
            tail = jnp.concatenate([rows[:16, 768:], rows[16:, 768:], vec], 1)
            ref[base : base + 32, :] = rows[:, :768].astype(ref.dtype)
            ref[base + 32 : base + 48, :] = tail.astype(ref.dtype)


def grad_sum_kernel(own, r1, r2, r3, grad_out, qv, i0, i1, i2, i3):
    line, _, core = spot()
    total = adder(own, r1, r2, r3)
    tail = total(slice(160, 176))
    grad_out[:, :768] = total(slice(128, 160))
    grad_out[:16, 768:] = tail[:, :256]
    grad_out[16:, 768:] = tail[:, 256:512]
    qv[...] = jnp.where(core == 0, tail[8:10, 512:544], tail[8:10, 544:576])
    for slot, ref in enumerate((i0, i1, i2, i3)):
        rows = pl.ds(pl.multiple_of(32 * (line ^ slot), 32), 32)
        ref[:32, :] = total(rows).astype(ref.dtype)
        ref[32:, :] = tail.astype(ref.dtype)


def join_in_kernel(i0, i1, i2, i3, out):
    line, _, _ = spot()
    for slot, ref in enumerate((i0, i1, i2, i3)):
        cols = pl.ds(pl.multiple_of((line ^ slot) * 1024, 1024), 1024)
        out[:, cols] = ref[...].astype(F32)


def join_qkv_kernel(i0, i1, i2, i3, out, gain, bias, vec_ref):
    line, _, _ = spot()
    vec = jnp.zeros((VEC, 256), F32)
    for slot, ref in enumerate((i0, i1, i2, i3)):
        for part in range(3):
            cols = pl.ds(pl.multiple_of(1024 * part + (line ^ slot) * 256, 256), 256)
            out[:, cols] = ref[:32, 256 * part : 256 * (part + 1)].astype(F32)
        vec = vec + ref[32:, 512:768].astype(F32)
    vec_ref[...] = owned_lanes(vec)
    gain[...] = vec_ref[pl.ds(line, 1), :].reshape(32)
    bias[...] = vec_ref[pl.ds(4 + line, 1), :].reshape(32)


def hold_kernel(x, out):
    out[...] = x[...]


def tokens_kernel(mixed, r1, r2, r3, qkv, w_out, *rest):
    low, low_rest, grad, grad_rest, tokens, cot, vectors, layer_out, grad_tokens = rest
    line, _, _ = spot()
    rows = low.shape[0]
    mine = pl.ds(pl.multiple_of(rows * line, rows), rows)
    branch = low[...] + low_rest[...].astype(F32)
    grad_ln = grad[...] + grad_rest[...].astype(F32)
    for k, ref in enumerate((mixed.at[mine, :], r1, r2, r3)):
        base = 256 * (line ^ k)
        part = pl.ds(pl.multiple_of(base, 256), 256)
        branch = branch + dot(ref[:, :256], w_out[part, :])
        for i in range(3):
            part = pl.ds(pl.multiple_of(base + 1024 * i, 256), 256)
            grad_ln = grad_ln + dot_nt(ref[:, 256 * (i + 1) : 256 * (i + 2)], qkv[:, part])
    own = tokens[:rows, :]
    branch = branch + own.astype(F32)
    layer_out[...] = (branch + full_row(vectors, 2) + full_row(vectors, 3)).astype(BF16)
    normed, inverse = normalise(own)
    g = grad_ln * full_row(vectors, 0)
    back = inverse * (
        g - jnp.mean(g, -1, keepdims=True) - normed * jnp.mean(g * normed, -1, keepdims=True)
    )
    grad_tokens[...] = (cot[mine, :].astype(F32) + back).astype(BF16)


def turn_tables(count):
    half_rot = ROT // 2
    inverse = 10000.0 ** (-2.0 * np.arange(half_rot) / ROT)
    angles = np.arange(count)[:, None] * inverse[None, :]
    cosine = np.ones((count, HEAD_DIM), np.float32)
    sine = np.zeros((count, HEAD_DIM), np.float32)
    cosine[:, :half_rot] = cosine[:, half_rot:ROT] = np.cos(angles)
    sine[:, :half_rot] = -np.sin(angles)
    sine[:, half_rot:ROT] = np.sin(angles)
    return tuple(np.concatenate([t, t], -1) for t in (cosine, sine))


def head_body(
    tokens,
    block_order,
    ln_gain,
    ln_bias,
    w_qkv,
    qv_bias,
    w_out,
    b_out,
    w_in,
    b_in,
    w_down,
    b_down,
    cotangent,
):
    positions = range(LINES * ACROSS)

    def over_lines(x, k):
        return lax.ppermute(x, "ctx", [(i, i ^ (k * ACROSS)) for i in positions])

    def over_places(x, j):
        return lax.ppermute(x, "ctx", [(i, i ^ j) for i in positions])

    def twin(x):
        return near(lax.ppermute(raw(x), "fsdp", [(0, 1), (1, 0)]))

    def with_lines(blocks):
        return [blocks[0]] + [near(over_lines(raw(blocks[k]), k)) for k in range(1, LINES)]

    def with_places(blocks):
        return [blocks[0]] + [near(over_places(raw(blocks[j]), j)) for j in range(1, ACROSS)]

    rows, width = tokens.shape[1], tokens.shape[2]
    half = w_qkv.shape[0]
    feed = w_in.shape[1]
    head_cols = width // LINES
    feed_cols = feed // LINES
    qkv_cols = 3 * head_cols
    length = rows * LINES * ACROSS
    line_rows = rows * LINES
    slot_rows = line_rows * 3 // 2
    rotation = turn_tables(length)
    packed_rows = 5 * half + feed_cols + VEC
    table = pltpu.SMEM((32, 128), jnp.int32)
    one_copy = pltpu.SemaphoreType.DMA((1,))
    block = 128 + 128 + VEC
    qkv_block = 128 + 32 + VEC

    last = []

    def run(kernel, out_shapes, scratch, *operands, after=(), loose_in=0):
        results = call(
            kernel, out_shapes, scratch, *operands, after=(*after, *last), loose_in=loose_in
        )
        last[:] = [far(results[0])] if isinstance(out_shapes[0], Far) else results[:1]
        return results
    (token_block,) = run(
        pack_kernel,
        [near((rows + VEC, width), BF16)],
        [],
        far(block_order.reshape(2)), far(tokens[0]),
    )
    from_two = over_lines(raw(token_block), 2)
    token_lines = [
        token_block,
        near(over_lines(raw(token_block), 1)),
        near(from_two),
        near(over_lines(from_two, 1)),
    ]
    (packed,) = run(
        prepare_kernel,
        [near((packed_rows, width), BF16)],
        [pltpu.SemaphoreType.DMA((6,))],
        far(w_qkv), far(w_in), far(w_out), far(w_down),
        *map(far, (ln_gain, ln_bias, b_out, b_down, qv_bias, b_in)),
        loose_in=4,
    )
    (cot_own,) = run(
        hold_kernel,
        [near((rows, width), BF16)],
        [],
        far(cotangent[0]),
        after=token_lines[1:3],
    )
    cot_two = over_lines(raw(cot_own), 2)
    cot_lines = [
        cot_own,
        near(over_lines(raw(cot_own), 1)),
        near(cot_two),
        near(over_lines(cot_two, 1)),
    ]
    qkv, in_rows, w_out_full, down_rows, vectors = run(
        assemble_kernel,
        [
            near((width, 3 * width), BF16),
            near((width, feed_cols), BF16),
            near((width, width), BF16),
            near((feed_cols, width), BF16),
            near((2 * VEC, half), F32),
        ],
        [pltpu.VMEM((2 * VEC, half), BF16), pltpu.SemaphoreType.DMA((13,))],
        packed, twin(packed),
        loose_in=2,
    )
    *slots, ln_low, ln_turned, normed = run(
        project_kernel,
        [near((slot_rows + VEC, 128), BF16)] * 4
        + [
            near((line_rows, width), BF16),
            near((width, line_rows), BF16),
            near((line_rows, width), F32),
        ],
        [],
        *token_lines, vectors, qkv,
    )
    slots_in = with_places(slots)
    hidden, active_turned, low_keep, low_send = run(
        feed_kernel,
        [
            near((line_rows, feed_cols), F32),
            near((feed_cols, line_rows), BF16),
            near((2 * rows, width), F32),
            near((2 * rows, width), BF16),
        ],
        [pltpu.VMEM((line_rows, feed_cols), BF16), pltpu.VMEM((line_rows, width), F32)],
        ln_low, in_rows, vectors, down_rows,
    )
    low_received = near(over_lines(raw(low_send), 1))
    qk_rows, kq_rows, value_rows, attended, lse, numbers = run(
        attend_kernel,
        [
            near((length, 128), BF16),
            near((length, 128), BF16),
            near((length, 64), BF16),
            near((length, 64), F32),
            near((length, 1), F32),
            near((32, 128), jnp.int32),
        ],
        [pltpu.VMEM((length, 128), BF16), table, one_copy],
        *slots_in, *rotation,
    )
    *back_slots, cot_rows = run(
        back_rows_kernel,
        [near((line_rows // 2, 128), BF16)] * 4 + [near((line_rows, width), BF16)],
        [],
        *cot_lines, w_out_full,
    )
    back_in = with_places(back_slots)
    grad_hidden, hidden_sums, feed_grad_low, grad_keep, grad_send = run(
        feed_grad_kernel,
        [
            near((line_rows, feed_cols), BF16),
            near((8, feed_cols), F32),
            near((line_rows, width), F32),
            near((2 * rows, width), F32),
            near((2 * rows, width), BF16),
        ],
        [],
        cot_rows, hidden, in_rows, down_rows,
    )
    grad_received = near(over_lines(raw(grad_send), 1))
    feed_send, feed_keep = run(
        feed_terms_kernel,
        [near((4 * block, width), BF16), near((4 * block, width), F32)],
        [pltpu.VMEM((256, 1024), F32)],
        cot_rows, active_turned, ln_turned, grad_hidden, hidden_sums,
    )
    feed_twin = twin(feed_send)
    *grad_slots, bias_sums = run(
        attend_back_kernel,
        [near((line_rows * 2, 128), BF16)] * 4 + [near((8, 128), F32)],
        [
            pltpu.VMEM((length, 64), BF16),
            pltpu.VMEM((128, length), F32),
            pltpu.VMEM((64, length), F32),
            pltpu.VMEM((length, 128), F32),
            pltpu.VMEM((length, 64), F32),
            table,
            one_copy,
        ],
        *back_in, numbers, qk_rows, kq_rows, value_rows, attended, lse, *rotation,
    )
    grad_slots_in = with_places(grad_slots)
    low_own, low_half = run(
        halve_kernel,
        [near((rows, width), F32), near((rows, width), BF16)],
        [],
        low_keep, low_received,
    )
    low_rest = near(over_lines(raw(low_half), 2))
    grad_own, grad_half = run(
        halve_kernel,
        [near((rows, width), F32), near((rows, width), BF16)],
        [],
        grad_keep, grad_received,
    )
    grad_rest = near(over_lines(raw(grad_half), 2))
    mixed, att_turned, *mixed_slots = run(
        unpack_kernel,
        [near((line_rows, width), BF16), near((head_cols, line_rows), BF16)]
        + [near((rows, width), BF16)] * 3,
        [],
        *grad_slots_in,
    )
    _, *mixed_in = with_lines([mixed, *mixed_slots])
    qkv_send, qkv_keep = run(
        grads_kernel,
        [near((4 * qkv_block, qkv_cols), BF16), near((4 * qkv_block, qkv_cols), F32)],
        [
            pltpu.VMEM((line_rows, width), F32),
            pltpu.VMEM((256, qkv_cols), F32),
            pltpu.VMEM((head_cols, width), F32),
        ],
        mixed, feed_grad_low, normed, ln_turned, qkv, att_turned, cot_rows, bias_sums,
    )
    qkv_terms = twin(qkv_send)
    feed_blocks = run(
        share_twin_kernel,
        [near((block, width), F32)] + [near((block, width), BF16)] * 3,
        [],
        feed_keep, feed_twin,
    )
    feed_in = with_places(feed_blocks)
    qkv_blocks = run(
        share_twin_kernel,
        [near((qkv_block, qkv_cols), F32)] + [near((qkv_block, qkv_cols), BF16)] * 3,
        [],
        qkv_keep, qkv_terms,
    )
    qkv_sums = with_places(qkv_blocks)
    grad_down, grad_b_in, grad_b, *in_slots = run(
        feed_sum_kernel,
        [far((128, width), F32), far((128,), F32), far((32,), F32), near((32, width), F32)]
        + [near((32, width), BF16)] * 3,
        [],
        *feed_in,
    )
    in_parts = with_lines(in_slots)
    layer_out, grad_tokens = run(
        tokens_kernel,
        [far((rows, width), BF16), far((rows, width), BF16)],
        [],
        mixed, *mixed_in, qkv, w_out_full, low_own, low_rest, grad_own, grad_rest,
        far(tokens[0]), cot_rows, vectors,
    )
    grad_out, grad_qv, *qkv_parts = run(
        grad_sum_kernel,
        [far((32, width), F32), far((2, 32), F32), near((32 + VEC, qkv_cols), F32)]
        + [near((32 + VEC, qkv_cols), BF16)] * 3,
        [],
        *qkv_sums,
    )
    qkv_parts = with_lines(qkv_parts)
    (grad_in,) = run(join_in_kernel, [far((32, feed), F32)], [], *in_parts)
    grad_qkv, grad_gain, grad_shift = run(
        join_qkv_kernel,
        [far((32, 3 * width), F32), far((32,), F32), far((32,), F32)],
        [pltpu.VMEM((VEC, 32), F32)],
        *qkv_parts,
    )
    return (
        layer_out[None],
        grad_tokens[None],
        grad_gain,
        grad_shift,
        grad_qkv,
        grad_qv,
        grad_out,
        grad_b,
        grad_in,
        grad_b_in,
        grad_down,
        grad_b,
    )


def solution(mesh):
    one_head_each = mesh.shape["ctx"] == HEADS and mesh.shape["fsdp"] == 2
    return jax.shard_map(
        head_body if one_head_each else body,
        mesh=mesh,
        in_specs=(
            P("fsdp", "ctx", None),
            P("ctx", None),
            P("fsdp"),
            P("fsdp"),
            P("fsdp", None),
            P(None, "fsdp"),
            P("fsdp", None),
            P("fsdp"),
            P("fsdp", None),
            P("fsdp"),
            P("fsdp", None),
            P("fsdp"),
            P("fsdp", "ctx", None),
        ),
        out_specs=(
            P("fsdp", "ctx", None),
            P("fsdp", "ctx", None),
            P(("ctx", "fsdp")),
            P(("ctx", "fsdp")),
            P(("ctx", "fsdp"), None),
            P(None, ("ctx", "fsdp")),
            P(("ctx", "fsdp"), None),
            P(("ctx", "fsdp")),
            P(("ctx", "fsdp"), None),
            P(("ctx", "fsdp")),
            P(("ctx", "fsdp"), None),
            P(("ctx", "fsdp")),
        ),
        check_vma=False,
    )
```
